128 devices in a mesh: obj: 16 (over y, z), pos: 8 (over x, core).
Axes of the slice: x: 4, y: 4, z: 4, core: 2. Of those that a mesh axis runs over, the one named last changes fastest.
Arguments:
- object_field: float32 [2, 2, 2048, 2048], P(None, None, 'obj'), may hold values from -4.2 to 4.2
- probe_modes: float32 [2, 2, 128, 128], replicated, may hold values from -6 to 6
- propagator_phase: float32 [128, 128], replicated, may hold values from -3.140625 to 3.140625
- offsets: int32 [2048, 2], P(('obj', 'pos')), may hold values from 0 to 1920, as said below
- measured: float32 [2048, 128, 128], P(('obj', 'pos')), may hold values from 0.5 to 20
Outputs:
- object_grad: float32 [2, 2, 2048, 2048], P(None, None, 'obj', 'pos')
The draws below stay inside these ranges and needn't reach their ends.
Inputs may be any that keep to these rules, and one draw needn't show every extreme that they name: `offsets`: in each aligned block of 16 rows (the positions of one device) at most 2 rows have the same top strip, their row offset divided by 128 and rounded down, and in every block some strip is the top strip of exactly 2 rows. Every window lies inside the object: row offset at most 1920, column offset at most 1920.
All inputs are finite; a program needn't handle non-finite values.
Results may differ from the reference program's by a relative error of at most 0.0042.
Values may be sent and summed in bfloat16 or wider, within the bound.
A program may use at most 128 MiB of HBM per device.

```python
import math
import jax
import jax.numpy as jnp
from jax import lax

PATCH = 128
MODES = 2
SLICES = 2
NX = 2048
CAP = 2
POS_DEV = 16
STRIP = 128
NPOS = 2048


def draw_offsets(key, part):
    key = jax.random.fold_in(key, 11)
    block_count = NPOS // POS_DEV
    strip_count = NX // STRIP

    def one_block(block_key):
        keys = jax.random.split(block_key, 6)
        ordering = jax.random.permutation(keys[0], CAP * strip_count)
        leading = ordering[0]
        partner = leading // CAP * CAP + (leading % CAP + 1) % CAP
        where_partner = jnp.argmax(ordering == partner)
        ordering = ordering.at[where_partner].set(ordering[1]).at[1].set(partner)
        top_strip = ordering[:POS_DEV] // CAP
        row_within = jax.random.randint(keys[1], (POS_DEV,), 0, STRIP)
        row_within = jnp.where(top_strip == strip_count - 1, row_within % (STRIP - PATCH + 1), row_within)
        col_start = jax.random.randint(keys[2], (POS_DEV,), 0, NX - PATCH + 1)
        low_item = jax.random.randint(keys[3], (), 0, POS_DEV)
        high_item = (low_item + 1 + jax.random.randint(keys[4], (), 0, POS_DEV - 1)) % POS_DEV
        items = jnp.arange(POS_DEV)
        col_start = jnp.where(items == low_item, 0, jnp.where(items == high_item, NX - PATCH, col_start))
        rows_out = jnp.stack([top_strip * STRIP + row_within, col_start], axis=1)
        shuffle = jax.random.permutation(keys[5], POS_DEV)
        return rows_out[shuffle]
    blocks_out = jax.vmap(one_block)(jax.random.split(key, block_count))
    return blocks_out.reshape(NPOS, 2).astype(jnp.int32)


def level_of(key, dims, shards, least, top_value):
    loudness, own = 1.0, jax.random.fold_in(key, 6)
    for axis_at, blocks in shards:
        draws = jnp.exp(jax.random.uniform(jax.random.fold_in(own, axis_at), (blocks,), jnp.float32, least / len(shards), top_value / len(shards)))
        loudness = loudness * jnp.repeat(draws, dims[axis_at] // blocks).reshape([-1 if axis == axis_at else 1 for axis in range(len(dims))])
    return loudness


def gaussian(rng, shape, deviation, limit, shards=(), kind=jnp.bfloat16):
    array = jax.random.normal(rng, shape, jnp.float32) * deviation
    if len(shards) > 0:
        array = level_of(rng, shape, shards, -0.22, 0.18) * array
    return jnp.clip(array, min=-limit, max=limit).astype(kind)


def setup_inputs(seed: int = 0) -> dict:
    streams_of = jax.random.split(jax.random.key(seed), 6)
    object_field = gaussian(streams_of[0], (2, SLICES, NX, NX), 0.7, 4.2, ((2, 16),), jnp.float32)
    probe_modes = gaussian(streams_of[1], (MODES, 2, PATCH, PATCH), 1.0, 6.0, (), jnp.float32)
    propagator_phase = jnp.clip(jax.random.uniform(streams_of[2], (PATCH, PATCH), jnp.float32, -3.140625, 3.140625), -3.140625, 3.140625)
    offsets = draw_offsets(jax.random.fold_in(streams_of[5], 71), 0)
    measured = jnp.clip(jnp.exp(math.log(20.0) - 3.6888795 * jax.random.uniform(streams_of[4], (NPOS, PATCH, PATCH), jnp.float32) ** level_of(streams_of[4], (NPOS, PATCH, PATCH), ((0, 128),), -0.2, 0.2)), 0.5, 20.0)
    return dict(object_field=object_field, probe_modes=probe_modes, propagator_phase=propagator_phase, offsets=offsets, measured=measured)


def dft_blocks(length, sign):
    index_row = jnp.arange(length, dtype=jnp.int32)
    phase_index = index_row[:, None] * index_row[None, :] % length
    angles = phase_index.astype(jnp.float32) * (2.0 * math.pi / length)
    scale_by = 1.0 / math.sqrt(length)
    cosine = jnp.cos(angles) * scale_by
    sine_part = -sign * jnp.sin(angles) * scale_by
    return jnp.stack([jnp.stack([cosine, -sine_part]), jnp.stack([sine_part, cosine])])

def transform(field, blocks):
    rows_done = jnp.einsum('caij,najk->ncik', blocks, field, precision=lax.Precision.HIGHEST)
    return jnp.einsum('naik,cakl->ncil', rows_done, blocks, precision=lax.Precision.HIGHEST)

def complex_product(left_factor, right_factor):
    real_part = left_factor[..., 0, :, :] * right_factor[..., 0, :, :] - left_factor[..., 1, :, :] * right_factor[..., 1, :, :]
    imag_part = left_factor[..., 0, :, :] * right_factor[..., 1, :, :] + left_factor[..., 1, :, :] * right_factor[..., 0, :, :]
    return jnp.stack([real_part, imag_part], axis=-3)

def window_loss(windows, probe_modes, kernel, amplitude, forward, inverse):
    position_count = windows.shape[0]
    mode_count = probe_modes.shape[0]
    length = probe_modes.shape[-1]
    wavefield = jnp.broadcast_to(probe_modes[None], (position_count,) + probe_modes.shape)
    for slice_index in range(windows.shape[2]):
        wavefield = complex_product(wavefield, windows[:, None, :, slice_index])
        if slice_index + 1 < windows.shape[2]:
            spectrum = transform(wavefield.reshape(position_count * mode_count, 2, length, length), forward)
            wavefield = transform(complex_product(spectrum, kernel), inverse).reshape(position_count, mode_count, 2, length, length)
    far_field = transform(wavefield.reshape(position_count * mode_count, 2, length, length), forward)
    intensity = 1.0 + lax.optimization_barrier(jnp.sum((far_field * far_field).reshape(position_count, mode_count * 2, length, length), axis=1))
    return jnp.sum((jnp.sqrt(intensity) - amplitude) ** 2)

def window_grads(windows, probe_modes, kernel, amplitude, forward, inverse):
    widened = windows.astype(jnp.float32)
    loss_value, pullback = jax.vjp(lambda window_f32: window_loss(window_f32, probe_modes, kernel, amplitude, forward, inverse), widened)
    return pullback(jnp.ones_like(loss_value))[0].astype(jnp.bfloat16)

def corner_index(row_start, col_start):
    zero_index = jnp.zeros((), jnp.int32)
    return (zero_index, zero_index, row_start.astype(jnp.int32), col_start.astype(jnp.int32))

def add_blocks(total, blocks, row_starts, col_starts):

    def add_one(item_index, running):
        item_index = item_index.astype(jnp.int32)
        block_f32 = blocks[item_index].astype(jnp.float32)
        corner = corner_index(row_starts[item_index], col_starts[item_index])
        current = lax.dynamic_slice(running, corner, block_f32.shape)
        return lax.dynamic_update_slice(running, current + block_f32, corner)
    return lax.fori_loop(0, blocks.shape[0], add_one, total)

def reference(object_field, probe_modes, propagator_phase, offsets, measured):
    rounded = object_field.astype(jnp.bfloat16)
    forward = dft_blocks(PATCH, 1.0)
    inverse = dft_blocks(PATCH, -1.0)
    kernel = jnp.stack([jnp.cos(propagator_phase), jnp.sin(propagator_phase)])
    amplitude = jnp.sqrt(measured)
    group_count = NPOS // POS_DEV
    offset_groups = offsets.reshape(group_count, POS_DEV, 2)
    amplitude_groups = amplitude.reshape(group_count, POS_DEV, PATCH, PATCH)

    def one_group(total, inputs):
        group_offsets, group_amplitude = inputs
        windows = jax.vmap(lambda corner: lax.dynamic_slice(rounded, corner_index(corner[0], corner[1]), (2, SLICES, PATCH, PATCH)))(group_offsets)
        window_grad = window_grads(windows, probe_modes, kernel, group_amplitude, forward, inverse)
        return (add_blocks(total, window_grad, group_offsets[:, 0], group_offsets[:, 1]), None)
    total, unused_out = lax.scan(one_group, jnp.zeros(object_field.shape, jnp.float32), (offset_groups, amplitude_groups))
    return total
```

```python
import functools
import math

import jax
import jax.numpy as jnp
import numpy as np
from jax import lax
from jax.experimental import pallas as pl
from jax.experimental.pallas import tpu as pltpu
from jax.sharding import PartitionSpec as P

CAP = 2
SIDE = 128
AMP = jnp.int16
AMP_MIDDLE, AMP_STEPS = 2.625, 16384.0
MESH = pl.DeviceIdType.MESH


def dft_operands():
    index = np.arange(SIDE)
    angles = (index[:, None] * index[None, :] % SIDE) * (2.0 * math.pi / SIDE)
    cosine = np.cos(angles) / math.sqrt(SIDE)
    sine = np.sin(angles) / math.sqrt(SIDE)

    def parts(block, axis):
        block = block.astype(np.float32)
        high = block.astype(jnp.bfloat16)
        low = (block - high.astype(np.float32)).astype(jnp.bfloat16)
        return np.concatenate([high, low, high], axis=axis)

    left, right = [], []
    for sign in (1.0, -1.0):
        s = sign * sine
        left.append(parts(np.block([[cosine, s], [-s, cosine]]), 1))
        right.append(parts(np.block([[cosine, -s], [s, cosine]]), 0))
    return np.stack(left), np.stack(right)


def coded(measured):
    return jnp.round((jnp.sqrt(measured) - AMP_MIDDLE) * AMP_STEPS).astype(jnp.int32).astype(AMP)


def decoded(code):
    return code.astype(jnp.int32).astype(jnp.float32) * (1.0 / AMP_STEPS) + AMP_MIDDLE


def split3(x, axis):
    high = x.astype(jnp.bfloat16)
    low = (x - high.astype(jnp.float32)).astype(jnp.bfloat16)
    return jnp.concatenate([high, high, low], axis=axis)


def transform2d(left, right, real, imag):
    fields = real.shape[1] // SIDE
    y = jnp.dot(left, split3(jnp.concatenate([real, imag], axis=0), 0), preferred_element_type=jnp.float32)
    rows = [
        jnp.concatenate([y[:SIDE, k * SIDE : (k + 1) * SIDE], y[SIDE:, k * SIDE : (k + 1) * SIDE]], axis=1)
        for k in range(fields)
    ]
    z = jnp.dot(split3(jnp.concatenate(rows, axis=0), 1), right, preferred_element_type=jnp.float32)
    out_real = jnp.concatenate([z[k * SIDE : (k + 1) * SIDE, :SIDE] for k in range(fields)], axis=1)
    out_imag = jnp.concatenate([z[k * SIDE : (k + 1) * SIDE, SIDE:] for k in range(fields)], axis=1)
    return out_real, out_imag


def grads_kernel(batch, own_ref, halo_ref, amp_ref, meta_ref, probe_ref, prop_ref, left_ref, right_ref, grad_ref, field, order):
    fields = 2 * batch

    def widen(index, _):
        plane, block = index // 16, index % 16
        columns = pl.ds(pl.multiple_of(block * SIDE, SIDE), SIDE)
        field[plane, block, :SIDE, :] = own_ref[plane, :, columns].astype(jnp.bfloat16).astype(jnp.float32)
        field[plane, block, SIDE:, :] = halo_ref[block // 2, plane, block % 2].astype(jnp.float32)
        grad_ref[plane, block] = jnp.zeros((2 * SIDE, SIDE), jnp.float32)
        return 0

    lax.fori_loop(0, 64, widen, 0)

    def collect(slot, count):
        order[count] = slot
        return count + (meta_ref[slot // 2, 0, slot % 2] > 0).astype(jnp.int32)

    count = lax.fori_loop(0, 32, collect, 0)
    lane = lax.broadcasted_iota(jnp.int32, (SIDE, SIDE), 1)

    def place(slot):
        code = jnp.maximum(meta_ref[slot // 2, 0, slot % 2] - 1, 0)
        row, col = code // 2048, code % 2048
        block, shift = col // SIDE, col % SIDE
        return pl.ds(row, SIDE), block, jnp.minimum(block + 1, 15), shift

    def cut(plane, where):
        rows, block, next_block, shift = where
        back = (SIDE - shift) % SIDE
        first = pltpu.roll(field[plane, block, rows, :], back, 1)
        second = pltpu.roll(field[plane, next_block, rows, :], back, 1)
        return jnp.where(lane < SIDE - shift, first, second)

    def add(plane, where, value):
        rows, block, next_block, shift = where
        moved = pltpu.roll(value.astype(jnp.bfloat16).astype(jnp.float32), shift, 1)
        zero = jnp.zeros_like(moved)
        grad_ref[plane, block, rows, :] += jnp.where(lane >= shift, moved, zero)
        grad_ref[plane, next_block, rows, :] += jnp.where(lane < shift, moved, zero)

    def side_by_side(parts):
        return jnp.concatenate(parts, axis=1)

    def step(index, _):
        slots, wheres, weights = [], [], []
        for k in range(batch):
            item = index * batch + k
            slot = order[jnp.minimum(item, count - 1)]
            slots.append(slot)
            wheres.append(place(slot))
            weights.append(jnp.where(item < count, 2.0, 0.0).astype(jnp.float32))
        t = [[cut(plane, where) for where in wheres] for plane in range(4)]
        t0r, t1r, t0i, t1i = [side_by_side([x for x in plane for _ in range(2)]) for plane in t]
        pr = side_by_side([probe_ref[0, 0], probe_ref[1, 0]] * batch)
        pi = side_by_side([probe_ref[0, 1], probe_ref[1, 1]] * batch)
        kr = side_by_side([prop_ref[0]] * fields)
        ki = side_by_side([prop_ref[1]] * fields)
        forward = (left_ref[0], right_ref[0])
        inverse = (left_ref[1], right_ref[1])
        wr, wi = pr * t0r - pi * t0i, pr * t0i + pi * t0r
        sr, si = transform2d(*forward, wr, wi)
        ur, ui = transform2d(*inverse, sr * kr - si * ki, sr * ki + si * kr)
        fr, fi = transform2d(*forward, ur * t1r - ui * t1i, ur * t1i + ui * t1r)
        power = fr * fr + fi * fi
        factors = []
        for k in range(batch):
            low = 2 * k * SIDE
            model = 1.0 + power[:, low : low + SIDE] + power[:, low + SIDE : low + 2 * SIDE]
            amplitude = decoded(amp_ref[slots[k]])
            factors += [weights[k] * (1.0 - amplitude * lax.rsqrt(model))] * 2
        q = side_by_side(factors)
        gr, gi = transform2d(*inverse, fr * q, fi * q)
        d1r, d1i = ur * gr + ui * gi, ur * gi - ui * gr
        hr, hi = transform2d(*forward, t1r * gr + t1i * gi, t1r * gi - t1i * gr)
        er, ei = transform2d(*inverse, kr * hr + ki * hi, kr * hi - ki * hr)
        d0r, d0i = pr * er + pi * ei, pr * ei - pi * er
        for k in range(batch):
            low = 2 * k * SIDE
            for plane, value in enumerate((d0r, d1r, d0i, d1i)):
                add(plane, wheres[k], value[:, low : low + SIDE] + value[:, low + SIDE : low + 2 * SIDE])
        return 0

    lax.fori_loop(0, (count + batch - 1) // batch, step, 0)


def grads_call(own, halo, amp, meta, probe, prop, batch=1):
    left, right = dft_operands()
    vmem = pl.BlockSpec(memory_space=pltpu.VMEM)
    return pl.pallas_call(
        functools.partial(grads_kernel, batch),
        out_shape=jax.ShapeDtypeStruct((4, 16, 2 * SIDE, SIDE), jnp.float32),
        in_specs=[vmem, vmem, vmem, pl.BlockSpec(memory_space=pltpu.SMEM)] + [vmem] * 4,
        out_specs=vmem,
        scratch_shapes=[pltpu.VMEM((4, 16, 2 * SIDE, SIDE), jnp.float32), pltpu.SMEM((33,), jnp.int32)],
        compiler_params=pltpu.CompilerParams(vmem_limit_bytes=56 * 2**20),
        name="window_gradients",
    )(own, halo, amp, meta, probe, prop, jnp.asarray(left), jnp.asarray(right))


def send_kernel(obj_ref, measured_ref, source_ref, code_ref, halo_ref, amp_ref, meta_ref, wide, chunk, amp_out, meta_out, local_sem, halo_send, halo_recv, amp_send, amp_recv, meta_send, meta_recv):
    strip, pos = lax.axis_index("obj"), lax.axis_index("pos")
    x, core = pos // 2, pos % 2
    load = pltpu.make_async_copy(obj_ref.at[:, :, pl.ds(pl.multiple_of(pos * 256, 256), 256)], wide, local_sem.at[0])
    load.start()
    barrier = pltpu.get_barrier_semaphore()

    def greet_strip(step, _):
        pl.semaphore_signal(barrier, inc=1, device_id=(lax.rem(strip + step, 16), pos), device_id_type=MESH)
        return 0

    lax.fori_loop(1, 16, greet_strip, 0)
    for step in range(1, 4):
        other = lax.rem(x + step, 4) * 2 + core
        pl.semaphore_signal(barrier, inc=1, device_id=(strip, other), device_id_type=MESH)
    twin = x * 2 + 1 - core
    pl.semaphore_signal(barrier, inc=1, device_id=(strip, twin), device_id_type=MESH)
    load.wait()
    for block in range(2):
        chunk[:, block] = wide[:, :, block * SIDE : (block + 1) * SIDE].astype(jnp.bfloat16)
    pl.semaphore_wait(barrier, 19)

    def forward_chunk(source, index, where, send):
        return pltpu.make_async_remote_copy(
            src_ref=source, dst_ref=halo_ref.at[index], send_sem=halo_send.at[send], recv_sem=halo_recv.at[index],
            device_id=where, device_id_type=MESH,
        )

    first = forward_chunk(chunk, pos, (lax.rem(strip + 15, 16), pos), 0)
    first.start()

    def amp_copy(target):
        return pltpu.make_async_remote_copy(
            src_ref=amp_out.at[target], dst_ref=amp_ref.at[strip], send_sem=amp_send.at[target], recv_sem=amp_recv.at[strip],
            device_id=(target, pos), device_id_type=MESH,
        )

    def meta_copy(target):
        return pltpu.make_async_remote_copy(
            src_ref=meta_out.at[target], dst_ref=meta_ref.at[strip], send_sem=meta_send.at[target], recv_sem=meta_recv.at[strip],
            device_id=(target, pos), device_id_type=MESH,
        )

    lane = lax.broadcasted_iota(jnp.int32, (8, SIDE), 1)

    def packed(target):
        codes = jnp.where(lane == 0, code_ref[2 * target], code_ref[2 * target + 1])
        values = [coded(measured_ref[source_ref[2 * target + k]]) for k in range(CAP)]
        return codes, values

    def pack(step, _):
        target = lax.rem(strip + step, 16)
        codes, values = packed(target)
        meta_out[target] = codes
        for k in range(CAP):
            amp_out[target, k] = values[k]
        amp_copy(target).start()
        meta_copy(target).start()
        return 0

    lax.fori_loop(1, 16, pack, 0)
    codes, values = packed(strip)
    meta_ref[strip] = codes
    for k in range(CAP):
        amp_ref[strip, k] = values[k]

    first.wait_recv()
    sends = [first]
    for step in (2, 1, 3):
        copy = forward_chunk(halo_ref.at[pos], pos, (strip, lax.rem(x + step, 4) * 2 + core), step)
        copy.start()
        sends.append(copy)
    copy = forward_chunk(halo_ref.at[pos], pos, (strip, twin), 4)
    copy.start()
    sends.append(copy)
    for step in (1, 3, 2):
        index = lax.rem(x + step, 4) * 2 + core
        forward_chunk(chunk, index, (strip, twin), 0).wait_recv()
        copy = forward_chunk(halo_ref.at[index], index, (strip, twin), 4 + step)
        copy.start()
        sends.append(copy)
    for step in range(4):
        index = lax.rem(x + step, 4) * 2 + 1 - core
        forward_chunk(chunk, index, (strip, twin), 0).wait_recv()

    def finish(step, _):
        target = lax.rem(strip + step, 16)
        source = lax.rem(strip + 16 - step, 16)
        amp_copy(target).wait_send()
        meta_copy(target).wait_send()
        pltpu.make_async_remote_copy(
            src_ref=amp_out.at[target], dst_ref=amp_ref.at[source], send_sem=amp_send.at[target], recv_sem=amp_recv.at[source],
            device_id=(target, pos), device_id_type=MESH,
        ).wait_recv()
        pltpu.make_async_remote_copy(
            src_ref=meta_out.at[target], dst_ref=meta_ref.at[source], send_sem=meta_send.at[target], recv_sem=meta_recv.at[source],
            device_id=(target, pos), device_id_type=MESH,
        ).wait_recv()
        return 0

    lax.fori_loop(1, 16, finish, 0)
    for copy in sends:
        copy.wait_send()


def send_call(obj, measured, source, code):
    vmem = pl.BlockSpec(memory_space=pltpu.VMEM)
    smem = pl.BlockSpec(memory_space=pltpu.SMEM)
    dma = pltpu.SemaphoreType.DMA
    return pl.pallas_call(
        send_kernel,
        out_shape=(
            jax.ShapeDtypeStruct((8, 4, 2, SIDE, SIDE), jnp.bfloat16),
            jax.ShapeDtypeStruct((16, CAP, SIDE, SIDE), AMP),
            jax.ShapeDtypeStruct((16, 8, SIDE), jnp.int32),
        ),
        in_specs=[pl.BlockSpec(memory_space=pl.ANY), vmem, smem, smem],
        out_specs=(vmem, vmem, vmem),
        scratch_shapes=[
            pltpu.VMEM((4, SIDE, 256), jnp.float32),
            pltpu.VMEM((4, 2, SIDE, SIDE), jnp.bfloat16),
            pltpu.VMEM((16, CAP, SIDE, SIDE), AMP),
            pltpu.VMEM((16, 8, SIDE), jnp.int32),
            dma((1,)),
            dma((8,)),
            dma((8,)),
            dma((16,)),
            dma((16,)),
            dma((16,)),
            dma((16,)),
        ],
        compiler_params=pltpu.CompilerParams(collective_id=0, has_side_effects=True, vmem_limit_bytes=32 * 2**20),
        name="exchange_inputs",
    )(obj, measured, source, code)


def sum_kernel(grad_ref, out_ref, half, summed, parts, low_in, low_out, total, twin_send, twin_recv, x_send, x_recv, low_send, low_recv):
    strip, pos = lax.axis_index("obj"), lax.axis_index("pos")
    x, core = pos // 2, pos % 2
    twin = (strip, x * 2 + 1 - core)
    below, above = (lax.rem(strip + 1, 16), pos), (lax.rem(strip + 15, 16), pos)
    barrier = pltpu.get_barrier_semaphore()
    peers = [(strip, lax.rem(x + step, 4) * 2 + core) for step in range(4)]
    for device in (twin, below, above, *peers[1:]):
        pl.semaphore_signal(barrier, inc=1, device_id=device, device_id_type=MESH)
    pl.semaphore_wait(barrier, 6)

    def columns(step, side):
        return pl.ds(lax.rem(x + step, 4) * 4 + 2 * side, 2)

    steps = (2, 1, 3, 0)
    twin_copies = {}
    for step in steps:
        copy = pltpu.make_async_remote_copy(
            src_ref=grad_ref.at[:, columns(step, 1 - core)], dst_ref=half.at[step], send_sem=twin_send.at[step],
            recv_sem=twin_recv.at[step], device_id=twin, device_id_type=MESH,
        )
        copy.start()
        twin_copies[step] = copy
    x_copies = {}
    for step in steps:
        twin_copies[step].wait_recv()
        first = lax.rem(x + step, 4) * 4 + 2 * core
        if step:
            for plane in range(4):
                for block in range(2):
                    summed[step - 1, plane, block] = (grad_ref[plane, first + block] + half[step, plane, block]).astype(jnp.bfloat16)
            copy = pltpu.make_async_remote_copy(
                src_ref=summed.at[step - 1], dst_ref=parts.at[step - 1], send_sem=x_send.at[step - 1],
                recv_sem=x_recv.at[step - 1], device_id=peers[step], device_id_type=MESH,
            )
            copy.start()
            x_copies[step] = copy
        else:
            for plane in range(4):
                for block in range(2):
                    total[plane, block] = grad_ref[plane, first + block] + half[step, plane, block]
    for step in (1, 3, 2):
        x_copies[step].wait_recv()
    for plane in range(4):
        for block in range(2):
            value = total[plane, block, SIDE:]
            for step in range(3):
                value += parts[step, plane, block, SIDE:].astype(jnp.float32)
            low_out[plane, block] = value.astype(jnp.bfloat16)
    copy = pltpu.make_async_remote_copy(
        src_ref=low_out, dst_ref=low_in, send_sem=low_send, recv_sem=low_recv, device_id=below, device_id_type=MESH,
    )
    copy.start()
    for plane in range(4):
        for block in range(2):
            value = total[plane, block, :SIDE]
            for step in range(3):
                value += parts[step, plane, block, :SIDE].astype(jnp.float32)
            total[plane, block, :SIDE] = value
    copy.wait_recv()
    for plane in range(4):
        for block in range(2):
            out_ref[plane, :, block * SIDE : (block + 1) * SIDE] = total[plane, block, :SIDE] + low_in[plane, block].astype(jnp.float32)
    copy.wait_send()
    for step in steps:
        twin_copies[step].wait_send()
    for step in (1, 2, 3):
        x_copies[step].wait_send()


def sum_call(grad):
    vmem = pl.BlockSpec(memory_space=pltpu.VMEM)
    dma = pltpu.SemaphoreType.DMA
    return pl.pallas_call(
        sum_kernel,
        out_shape=jax.ShapeDtypeStruct((4, SIDE, 256), jnp.float32),
        in_specs=[vmem],
        out_specs=vmem,
        scratch_shapes=[
            pltpu.VMEM((4, 4, 2, 2 * SIDE, SIDE), jnp.float32),
            pltpu.VMEM((3, 4, 2, 2 * SIDE, SIDE), jnp.bfloat16),
            pltpu.VMEM((3, 4, 2, 2 * SIDE, SIDE), jnp.bfloat16),
            pltpu.VMEM((4, 2, SIDE, SIDE), jnp.bfloat16),
            pltpu.VMEM((4, 2, SIDE, SIDE), jnp.bfloat16),
            pltpu.VMEM((4, 2, 2 * SIDE, SIDE), jnp.float32),
            dma((4,)),
            dma((4,)),
            dma((3,)),
            dma((3,)),
            dma,
            dma,
        ],
        compiler_params=pltpu.CompilerParams(collective_id=1, has_side_effects=True, vmem_limit_bytes=32 * 2**20),
        name="sum_gradients",
    )(grad)


def per_device(object_field, probe_modes, propagator_phase, offsets, measured):
    obj = object_field.reshape(4, SIDE, object_field.shape[3])
    position = jnp.arange(offsets.shape[0], dtype=jnp.int32)
    top = offsets[:, 0] // SIDE
    earlier = (top[:, None] == top[None, :]) & (position[:, None] > position[None, :])
    slot = top * CAP + jnp.sum(earlier.astype(jnp.int32), axis=1)
    chosen = (slot[None, :] == jnp.arange(16 * CAP, dtype=jnp.int32)[:, None]).astype(jnp.int32)
    source = jnp.sum(chosen * position[None, :], axis=1)
    code = jnp.sum(chosen * (1 + (offsets[:, 0] % SIDE) * 2048 + offsets[:, 1])[None, :], axis=1)
    prop = jnp.stack([jnp.cos(propagator_phase), jnp.sin(propagator_phase)])
    halo, amp, meta = send_call(obj, measured, source, code)
    grad = grads_call(obj, halo, amp.reshape(16 * CAP, SIDE, SIDE), meta, probe_modes, prop)
    return sum_call(grad).reshape(2, 2, SIDE, 256)


def solution(mesh):
    placed = (
        P(None, None, "obj", None),
        P(),
        P(),
        P(("obj", "pos"), None),
        P(("obj", "pos"), None, None),
    )
    return jax.shard_map(
        per_device,
        mesh=mesh,
        in_specs=placed,
        out_specs=P(None, None, "obj", "pos"),
        check_vma=False,
    )
```

```python
import functools
import math

import jax
import jax.numpy as jnp
import numpy as np
from jax import lax
from jax.experimental import pallas as pl
from jax.experimental.pallas import tpu as pltpu
from jax.sharding import PartitionSpec as P

CAP = 2
SIDE = 128
SPAN = 10
LOW_COL, HIGH_COL = 768, 1152
AMP = jnp.int16
AMP_MIDDLE, AMP_STEPS = 2.625, 16384.0
MESH = pl.DeviceIdType.MESH


def dft_operands():
    index = np.arange(SIDE)
    angles = (index[:, None] * index[None, :] % SIDE) * (2.0 * math.pi / SIDE)
    cosine = np.cos(angles) / math.sqrt(SIDE)
    sine = np.sin(angles) / math.sqrt(SIDE)

    def parts(block, axis):
        block = block.astype(np.float32)
        high = block.astype(jnp.bfloat16)
        low = (block - high.astype(np.float32)).astype(jnp.bfloat16)
        return np.concatenate([high, low, high], axis=axis)

    left, right = [], []
    for sign in (1.0, -1.0):
        s = sign * sine
        left.append(parts(np.block([[cosine, s], [-s, cosine]]), 1))
        right.append(parts(np.block([[cosine, -s], [s, cosine]]), 0))
    return np.stack(left), np.stack(right)


def coded(measured):
    return jnp.round((jnp.sqrt(measured) - AMP_MIDDLE) * AMP_STEPS).astype(jnp.int32).astype(AMP)


def decoded(code):
    return code.astype(jnp.int32).astype(jnp.float32) * (1.0 / AMP_STEPS) + AMP_MIDDLE


def split3(x, axis):
    high = x.astype(jnp.bfloat16)
    low = (x - high.astype(jnp.float32)).astype(jnp.bfloat16)
    return jnp.concatenate([high, high, low], axis=axis)


def transform2d(left, right, which, real, imag):
    fields = real.shape[1] // SIDE
    y = jnp.dot(left[which], split3(jnp.concatenate([real, imag], axis=0), 0), preferred_element_type=jnp.float32)
    yield
    rows = [
        jnp.concatenate([y[:SIDE, k * SIDE : (k + 1) * SIDE], y[SIDE:, k * SIDE : (k + 1) * SIDE]], axis=1)
        for k in range(fields)
    ]
    z = jnp.dot(split3(jnp.concatenate(rows, axis=0), 1), right[which], preferred_element_type=jnp.float32)
    yield
    out_real = jnp.concatenate([z[k * SIDE : (k + 1) * SIDE, :SIDE] for k in range(fields)], axis=1)
    out_imag = jnp.concatenate([z[k * SIDE : (k + 1) * SIDE, SIDE:] for k in range(fields)], axis=1)
    return out_real, out_imag


def grads_kernel(obj_ref, halo_ref, amp_hbm, meta_ref, probe_hbm, phase_hbm, left_hbm, right_hbm, grad_hbm,
                 field, grad, own, halo, amp, probe, phase, left_ref, right_ref, prop_ref, packed, order, sems, out_sem):
    core = lax.axis_index("pos") % 2
    base = 6 * core
    columns = pl.ds(pl.multiple_of(base * SIDE, SIDE), SPAN * SIDE)
    loads = [
        pltpu.make_async_copy(source, target, sems.at[k])
        for k, (source, target) in enumerate([
            (obj_ref.at[:, :, columns], own),
            (halo_ref, halo),
            (phase_hbm, phase),
            (probe_hbm, probe),
            (left_hbm, left_ref),
            (right_hbm, right_ref),
            (amp_hbm, amp),
        ])
    ]
    for load in loads:
        load.start()

    def read(slot):
        code = meta_ref[slot // 32, slot % 32 // 2, 0, slot % 2] - 1
        return code >= 0, code // 2048, code % 2048

    def tally(slot, counts):
        valid, _, col = read(slot)
        here = valid.astype(jnp.int32)
        first = here * (col < LOW_COL).astype(jnp.int32)
        last = here * (col > HIGH_COL).astype(jnp.int32)
        return counts[0] + here, counts[1] + first, counts[2] + last

    whole, first_only, last_only = lax.fori_loop(0, 64, tally, (0, 0, 0))
    either = whole - first_only - last_only
    to_first = jnp.clip((whole + 1) // 2 - first_only, 0, either)

    def collect(slot, state):
        count, seen = state
        valid, _, col = read(slot)
        free = (col >= LOW_COL) & (col <= HIGH_COL)
        on_first = (col < LOW_COL) | (free & (seen < to_first))
        order[count] = slot
        mine = valid & (on_first == (core == 0))
        return count + mine.astype(jnp.int32), seen + (valid & free).astype(jnp.int32)

    count, _ = lax.fori_loop(0, 64, collect, (0, 0))
    loads[0].wait()
    loads[1].wait()

    def widen(index, _):
        plane, block = index // SPAN, index % SPAN
        inside = block + base - 8 * core
        within = (inside >= 0) & (inside < 8)
        extra = block + base - (8 - 2 * core)
        part = jnp.where(within, inside // 2, plane)
        tile = jnp.where(within, plane * 2 + inside % 2, 8 + extra)
        span = pl.ds(pl.multiple_of(block * SIDE, SIDE), SIDE)
        field[plane, block, :SIDE, :] = own[plane, :, span].astype(jnp.bfloat16).astype(jnp.float32)
        field[plane, block, SIDE:, :] = halo[part, tile].astype(jnp.float32)
        grad[block, plane] = jnp.zeros((2 * SIDE, SIDE), jnp.float32)
        return 0

    lax.fori_loop(0, 4 * SPAN, widen, 0)
    loads[2].wait()
    prop_ref[0] = jnp.cos(phase[...])
    prop_ref[1] = jnp.sin(phase[...])
    for load in loads[3:]:
        load.wait()
    lane = lax.broadcasted_iota(jnp.int32, (SIDE, SIDE), 1)

    def place(slot):
        valid, row, col = read(slot)
        row, col = jnp.where(valid, row, 0), jnp.where(valid, col, base * SIDE)
        block, shift = jnp.clip(col // SIDE - base, 0, SPAN - 1), col % SIDE
        return pl.ds(row, SIDE), block, jnp.minimum(block + 1, SPAN - 1), shift

    def cut(plane, where):
        rows, block, next_block, shift = where
        back = (SIDE - shift) % SIDE
        first = pltpu.roll(field[plane, block, rows, :], back, 1)
        second = pltpu.roll(field[plane, next_block, rows, :], back, 1)
        return jnp.where(lane < SIDE - shift, first, second)

    def add(plane, where, value):
        rows, block, next_block, shift = where
        moved = pltpu.roll(value.astype(jnp.bfloat16).astype(jnp.float32), shift, 1)
        zero = jnp.zeros_like(moved)
        grad[block, plane, rows, :] += jnp.where(lane >= shift, moved, zero)
        grad[next_block, plane, rows, :] += jnp.where(lane < shift, moved, zero)

    def pair(parts):
        return jnp.concatenate(parts, axis=1)

    forward = (left_ref, right_ref, 0)
    inverse = (left_ref, right_ref, 1)

    def stages(where, slot, weight):
        t0r, t1r, t0i, t1i = [pair([cut(plane, where)] * 2) for plane in range(4)]
        pr, pi = [pair([probe[0, k], probe[1, k]]) for k in range(2)]
        kr, ki = [pair([prop_ref[k]] * 2) for k in range(2)]
        wr, wi = pr * t0r - pi * t0i, pr * t0i + pi * t0r
        yield
        sr, si = yield from transform2d(*forward, wr, wi)
        ur, ui = yield from transform2d(*inverse, sr * kr - si * ki, sr * ki + si * kr)
        fr, fi = yield from transform2d(*forward, ur * t1r - ui * t1i, ur * t1i + ui * t1r)
        power = fr * fr + fi * fi
        model = 1.0 + power[:, :SIDE] + power[:, SIDE:]
        amplitude = decoded(amp[slot // 32, slot % 32 // 2, slot % 2])
        factor = pair([weight * (1.0 - amplitude * lax.rsqrt(model))] * 2)
        gr, gi = yield from transform2d(*inverse, fr * factor, fi * factor)
        for plane, value in ((1, ur * gr + ui * gi), (3, ur * gi - ui * gr)):
            add(plane, where, value[:, :SIDE] + value[:, SIDE:])
        hr, hi = yield from transform2d(*forward, t1r * gr + t1i * gi, t1r * gi - t1i * gr)
        er, ei = yield from transform2d(*inverse, kr * hr + ki * hi, kr * hi - ki * hr)
        for plane, value in ((0, pr * er + pi * ei), (2, pr * ei - pi * er)):
            add(plane, where, value[:, :SIDE] + value[:, SIDE:])

    def step(groups, start, index, _):
        running = []
        for group in range(groups):
            item = start + index * groups + group
            slot = order[jnp.minimum(item, count - 1)]
            weight = jnp.where(item < count, 2.0, 0.0).astype(jnp.float32)
            running.append(stages(place(slot), slot, weight))
        while running:
            running = [machine for machine in running if next(machine, 0) is None]
        return 0

    fours = (count + 1) // 4
    lax.fori_loop(0, fours, functools.partial(step, 4, 0), 0)
    rest = jnp.clip((count - 4 * fours + 1) // 2, 0, 1)
    lax.fori_loop(0, rest, functools.partial(step, 2, 4 * fours), 0)

    def give(block):
        return pltpu.make_async_copy(packed.at[block], grad_hbm.at[block], out_sem.at[block])

    def pack(block, _):
        packed[block] = grad[block].astype(jnp.bfloat16)
        give(block).start()
        return 0

    lax.fori_loop(0, SPAN, pack, 0)
    lax.fori_loop(0, SPAN, lambda block, _: (give(block).wait(), 0)[1], 0)


def grads_call(obj, halo, amp, meta, probe, phase):
    left, right = dft_operands()
    hbm = pl.BlockSpec(memory_space=pl.ANY)
    dma = pltpu.SemaphoreType.DMA
    return pl.pallas_call(
        grads_kernel,
        out_shape=jax.ShapeDtypeStruct((SPAN, 4, 2 * SIDE, SIDE), jnp.bfloat16),
        in_specs=[hbm, hbm, hbm, pl.BlockSpec(memory_space=pltpu.SMEM)] + [hbm] * 4,
        out_specs=hbm,
        scratch_shapes=[
            pltpu.VMEM((4, SPAN, 2 * SIDE, SIDE), jnp.float32),
            pltpu.VMEM((SPAN, 4, 2 * SIDE, SIDE), jnp.float32),
            pltpu.VMEM((4, SIDE, SPAN * SIDE), jnp.float32),
            pltpu.VMEM(halo.shape, halo.dtype),
            pltpu.VMEM(amp.shape, amp.dtype),
            pltpu.VMEM(probe.shape, probe.dtype),
            pltpu.VMEM(phase.shape, phase.dtype),
            pltpu.VMEM(left.shape, jnp.bfloat16),
            pltpu.VMEM(right.shape, jnp.bfloat16),
            pltpu.VMEM((2, SIDE, SIDE), jnp.float32),
            pltpu.VMEM((SPAN, 4, 2 * SIDE, SIDE), jnp.bfloat16),
            pltpu.SMEM((65,), jnp.int32),
            dma((7,)),
            dma((SPAN,)),
        ],
        compiler_params=pltpu.CompilerParams(vmem_limit_bytes=56 * 2**20),
        name="window_gradients",
    )(obj, halo, amp, meta, probe, phase, jnp.asarray(left), jnp.asarray(right))


def send_kernel(obj_ref, measured_ref, offsets_ref, halo_ref, amp_ref, meta_ref,
                wide, extra, measured, chunk, amp_out, meta_out, local_sem, halo_send, halo_recv, amp_send, amp_recv, meta_send, meta_recv, twin_send, twin_recv):
    strip, pos = lax.axis_index("obj"), lax.axis_index("pos")
    x, core = pos // 2, pos % 2
    twin = (strip, x * 2 + 1 - core)

    def span(block):
        return pl.ds(pl.multiple_of(block * SIDE, SIDE), 2 * SIDE)

    loads = [
        pltpu.make_async_copy(obj_ref.at[:, :, span(8 * core + 2 * x)], wide, local_sem.at[0]),
        pltpu.make_async_copy(obj_ref.at[x, :, span(8 - 2 * core)], extra, local_sem.at[1]),
        pltpu.make_async_copy(measured_ref, measured, local_sem.at[2]),
    ]
    for load in loads:
        load.start()
    barrier = pltpu.get_barrier_semaphore()

    def greet_strip(step, _):
        pl.semaphore_signal(barrier, inc=1, device_id=(lax.rem(strip + step, 16), pos), device_id_type=MESH)
        return 0

    lax.fori_loop(1, 16, greet_strip, 0)
    for step in range(1, 4):
        other = lax.rem(x + step, 4) * 2 + core
        pl.semaphore_signal(barrier, inc=1, device_id=(strip, other), device_id_type=MESH)
    pl.semaphore_signal(barrier, inc=1, device_id=twin, device_id_type=MESH)
    loads[0].wait()
    loads[1].wait()
    for block in range(2):
        lanes = slice(block * SIDE, (block + 1) * SIDE)
        for plane in range(4):
            chunk[plane * 2 + block] = wide[plane, :, lanes].astype(jnp.bfloat16)
        chunk[8 + block] = extra[:, lanes].astype(jnp.bfloat16)
    pl.semaphore_wait(barrier, 19)

    def spread(source, index, where, send):
        return pltpu.make_async_remote_copy(
            src_ref=source, dst_ref=halo_ref.at[index], send_sem=halo_send.at[send], recv_sem=halo_recv.at[index],
            device_id=where, device_id_type=MESH,
        )

    first = spread(chunk, x, (lax.rem(strip + 15, 16), pos), 0)
    first.start()

    def amp_copy(target, source):
        return pltpu.make_async_remote_copy(
            src_ref=amp_out.at[target], dst_ref=amp_ref.at[core, source], send_sem=amp_send.at[target],
            recv_sem=amp_recv.at[source], device_id=(target, pos), device_id_type=MESH,
        )

    def meta_copy(target, source):
        return pltpu.make_async_remote_copy(
            src_ref=meta_out.at[target], dst_ref=meta_ref.at[core, source], send_sem=meta_send.at[target],
            recv_sem=meta_recv.at[source], device_id=(target, pos), device_id_type=MESH,
        )

    def to_twin(source, side):
        return pltpu.make_async_remote_copy(
            src_ref=amp_ref.at[core, source], dst_ref=amp_ref.at[side, source], send_sem=twin_send.at[source],
            recv_sem=twin_recv.at[source], device_id=twin, device_id_type=MESH,
        )

    def meta_to_twin(side):
        return pltpu.make_async_remote_copy(
            src_ref=meta_ref.at[core], dst_ref=meta_ref.at[side], send_sem=twin_send.at[16],
            recv_sem=twin_recv.at[16], device_id=twin, device_id_type=MESH,
        )

    lane = lax.broadcasted_iota(jnp.int32, (8, SIDE), 1)
    loads[2].wait()

    def packed(target):
        where, codes, seen = [jnp.int32(0)] * CAP, [jnp.int32(0)] * CAP, jnp.int32(0)
        for item in range(offsets_ref.shape[0]):
            row, col = offsets_ref[item, 0], offsets_ref[item, 1]
            here = row // SIDE == target
            for k in range(CAP):
                take = here & (seen == k)
                where[k] = jnp.where(take, item, where[k])
                codes[k] = jnp.where(take, 1 + row % SIDE * 2048 + col, codes[k])
            seen = seen + here.astype(jnp.int32)
        return jnp.where(lane == 0, codes[0], codes[1]), [coded(measured[index]) for index in where]

    def pack(step, _):
        target = lax.rem(strip + step, 16)
        codes, values = packed(target)
        meta_out[target] = codes
        for k in range(CAP):
            amp_out[target, k] = values[k]
        amp_copy(target, strip).start()
        meta_copy(target, strip).start()
        return 0

    lax.fori_loop(1, 16, pack, 0)
    codes, values = packed(strip)
    meta_ref[core, strip] = codes
    for k in range(CAP):
        amp_ref[core, strip, k] = values[k]
    to_twin(strip, core).start()

    first.wait_recv()
    sends = [first]
    for step in (2, 1, 3):
        copy = spread(halo_ref.at[x], x, (strip, lax.rem(x + step, 4) * 2 + core), step)
        copy.start()
        sends.append(copy)

    def relay(step, _):
        source = lax.rem(strip + 16 - step, 16)
        amp_copy(source, source).wait_recv()
        meta_copy(source, source).wait_recv()
        to_twin(source, core).start()
        return 0

    lax.fori_loop(1, 16, relay, 0)
    meta_to_twin(core).start()

    def finish(step, _):
        target = lax.rem(strip + step, 16)
        amp_copy(target, strip).wait_send()
        meta_copy(target, strip).wait_send()
        return 0

    lax.fori_loop(1, 16, finish, 0)

    def finish_twin(source, _):
        to_twin(source, core).wait_send()
        to_twin(source, 1 - core).wait_recv()
        return 0

    lax.fori_loop(0, 16, finish_twin, 0)
    meta_to_twin(core).wait_send()
    meta_to_twin(1 - core).wait_recv()
    for step in (1, 3, 2):
        spread(chunk, lax.rem(x + step, 4), (strip, pos), 0).wait_recv()
    for copy in sends:
        copy.wait_send()


def send_call(obj, measured, offsets):
    hbm = pl.BlockSpec(memory_space=pl.ANY)
    vmem = pl.BlockSpec(memory_space=pltpu.VMEM)
    dma = pltpu.SemaphoreType.DMA
    return pl.pallas_call(
        send_kernel,
        out_shape=(
            jax.ShapeDtypeStruct((4, 10, SIDE, SIDE), jnp.bfloat16),
            jax.ShapeDtypeStruct((2, 16, CAP, SIDE, SIDE), AMP),
            jax.ShapeDtypeStruct((2, 16, 8, SIDE), jnp.int32),
        ),
        in_specs=[hbm, hbm, pl.BlockSpec(memory_space=pltpu.SMEM)],
        out_specs=(vmem, vmem, vmem),
        scratch_shapes=[
            pltpu.VMEM((4, SIDE, 2 * SIDE), jnp.float32),
            pltpu.VMEM((SIDE, 2 * SIDE), jnp.float32),
            pltpu.VMEM(measured.shape, jnp.float32),
            pltpu.VMEM((10, SIDE, SIDE), jnp.bfloat16),
            pltpu.VMEM((16, CAP, SIDE, SIDE), AMP),
            pltpu.VMEM((16, 8, SIDE), jnp.int32),
            dma((3,)),
            dma((4,)),
            dma((4,)),
            dma((16,)),
            dma((16,)),
            dma((16,)),
            dma((16,)),
            dma((17,)),
            dma((17,)),
        ],
        compiler_params=pltpu.CompilerParams(collective_id=0, has_side_effects=True, vmem_limit_bytes=40 * 2**20),
        name="exchange_inputs",
    )(obj, measured, offsets)


def sum_kernel(grad_ref, out_ref, mine, theirs, joined, parts, low_in, low_out, local_sem, twin_send, twin_recv, x_send, x_recv, low_send, low_recv):
    strip, pos = lax.axis_index("obj"), lax.axis_index("pos")
    x, core = pos // 2, pos % 2
    twin = (strip, x * 2 + 1 - core)
    below, above = (lax.rem(strip + 1, 16), pos), (lax.rem(strip + 15, 16), pos)
    shared = 3 - 3 * core
    load = pltpu.make_async_copy(grad_ref.at[pl.ds(2 * shared + 2 * core, 2)], mine, local_sem)
    load.start()
    barrier = pltpu.get_barrier_semaphore()
    for step in range(1, 8):
        pl.semaphore_signal(barrier, inc=1, device_id=(strip, lax.rem(pos + step, 8)), device_id_type=MESH)
    for device in (below, above):
        pl.semaphore_signal(barrier, inc=1, device_id=device, device_id_type=MESH)
    pl.semaphore_wait(barrier, 9)
    to_twin = pltpu.make_async_remote_copy(
        src_ref=grad_ref.at[pl.ds(8 - 8 * core, 2)], dst_ref=theirs, send_sem=twin_send, recv_sem=twin_recv,
        device_id=twin, device_id_type=MESH,
    )
    to_twin.start()
    halves = (pl.ds(SIDE, SIDE), pl.ds(0, SIDE))

    def remote(pair, source, half, target, start):
        return pltpu.make_async_remote_copy(
            src_ref=source.at[:, :, halves[half]], dst_ref=parts.at[start, half], send_sem=x_send.at[pair, half],
            recv_sem=x_recv.at[start, half], device_id=(strip, target), device_id_type=MESH,
        )

    def local(source, half):
        return pltpu.make_async_copy(source.at[:, :, halves[half]], parts.at[x, half], x_recv.at[x, half])

    def give(pair, source, half):
        target = 4 * core + pair

        @pl.when(target != pos)
        def _():
            remote(pair, source, half, target, x).start()

        @pl.when(target == pos)
        def _():
            local(source, half).start()

    def block_pair(pair):
        return grad_ref.at[pl.ds(2 * pair + 2 * core, 2)]

    pairs = [lax.rem(shared + step, 4) for step in range(1, 4)]
    for half in range(2):
        for pair in pairs:
            give(pair, block_pair(pair), half)
    load.wait()
    to_twin.wait_recv()
    for half in range(2):
        for block in range(2):
            for plane in range(4):
                rows = slice(SIDE, None) if half == 0 else slice(0, SIDE)
                joined[block, plane, rows] = (
                    mine[block, plane, rows].astype(jnp.float32) + theirs[block, plane, rows].astype(jnp.float32)
                ).astype(jnp.bfloat16)
        give(shared, joined, half)

    def arrived(half):
        for start in range(4):
            remote(0, joined, half, pos, start).wait_recv()

    def total(half, block, plane):
        value = parts[0, half, block, plane].astype(jnp.float32)
        for start in range(1, 4):
            value += parts[start, half, block, plane].astype(jnp.float32)
        return value

    arrived(0)
    for block in range(2):
        for plane in range(4):
            low_out[block, plane] = total(0, block, plane).astype(jnp.bfloat16)
    shift = pltpu.make_async_remote_copy(
        src_ref=low_out, dst_ref=low_in, send_sem=low_send, recv_sem=low_recv, device_id=below, device_id_type=MESH,
    )
    shift.start()
    arrived(1)
    shift.wait_recv()
    for block in range(2):
        for plane in range(4):
            out_ref[plane, :, block * SIDE : (block + 1) * SIDE] = total(1, block, plane) + low_in[block, plane].astype(jnp.float32)
    shift.wait_send()
    to_twin.wait_send()
    for half in range(2):
        for pair in range(4):
            target = 4 * core + pair

            @pl.when(target != pos)
            def _():
                remote(pair, joined, half, target, x).wait_send()


def sum_call(grad):
    dma = pltpu.SemaphoreType.DMA
    two = (2, 4, 2 * SIDE, SIDE)
    return pl.pallas_call(
        sum_kernel,
        out_shape=jax.ShapeDtypeStruct((4, SIDE, 2 * SIDE), jnp.float32),
        in_specs=[pl.BlockSpec(memory_space=pl.ANY)],
        out_specs=pl.BlockSpec(memory_space=pltpu.VMEM),
        scratch_shapes=[
            pltpu.VMEM(two, jnp.bfloat16),
            pltpu.VMEM(two, jnp.bfloat16),
            pltpu.VMEM(two, jnp.bfloat16),
            pltpu.VMEM((4, 2, 2, 4, SIDE, SIDE), jnp.bfloat16),
            pltpu.VMEM((2, 4, SIDE, SIDE), jnp.bfloat16),
            pltpu.VMEM((2, 4, SIDE, SIDE), jnp.bfloat16),
            dma,
            dma,
            dma,
            dma((4, 2)),
            dma((4, 2)),
            dma,
            dma,
        ],
        compiler_params=pltpu.CompilerParams(collective_id=1, has_side_effects=True, vmem_limit_bytes=40 * 2**20),
        name="sum_gradients",
    )(grad)


def per_device(object_field, probe_modes, propagator_phase, offsets, measured):
    obj = object_field.reshape(4, SIDE, object_field.shape[3])
    halo, amp, meta = send_call(obj, measured, offsets)
    grad = grads_call(obj, halo, amp, meta, probe_modes, propagator_phase)
    return sum_call(grad).reshape(2, 2, SIDE, 2 * SIDE)


def solution(mesh):
    placed = (
        P(None, None, "obj", None),
        P(),
        P(),
        P(("obj", "pos"), None),
        P(("obj", "pos"), None, None),
    )
    return jax.shard_map(
        per_device,
        mesh=mesh,
        in_specs=placed,
        out_specs=P(None, None, "obj", "pos"),
        check_vma=False,
    )
```

```python
import functools
import math

import jax
import jax.numpy as jnp
import numpy as np
from jax import lax
from jax.experimental import pallas as pl
from jax.experimental.pallas import tpu as pltpu
from jax.sharding import PartitionSpec as P

CAP = 2
SIDE = 128
META_TILE = (1, 128)
PIECES = 5
K2_LIMIT = 30
SPAN = 10
LOW_COL, HIGH_COL = 768, 1152
AMP = jnp.int16
AMP_MIDDLE, AMP_STEPS = 2.625, 16384.0
MESH = pl.DeviceIdType.MESH


def dft_operands():
    index = np.arange(SIDE)
    angles = (index[:, None] * index[None, :] % SIDE) * (2.0 * math.pi / SIDE)
    cosine = np.cos(angles) / math.sqrt(SIDE)
    sine = np.sin(angles) / math.sqrt(SIDE)

    def parts(block, axis):
        block = block.astype(np.float32)
        high = block.astype(jnp.bfloat16)
        low = (block - high.astype(np.float32)).astype(jnp.bfloat16)
        return np.concatenate([high, low, high], axis=axis)

    left, right = [], []
    for sign in (1.0, -1.0):
        s = sign * sine
        left.append(parts(np.block([[cosine, s], [-s, cosine]]), 1))
        right.append(parts(np.block([[cosine, -s], [s, cosine]]), 0))
    return np.stack(left), np.stack(right)


def coded(measured):
    return jnp.round((jnp.sqrt(measured) - AMP_MIDDLE) * AMP_STEPS).astype(jnp.int32).astype(AMP)


def decoded(code):
    return code.astype(jnp.int32).astype(jnp.float32) * (1.0 / AMP_STEPS) + AMP_MIDDLE


def split3(x, axis):
    high = x.astype(jnp.bfloat16)
    low = (x - high.astype(jnp.float32)).astype(jnp.bfloat16)
    return jnp.concatenate([high, high, low], axis=axis)


def transform2d(left, right, which, real, imag):
    fields = real.shape[1] // SIDE
    y = jnp.dot(left[which], split3(jnp.concatenate([real, imag], axis=0), 0), preferred_element_type=jnp.float32)
    yield
    rows = [
        jnp.concatenate([y[:SIDE, k * SIDE : (k + 1) * SIDE], y[SIDE:, k * SIDE : (k + 1) * SIDE]], axis=1)
        for k in range(fields)
    ]
    z = jnp.dot(split3(jnp.concatenate(rows, axis=0), 1), right[which], preferred_element_type=jnp.float32)
    yield
    out_real = jnp.concatenate([z[k * SIDE : (k + 1) * SIDE, :SIDE] for k in range(fields)], axis=1)
    out_imag = jnp.concatenate([z[k * SIDE : (k + 1) * SIDE, SIDE:] for k in range(fields)], axis=1)
    return out_real, out_imag


def grads_kernel(obj_ref, halo, amp, meta_hbm, probe, phase, left_hbm, right_hbm, packed,
                 field, grad, prop_ref, left_ref, right_ref, meta_ref, order, sems):
    core = lax.axis_index("pos") % 2
    base = 6 * core
    meta_load = pltpu.make_async_copy(meta_hbm, meta_ref, sems.at[0])
    meta_load.start()
    left_load = pltpu.make_async_copy(left_hbm, left_ref, sems.at[1])
    left_load.start()
    right_load = pltpu.make_async_copy(right_hbm, right_ref, sems.at[2])
    right_load.start()

    def widen(index, _):
        plane, block = index // SPAN, index % SPAN
        inside = block + base - 8 * core
        within = (inside >= 0) & (inside < 8)
        extra = block + base - (8 - 2 * core)
        part = jnp.where(within, inside // 2, plane)
        tile = jnp.where(within, plane * 2 + inside % 2, 8 + extra)
        span = pl.ds(pl.multiple_of((base + block) * SIDE, SIDE), SIDE)
        field[plane, block, :SIDE, :] = obj_ref[plane, :, span].astype(jnp.bfloat16).astype(jnp.float32)
        field[plane, block, SIDE:, :] = halo[part, tile].astype(jnp.float32)
        grad[block, plane] = jnp.zeros((2 * SIDE, SIDE), jnp.float32)
        return 0

    lax.fori_loop(0, 4 * SPAN, widen, 0)
    prop_ref[0] = jnp.cos(phase[...])
    prop_ref[1] = jnp.sin(phase[...])
    meta_load.wait()
    left_load.wait()
    right_load.wait()

    def read(slot):
        code = meta_ref[slot // 32, slot % 32 // 2, 0, slot % 2] - 1
        return code >= 0, code // 2048, code % 2048

    def tally(slot, counts):
        valid, _, col = read(slot)
        here = valid.astype(jnp.int32)
        first = here * (col < LOW_COL).astype(jnp.int32)
        last = here * (col > HIGH_COL).astype(jnp.int32)
        return counts[0] + here, counts[1] + first, counts[2] + last

    whole, first_only, last_only = lax.fori_loop(0, 64, tally, (0, 0, 0), unroll=8)
    either = whole - first_only - last_only
    to_first = jnp.clip((whole + 1) // 2 - first_only, 0, either)

    def collect(slot, state):
        count, seen = state
        valid, _, col = read(slot)
        free = (col >= LOW_COL) & (col <= HIGH_COL)
        on_first = (col < LOW_COL) | (free & (seen < to_first))
        order[count] = slot
        mine = valid & (on_first == (core == 0))
        return count + mine.astype(jnp.int32), seen + (valid & free).astype(jnp.int32)

    count, _ = lax.fori_loop(0, 64, collect, (0, 0), unroll=8)
    lane = lax.broadcasted_iota(jnp.int32, (SIDE, SIDE), 1)

    def place(slot):
        valid, row, col = read(slot)
        row, col = jnp.where(valid, row, 0), jnp.where(valid, col, base * SIDE)
        block, shift = jnp.clip(col // SIDE - base, 0, SPAN - 1), col % SIDE
        return pl.ds(row, SIDE), block, jnp.minimum(block + 1, SPAN - 1), shift

    def cut(plane, where):
        rows, block, next_block, shift = where
        back = (SIDE - shift) % SIDE
        first = pltpu.roll(field[plane, block, rows, :], back, 1)
        second = pltpu.roll(field[plane, next_block, rows, :], back, 1)
        return jnp.where(lane < SIDE - shift, first, second)

    def add(plane, where, value):
        rows, block, next_block, shift = where
        moved = pltpu.roll(value.astype(jnp.bfloat16).astype(jnp.float32), shift, 1)
        zero = jnp.zeros_like(moved)
        grad[block, plane, rows, :] += jnp.where(lane >= shift, moved, zero)
        grad[next_block, plane, rows, :] += jnp.where(lane < shift, moved, zero)

    def pair(parts):
        return jnp.concatenate(parts, axis=1)

    forward = (left_ref, right_ref, 0)
    inverse = (left_ref, right_ref, 1)

    def stages(where, slot, weight):
        t0r, t1r, t0i, t1i = [pair([cut(plane, where)] * 2) for plane in range(4)]
        pr, pi = [pair([probe[0, k], probe[1, k]]) for k in range(2)]
        kr, ki = [pair([prop_ref[k]] * 2) for k in range(2)]
        wr, wi = pr * t0r - pi * t0i, pr * t0i + pi * t0r
        yield
        sr, si = yield from transform2d(*forward, wr, wi)
        ur, ui = yield from transform2d(*inverse, sr * kr - si * ki, sr * ki + si * kr)
        fr, fi = yield from transform2d(*forward, ur * t1r - ui * t1i, ur * t1i + ui * t1r)
        power = fr * fr + fi * fi
        model = 1.0 + power[:, :SIDE] + power[:, SIDE:]
        amplitude = decoded(amp[slot // 32, slot % 32 // 2, slot % 2])
        factor = pair([weight * (1.0 - amplitude * lax.rsqrt(model))] * 2)
        gr, gi = yield from transform2d(*inverse, fr * factor, fi * factor)
        for plane, value in ((1, ur * gr + ui * gi), (3, ur * gi - ui * gr)):
            add(plane, where, value[:, :SIDE] + value[:, SIDE:])
        hr, hi = yield from transform2d(*forward, t1r * gr + t1i * gi, t1r * gi - t1i * gr)
        er, ei = yield from transform2d(*inverse, kr * hr + ki * hi, kr * hi - ki * hr)
        for plane, value in ((0, pr * er + pi * ei), (2, pr * ei - pi * er)):
            add(plane, where, value[:, :SIDE] + value[:, SIDE:])

    def step(groups, start, index, _):
        running = []
        for group in range(groups):
            item = start + index * groups + group
            slot = order[jnp.minimum(item, count - 1)]
            weight = jnp.where(item < count, 2.0, 0.0).astype(jnp.float32)
            running.append(stages(place(slot), slot, weight))
        while running:
            running = [machine for machine in running if next(machine, 0) is None]
        return 0

    fours = (count + 1) // 4
    lax.fori_loop(0, fours, functools.partial(step, 4, 0), 0)
    rest = jnp.clip((count - 4 * fours + 1) // 2, 0, 1)
    lax.fori_loop(0, rest, functools.partial(step, 2, 4 * fours), 0)

    def pack(block, _):
        packed[block] = grad[block].astype(jnp.bfloat16)
        return 0

    lax.fori_loop(0, SPAN, pack, 0)


def grads_call(obj, halo, amp, meta, probe, phase):
    left, right = [pltpu.with_memory_space_constraint(jnp.asarray(x), pltpu.HBM) for x in dft_operands()]
    hbm = pl.BlockSpec(memory_space=pltpu.HBM)
    vmem = pl.BlockSpec(memory_space=pltpu.VMEM)
    return pl.pallas_call(
        grads_kernel,
        out_shape=jax.ShapeDtypeStruct((SPAN, 4, 2 * SIDE, SIDE), jnp.bfloat16),
        in_specs=[vmem] * 6 + [hbm] * 2,
        out_specs=vmem,
        scratch_shapes=[
            pltpu.VMEM((4, SPAN, 2 * SIDE, SIDE), jnp.float32),
            pltpu.VMEM((SPAN, 4, 2 * SIDE, SIDE), jnp.float32),
            pltpu.VMEM((2, SIDE, SIDE), jnp.float32),
            pltpu.VMEM(left.shape, jnp.bfloat16),
            pltpu.VMEM(right.shape, jnp.bfloat16),
            pltpu.SMEM(meta.shape, jnp.int32),
            pltpu.SMEM((65,), jnp.int32),
            pltpu.SemaphoreType.DMA((3,)),
        ],
        compiler_params=pltpu.CompilerParams(vmem_limit_bytes=K2_LIMIT * 2**20),
        name="window_gradients",
    )(obj, halo, amp, meta, probe, phase, left, right)


def send_kernel(obj_ref, measured_ref, offsets_ref, halo_ref, amp_ref, meta_ref,
                wide, extra, measured, chunk, amp_out, meta_out, local_sem, halo_send, halo_recv, amp_send, amp_recv, meta_send, meta_recv, twin_send, twin_recv):
    strip, pos = lax.axis_index("obj"), lax.axis_index("pos")
    x, core = pos // 2, pos % 2
    twin = (strip, x * 2 + 1 - core)

    def span(block):
        return pl.ds(pl.multiple_of(block * SIDE, SIDE), 2 * SIDE)

    loads = [
        pltpu.make_async_copy(obj_ref.at[:, :, span(8 * core + 2 * x)], wide, local_sem.at[0]),
        pltpu.make_async_copy(obj_ref.at[x, :, span(8 - 2 * core)], extra, local_sem.at[1]),
        pltpu.make_async_copy(measured_ref, measured, local_sem.at[2]),
    ]
    for load in loads:
        load.start()
    barrier = pltpu.get_barrier_semaphore()

    def greet_strip(step, _):
        pl.semaphore_signal(barrier, inc=1, device_id=(lax.rem(strip + step, 16), pos), device_id_type=MESH)
        return 0

    lax.fori_loop(1, 16, greet_strip, 0)
    for step in range(1, 4):
        other = lax.rem(x + step, 4) * 2 + core
        pl.semaphore_signal(barrier, inc=1, device_id=(strip, other), device_id_type=MESH)
    pl.semaphore_signal(barrier, inc=1, device_id=twin, device_id_type=MESH)
    loads[0].wait()
    loads[1].wait()
    for block in range(2):
        lanes = slice(block * SIDE, (block + 1) * SIDE)
        for plane in range(4):
            chunk[plane * 2 + block] = wide[plane, :, lanes].astype(jnp.bfloat16)
        chunk[8 + block] = extra[:, lanes].astype(jnp.bfloat16)
    pl.semaphore_wait(barrier, 19)

    def piece(number):
        return pl.ds(number * (10 // PIECES), 10 // PIECES)

    def spread(source, index, number, where, send):
        return pltpu.make_async_remote_copy(
            src_ref=source.at[piece(number)], dst_ref=halo_ref.at[index, piece(number)], send_sem=halo_send.at[send, number],
            recv_sem=halo_recv.at[index, number], device_id=where, device_id_type=MESH,
        )

    above = (lax.rem(strip + 15, 16), pos)
    for number in range(PIECES):
        spread(chunk, x, number, above, 0).start()

    def amp_copy(target, source):
        return pltpu.make_async_remote_copy(
            src_ref=amp_out.at[target], dst_ref=amp_ref.at[core, source], send_sem=amp_send.at[target],
            recv_sem=amp_recv.at[source], device_id=(target, pos), device_id_type=MESH,
        )

    def meta_copy(target, source):
        return pltpu.make_async_remote_copy(
            src_ref=meta_out.at[target], dst_ref=meta_ref.at[core, source], send_sem=meta_send.at[target],
            recv_sem=meta_recv.at[source], device_id=(target, pos), device_id_type=MESH,
        )

    def to_twin(source, side):
        return pltpu.make_async_remote_copy(
            src_ref=amp_ref.at[core, source], dst_ref=amp_ref.at[side, source], send_sem=twin_send.at[source],
            recv_sem=twin_recv.at[source], device_id=twin, device_id_type=MESH,
        )

    def meta_to_twin(side):
        return pltpu.make_async_remote_copy(
            src_ref=meta_ref.at[core], dst_ref=meta_ref.at[side], send_sem=twin_send.at[16],
            recv_sem=twin_recv.at[16], device_id=twin, device_id_type=MESH,
        )

    lane = lax.broadcasted_iota(jnp.int32, META_TILE, 1)
    loads[2].wait()

    def packed(target):
        where, codes, seen = [jnp.int32(0)] * CAP, [jnp.int32(0)] * CAP, jnp.int32(0)
        for item in range(offsets_ref.shape[1]):
            row, col = offsets_ref[0, item], offsets_ref[1, item]
            here = row // SIDE == target
            for k in range(CAP):
                take = here & (seen == k)
                where[k] = jnp.where(take, item, where[k])
                codes[k] = jnp.where(take, 1 + row % SIDE * 2048 + col, codes[k])
            seen = seen + here.astype(jnp.int32)
        return jnp.where(lane == 0, codes[0], codes[1]), [coded(measured[index]) for index in where]

    def pack(step, _):
        target = lax.rem(strip + step, 16)
        codes, values = packed(target)
        meta_out[target] = codes
        for k in range(CAP):
            amp_out[target, k] = values[k]
        amp_copy(target, strip).start()
        meta_copy(target, strip).start()
        return 0

    def forward(number):
        spread(chunk, x, number, above, 0).wait_recv()
        for step in (2, 1, 3):
            spread(halo_ref.at[x], x, number, (strip, lax.rem(x + step, 4) * 2 + core), step).start()

    bounds = [1, 6] + [6 + (10 * k) // PIECES for k in range(1, PIECES)] + [16]
    lax.fori_loop(bounds[0], bounds[1], pack, 0)
    for number in range(PIECES):
        forward(number)
        lax.fori_loop(bounds[number + 1], bounds[number + 2], pack, 0)
    codes, values = packed(strip)
    meta_ref[core, strip] = codes
    for k in range(CAP):
        amp_ref[core, strip, k] = values[k]
    to_twin(strip, core).start()

    def relay(step, _):
        source = lax.rem(strip + 16 - step, 16)
        amp_copy(source, source).wait_recv()
        meta_copy(source, source).wait_recv()
        to_twin(source, core).start()
        return 0

    lax.fori_loop(1, 16, relay, 0)
    meta_to_twin(core).start()

    def finish(step, _):
        target = lax.rem(strip + step, 16)
        amp_copy(target, strip).wait_send()
        meta_copy(target, strip).wait_send()
        return 0

    lax.fori_loop(1, 16, finish, 0)

    def finish_twin(source, _):
        to_twin(source, core).wait_send()
        to_twin(source, 1 - core).wait_recv()
        return 0

    lax.fori_loop(0, 16, finish_twin, 0)
    meta_to_twin(core).wait_send()
    meta_to_twin(1 - core).wait_recv()
    for number in range(PIECES):
        for step in range(1, 4):
            spread(chunk, lax.rem(x + step, 4), number, (strip, pos), 0).wait_recv()
        for step in range(4):
            spread(chunk, x, number, (strip, pos), step).wait_send()


def send_call(obj, measured, offsets):
    hbm = pl.BlockSpec(memory_space=pltpu.HBM)
    vmem = pl.BlockSpec(memory_space=pltpu.VMEM)
    dma = pltpu.SemaphoreType.DMA
    return pl.pallas_call(
        send_kernel,
        out_shape=(
            jax.ShapeDtypeStruct((4, 10, SIDE, SIDE), jnp.bfloat16),
            jax.ShapeDtypeStruct((2, 16, CAP, SIDE, SIDE), AMP),
            jax.ShapeDtypeStruct((2, 16, *META_TILE), jnp.int32),
        ),
        in_specs=[hbm, hbm, pl.BlockSpec(memory_space=pltpu.SMEM)],
        out_specs=(vmem, vmem, vmem),
        scratch_shapes=[
            pltpu.VMEM((4, SIDE, 2 * SIDE), jnp.float32),
            pltpu.VMEM((SIDE, 2 * SIDE), jnp.float32),
            pltpu.VMEM(measured.shape, jnp.float32),
            pltpu.VMEM((10, SIDE, SIDE), jnp.bfloat16),
            pltpu.VMEM((16, CAP, SIDE, SIDE), AMP),
            pltpu.VMEM((16, *META_TILE), jnp.int32),
            dma((3,)),
            dma((4, PIECES)),
            dma((4, PIECES)),
            dma((16,)),
            dma((16,)),
            dma((16,)),
            dma((16,)),
            dma((17,)),
            dma((17,)),
        ],
        compiler_params=pltpu.CompilerParams(collective_id=0, has_side_effects=True, vmem_limit_bytes=16 * 2**20),
        name="exchange_inputs",
    )(
        pltpu.with_memory_space_constraint(obj, pltpu.HBM), pltpu.with_memory_space_constraint(measured, pltpu.HBM), offsets
    )


def sum_kernel(grad_ref, out_ref, theirs, joined, parts, low_in, low_out, twin_send, twin_recv, x_send, x_recv, low_send, low_recv):
    strip, pos = lax.axis_index("obj"), lax.axis_index("pos")
    x, core = pos // 2, pos % 2
    twin = (strip, x * 2 + 1 - core)
    below, above = (lax.rem(strip + 1, 16), pos), (lax.rem(strip + 15, 16), pos)
    shared = 3 - 3 * core
    mine = 2 * shared + 2 * core
    barrier = pltpu.get_barrier_semaphore()
    for step in range(1, 8):
        pl.semaphore_signal(barrier, inc=1, device_id=(strip, lax.rem(pos + step, 8)), device_id_type=MESH)
    for device in (below, above):
        pl.semaphore_signal(barrier, inc=1, device_id=device, device_id_type=MESH)
    pl.semaphore_wait(barrier, 9)
    to_twin = pltpu.make_async_remote_copy(
        src_ref=grad_ref.at[pl.ds(8 - 8 * core, 2)], dst_ref=theirs, send_sem=twin_send, recv_sem=twin_recv,
        device_id=twin, device_id_type=MESH,
    )
    to_twin.start()
    halves = (pl.ds(SIDE, SIDE), pl.ds(0, SIDE))

    def remote(pair, source, half, target, start):
        return pltpu.make_async_remote_copy(
            src_ref=source.at[:, :, halves[half]], dst_ref=parts.at[start, half], send_sem=x_send.at[pair, half],
            recv_sem=x_recv.at[start, half], device_id=(strip, target), device_id_type=MESH,
        )

    def local(source, half):
        return pltpu.make_async_copy(source.at[:, :, halves[half]], parts.at[x, half], x_recv.at[x, half])

    def give(pair, source, half):
        target = 4 * core + pair

        @pl.when(target != pos)
        def _():
            remote(pair, source, half, target, x).start()

        @pl.when(target == pos)
        def _():
            local(source, half).start()

    def block_pair(pair):
        return grad_ref.at[pl.ds(2 * pair + 2 * core, 2)]

    pairs = [lax.rem(shared + step, 4) for step in range(1, 4)]
    for half in range(2):
        for pair in pairs:
            give(pair, block_pair(pair), half)
    to_twin.wait_recv()
    for half in range(2):
        for block in range(2):
            for plane in range(4):
                rows = slice(SIDE, None) if half == 0 else slice(0, SIDE)
                joined[block, plane, rows] = (
                    grad_ref[mine + block, plane, rows].astype(jnp.float32) + theirs[block, plane, rows].astype(jnp.float32)
                ).astype(jnp.bfloat16)
        give(shared, joined, half)

    def arrived(half):
        for start in range(4):
            remote(0, joined, half, pos, start).wait_recv()

    def total(half, block, plane):
        value = parts[0, half, block, plane].astype(jnp.float32)
        for start in range(1, 4):
            value += parts[start, half, block, plane].astype(jnp.float32)
        return value

    arrived(0)
    for block in range(2):
        for plane in range(4):
            low_out[block, plane] = total(0, block, plane).astype(jnp.bfloat16)
    shift = pltpu.make_async_remote_copy(
        src_ref=low_out, dst_ref=low_in, send_sem=low_send, recv_sem=low_recv, device_id=below, device_id_type=MESH,
    )
    shift.start()
    arrived(1)
    shift.wait_recv()
    for block in range(2):
        for plane in range(4):
            out_ref[plane, :, block * SIDE : (block + 1) * SIDE] = total(1, block, plane) + low_in[block, plane].astype(jnp.float32)
    shift.wait_send()
    to_twin.wait_send()
    for half in range(2):
        for pair in range(4):
            target = 4 * core + pair

            @pl.when(target != pos)
            def _():
                remote(pair, joined, half, target, x).wait_send()


def sum_call(grad):
    dma = pltpu.SemaphoreType.DMA
    two = (2, 4, 2 * SIDE, SIDE)
    return pl.pallas_call(
        sum_kernel,
        out_shape=jax.ShapeDtypeStruct((4, SIDE, 2 * SIDE), jnp.float32),
        in_specs=[pl.BlockSpec(memory_space=pltpu.VMEM)],
        out_specs=pl.BlockSpec(memory_space=pltpu.VMEM),
        scratch_shapes=[
            pltpu.VMEM(two, jnp.bfloat16),
            pltpu.VMEM(two, jnp.bfloat16),
            pltpu.VMEM((4, 2, 2, 4, SIDE, SIDE), jnp.bfloat16),
            pltpu.VMEM((2, 4, SIDE, SIDE), jnp.bfloat16),
            pltpu.VMEM((2, 4, SIDE, SIDE), jnp.bfloat16),
            dma,
            dma,
            dma((4, 2)),
            dma((4, 2)),
            dma,
            dma,
        ],
        compiler_params=pltpu.CompilerParams(collective_id=1, has_side_effects=True, vmem_limit_bytes=20 * 2**20),
        name="sum_gradients",
    )(grad)


def per_device(object_field, probe_modes, propagator_phase, offsets, measured):
    obj = object_field.reshape(4, SIDE, object_field.shape[3])
    halo, amp, meta = send_call(obj, measured, offsets.T)
    grad = grads_call(obj, halo, amp, meta, probe_modes, propagator_phase)
    return sum_call(grad).reshape(2, 2, SIDE, 2 * SIDE)


def solution(mesh):
    placed = (
        P(None, None, "obj", None),
        P(),
        P(),
        P(("obj", "pos"), None),
        P(("obj", "pos"), None, None),
    )
    return jax.shard_map(
        per_device,
        mesh=mesh,
        in_specs=placed,
        out_specs=P(None, None, "obj", "pos"),
        check_vma=False,
    )
```

```python
import functools
import math

import jax
import jax.numpy as jnp
import numpy as np
from jax import lax
from jax.experimental import pallas as pl
from jax.experimental.pallas import tpu as pltpu
from jax.sharding import PartitionSpec as P

CAP = 2
SIDE = 128
META_TILE = (1, 128)
PIECES = 5
K2_LIMIT = 30
SPAN = 10
LOW_COL, HIGH_COL = 768, 1152
AMP = jnp.int16
AMP_MIDDLE, AMP_STEPS = 2.625, 16384.0
MESH = pl.DeviceIdType.MESH


def dft_operands():
    index = np.arange(SIDE)
    angles = (index[:, None] * index[None, :] % SIDE) * (2.0 * math.pi / SIDE)
    wave = np.cos(angles) / math.sqrt(SIDE)
    wave[SIDE // 2 + 1 :] = np.sin(angles[1 : SIDE // 2]) / math.sqrt(SIDE)

    def product(block):
        block = block.astype(np.float32)
        high = block.astype(jnp.bfloat16)
        low = (block - high.astype(np.float32)).astype(jnp.bfloat16)
        return np.block([[high, high], [low, np.zeros_like(low)]])

    order = np.zeros((SIDE, SIDE), jnp.bfloat16)
    order[index, np.where(index <= SIDE // 2, index, SIDE + SIDE // 2 - index)] = 1
    return np.stack([product(wave), product(wave.T)]), order


def coded(measured):
    return jnp.round((jnp.sqrt(measured) - AMP_MIDDLE) * AMP_STEPS)


def decoded(code):
    return code.astype(jnp.int32).astype(jnp.float32) * (1.0 / AMP_STEPS) + AMP_MIDDLE


def multiply(left, planes):
    x = jnp.concatenate(planes, axis=1)
    high = x.astype(jnp.bfloat16)
    low = (x - high.astype(jnp.float32)).astype(jnp.bfloat16)
    y = jnp.dot(left, jnp.concatenate([high, low], axis=0), preferred_element_type=jnp.float32)
    y = y[:SIDE] + y[SIDE:]
    return [y[:, k * SIDE : (k + 1) * SIDE] for k in range(len(planes))]


def halves(plane):
    return plane[: SIDE // 2], plane[SIDE // 2 :]


def with_first_row(first, rest):
    row = lax.broadcasted_iota(jnp.int32, (8, SIDE), 0)
    return jnp.concatenate([jnp.where(row == 0, first[:8], rest[:8]), rest[8:]], axis=0)


def unfold(real, imag):
    (tr, br), (ti, bi) = halves(real), halves(imag)
    return (
        jnp.concatenate([with_first_row(tr, tr + bi), with_first_row(br, tr - bi)], axis=0),
        jnp.concatenate([with_first_row(ti, ti - br), with_first_row(bi, ti + br)], axis=0),
    )


def fold(real, imag):
    (tr, br), (ti, bi) = halves(real), halves(imag)
    return (
        jnp.concatenate([with_first_row(tr, tr + br), with_first_row(br, bi - ti)], axis=0),
        jnp.concatenate([with_first_row(ti, ti + bi), with_first_row(bi, tr - br)], axis=0),
    )


def to_frequency(waves, fields):
    for turn in (True, False):
        planes = multiply(waves[0], [plane for field in fields for plane in field])
        yield
        fields = [unfold(*planes[k : k + 2]) for k in range(0, len(planes), 2)]
        if turn:
            fields = [(real.T, imag.T) for real, imag in fields]
    return fields


def from_frequency(waves, fields):
    for turn in (True, False):
        planes = multiply(waves[1], [plane for field in fields for plane in fold(*field)])
        yield
        if turn:
            planes = [plane.T for plane in planes]
        fields = [tuple(planes[k : k + 2]) for k in range(0, len(planes), 2)]
    return fields


def product(left, right):
    return left[0] * right[0] - left[1] * right[1], left[0] * right[1] + left[1] * right[0]


def conjugate_product(left, right):
    return left[0] * right[0] + left[1] * right[1], left[0] * right[1] - left[1] * right[0]


def grads_kernel(field, amp, meta_hbm, probe, prop_ref, waves_hbm, packed, grad, waves, meta_ref, order, sems):
    core = lax.axis_index("pos") % 2
    base = 6 * core
    meta_load = pltpu.make_async_copy(meta_hbm, meta_ref, sems.at[0])
    meta_load.start()
    waves_load = pltpu.make_async_copy(waves_hbm, waves, sems.at[1])
    waves_load.start()

    def clear(block, _):
        grad[block] = jnp.zeros((4, 2 * SIDE, SIDE), jnp.float32)
        return 0

    lax.fori_loop(0, SPAN, clear, 0)
    meta_load.wait()
    waves_load.wait()

    def read(slot):
        code = meta_ref[slot // 32, slot % 32 // 2, 0, slot % 2] - 1
        return code >= 0, code // 2048, code % 2048

    def tally(slot, counts):
        valid, _, col = read(slot)
        here = valid.astype(jnp.int32)
        first = here * (col < LOW_COL).astype(jnp.int32)
        last = here * (col > HIGH_COL).astype(jnp.int32)
        return counts[0] + here, counts[1] + first, counts[2] + last

    whole, first_only, last_only = lax.fori_loop(0, 64, tally, (0, 0, 0), unroll=8)
    either = whole - first_only - last_only
    to_first = jnp.clip((whole + 1) // 2 - first_only, 0, either)

    def collect(slot, state):
        count, seen = state
        valid, _, col = read(slot)
        free = (col >= LOW_COL) & (col <= HIGH_COL)
        on_first = (col < LOW_COL) | (free & (seen < to_first))
        order[count] = slot
        mine = valid & (on_first == (core == 0))
        return count + mine.astype(jnp.int32), seen + (valid & free).astype(jnp.int32)

    count, _ = lax.fori_loop(0, 64, collect, (0, 0), unroll=8)
    lane = lax.broadcasted_iota(jnp.int32, (SIDE, SIDE), 1)

    def place(slot):
        valid, row, col = read(slot)
        row, col = jnp.where(valid, row, 0), jnp.where(valid, col, base * SIDE)
        block, shift = jnp.clip(col // SIDE - base, 0, SPAN - 1), col % SIDE
        return pl.ds(row, SIDE), block, jnp.minimum(block + 1, SPAN - 1), shift

    def cut(plane, where):
        rows, block, next_block, shift = where
        back = (SIDE - shift) % SIDE
        first = pltpu.roll(field[plane, block, rows, :], back, 1)
        second = pltpu.roll(field[plane, next_block, rows, :], back, 1)
        return jnp.where(lane < SIDE - shift, first, second)

    def add(plane, where, value):
        rows, block, next_block, shift = where
        moved = pltpu.roll(value.astype(jnp.bfloat16).astype(jnp.float32), shift, 1)
        zero = jnp.zeros_like(moved)
        grad[block, plane, rows, :] += jnp.where(lane >= shift, moved, zero)
        grad[next_block, plane, rows, :] += jnp.where(lane < shift, moved, zero)

    def stages(where, slot, weight):
        t0, t1 = [(cut(k, where), cut(k + 2, where)) for k in range(2)]
        probes = [(probe[m, 0], probe[m, 1]) for m in range(2)]
        prop = (prop_ref[0], prop_ref[1])
        fields = [product(p, t0) for p in probes]
        yield
        fields = yield from to_frequency(waves, fields)
        middle = yield from from_frequency(waves, [product(f, prop) for f in fields])
        far = yield from to_frequency(waves, [product(u, t1) for u in middle])
        model = 1.0 + sum(real * real + imag * imag for real, imag in far)
        factor = weight * (1.0 - decoded(amp[slot // 32, slot % 32 // 2, slot % 2]) * lax.rsqrt(model))
        fields = yield from from_frequency(waves, [(real * factor, imag * factor) for real, imag in far])

        def add_slice(k, parts):
            add(k, where, parts[0][0] + parts[1][0])
            add(k + 2, where, parts[0][1] + parts[1][1])

        add_slice(1, [conjugate_product(u, g) for u, g in zip(middle, fields)])
        fields = yield from to_frequency(waves, [conjugate_product(t1, g) for g in fields])
        fields = yield from from_frequency(waves, [conjugate_product(prop, h) for h in fields])
        add_slice(0, [conjugate_product(p, e) for p, e in zip(probes, fields)])

    def step(groups, start, index, _):
        running = []
        for group in range(groups):
            item = start + index * groups + group
            slot = order[jnp.minimum(item, count - 1)]
            weight = jnp.where(item < count, 2.0, 0.0).astype(jnp.float32)
            running.append(stages(place(slot), slot, weight))
        while running:
            running = [machine for machine in running if next(machine, 0) is None]
        return 0

    fours = (count + 1) // 4
    lax.fori_loop(0, fours, functools.partial(step, 4, 0), 0)
    rest = jnp.clip((count - 4 * fours + 1) // 2, 0, 1)
    lax.fori_loop(0, rest, functools.partial(step, 2, 4 * fours), 0)

    def pack(block, _):
        packed[block] = grad[block].astype(jnp.bfloat16)
        return 0

    lax.fori_loop(0, SPAN, pack, 0)


def grads_call(field, amp, meta, probe, prop, waves):
    hbm = pl.BlockSpec(memory_space=pltpu.HBM)
    vmem = pl.BlockSpec(memory_space=pltpu.VMEM)
    return pl.pallas_call(
        grads_kernel,
        out_shape=jax.ShapeDtypeStruct((SPAN, 4, 2 * SIDE, SIDE), jnp.bfloat16),
        in_specs=[vmem] * 5 + [hbm],
        out_specs=vmem,
        scratch_shapes=[
            pltpu.VMEM((SPAN, 4, 2 * SIDE, SIDE), jnp.float32),
            pltpu.VMEM(waves.shape, jnp.bfloat16),
            pltpu.SMEM(meta.shape, jnp.int32),
            pltpu.SMEM((65,), jnp.int32),
            pltpu.SemaphoreType.DMA((2,)),
        ],
        compiler_params=pltpu.CompilerParams(vmem_limit_bytes=K2_LIMIT * 2**20),
        name="window_gradients",
    )(field, amp, meta, probe, prop, pltpu.with_memory_space_constraint(waves, pltpu.HBM))


def send_kernel(obj_ref, measured_ref, phase_hbm, turn_hbm, offsets_ref, field, amp_ref, meta_ref, prop_ref,
                wide, extra, measured, own, phase, turn, halo_ref, codes_ref, chunk, amp_out, meta_out, local_sem, halo_send, halo_recv, amp_send, amp_recv, meta_send, meta_recv, twin_send, twin_recv):
    strip, pos = lax.axis_index("obj"), lax.axis_index("pos")
    x, core = pos // 2, pos % 2
    twin = (strip, x * 2 + 1 - core)

    def span(block):
        return pl.ds(pl.multiple_of(block * SIDE, SIDE), 2 * SIDE)

    loads = [
        pltpu.make_async_copy(obj_ref.at[:, :, span(8 * core + 2 * x)], wide, local_sem.at[0]),
        pltpu.make_async_copy(obj_ref.at[x, :, span(8 - 2 * core)], extra, local_sem.at[1]),
        pltpu.make_async_copy(measured_ref, measured, local_sem.at[2]),
        pltpu.make_async_copy(turn_hbm, turn, local_sem.at[3]),
        pltpu.make_async_copy(phase_hbm, phase, local_sem.at[4]),
        pltpu.make_async_copy(obj_ref.at[:, :, pl.ds(pl.multiple_of(6 * core * SIDE, SIDE), SPAN * SIDE)], own, local_sem.at[5]),
    ]
    for load in loads:
        load.start()
    barrier = pltpu.get_barrier_semaphore()

    def greet_strip(step, _):
        pl.semaphore_signal(barrier, inc=1, device_id=(lax.rem(strip + step, 16), pos), device_id_type=MESH)
        return 0

    lax.fori_loop(1, 16, greet_strip, 0)
    for step in range(1, 4):
        other = lax.rem(x + step, 4) * 2 + core
        pl.semaphore_signal(barrier, inc=1, device_id=(strip, other), device_id_type=MESH)
    pl.semaphore_signal(barrier, inc=1, device_id=twin, device_id_type=MESH)
    loads[0].wait()
    loads[1].wait()
    for block in range(2):
        lanes = slice(block * SIDE, (block + 1) * SIDE)
        for plane in range(4):
            chunk[plane * 2 + block] = wide[plane, :, lanes].astype(jnp.bfloat16)
        chunk[8 + block] = extra[:, lanes].astype(jnp.bfloat16)
    pl.semaphore_wait(barrier, 19)

    def piece(number):
        return pl.ds(number * (10 // PIECES), 10 // PIECES)

    def spread(source, index, number, where, send):
        return pltpu.make_async_remote_copy(
            src_ref=source.at[piece(number)], dst_ref=halo_ref.at[index, piece(number)], send_sem=halo_send.at[send, number],
            recv_sem=halo_recv.at[index, number], device_id=where, device_id_type=MESH,
        )

    above = (lax.rem(strip + 15, 16), pos)
    for number in range(PIECES):
        spread(chunk, x, number, above, 0).start()

    def amp_copy(target, source):
        return pltpu.make_async_remote_copy(
            src_ref=amp_out.at[target], dst_ref=amp_ref.at[core, source], send_sem=amp_send.at[target],
            recv_sem=amp_recv.at[source], device_id=(target, pos), device_id_type=MESH,
        )

    def meta_copy(target, source):
        return pltpu.make_async_remote_copy(
            src_ref=meta_out.at[target], dst_ref=meta_ref.at[core, source], send_sem=meta_send.at[target],
            recv_sem=meta_recv.at[source], device_id=(target, pos), device_id_type=MESH,
        )

    def to_twin(source, side):
        return pltpu.make_async_remote_copy(
            src_ref=amp_ref.at[core, source], dst_ref=amp_ref.at[side, source], send_sem=twin_send.at[source],
            recv_sem=twin_recv.at[source], device_id=twin, device_id_type=MESH,
        )

    def meta_to_twin(side):
        return pltpu.make_async_remote_copy(
            src_ref=meta_ref.at[core], dst_ref=meta_ref.at[side], send_sem=twin_send.at[16],
            recv_sem=twin_recv.at[16], device_id=twin, device_id_type=MESH,
        )

    lane = lax.broadcasted_iota(jnp.int32, META_TILE, 1)
    loads[2].wait()
    loads[3].wait()
    turn_back = turn[...].astype(jnp.float32).T.astype(jnp.bfloat16)

    def reorder(planes):
        rows = jnp.dot(jnp.concatenate(planes, axis=0).astype(jnp.bfloat16), turn_back, preferred_element_type=jnp.float32)
        rows = [rows[k * SIDE : (k + 1) * SIDE].T for k in range(len(planes))]
        rows = jnp.dot(jnp.concatenate(rows, axis=0).astype(jnp.bfloat16), turn_back, preferred_element_type=jnp.float32)
        return [rows[k * SIDE : (k + 1) * SIDE] for k in range(len(planes))]

    def encode(group, _):
        codes = [coded(measured[4 * group + k]) for k in range(4)]
        high = [jnp.floor(code * (1.0 / 256.0)) for code in codes]
        planes = reorder(high + [code - 256.0 * part for code, part in zip(codes, high)])
        for k in range(4):
            codes_ref[4 * group + k] = (256.0 * planes[k] + planes[4 + k]).astype(jnp.int32).astype(AMP)
        return 0

    lax.fori_loop(0, measured.shape[0] // 4, encode, 0)

    def packed(target):
        where, codes, seen = [jnp.int32(0)] * CAP, [jnp.int32(0)] * CAP, jnp.int32(0)
        for item in range(offsets_ref.shape[1]):
            row, col = offsets_ref[0, item], offsets_ref[1, item]
            here = row // SIDE == target
            for k in range(CAP):
                take = here & (seen == k)
                where[k] = jnp.where(take, item, where[k])
                codes[k] = jnp.where(take, 1 + row % SIDE * 2048 + col, codes[k])
            seen = seen + here.astype(jnp.int32)
        return jnp.where(lane == 0, codes[0], codes[1]), [codes_ref[index] for index in where]

    def pack(step, _):
        target = lax.rem(strip + step, 16)
        codes, values = packed(target)
        meta_out[target] = codes
        for k in range(CAP):
            amp_out[target, k] = values[k]
        amp_copy(target, strip).start()
        meta_copy(target, strip).start()
        return 0

    def forward(number):
        spread(chunk, x, number, above, 0).wait_recv()
        for step in (2, 1, 3):
            spread(halo_ref.at[x], x, number, (strip, lax.rem(x + step, 4) * 2 + core), step).start()

    bounds = [1, 6] + [6 + (10 * k) // PIECES for k in range(1, PIECES)] + [16]
    lax.fori_loop(bounds[0], bounds[1], pack, 0)
    for number in range(PIECES):
        forward(number)
        lax.fori_loop(bounds[number + 1], bounds[number + 2], pack, 0)
    codes, values = packed(strip)
    meta_ref[core, strip] = codes
    for k in range(CAP):
        amp_ref[core, strip, k] = values[k]
    to_twin(strip, core).start()

    loads[4].wait()
    value, planes = phase[...], []
    for _ in range(3):
        planes.append(value.astype(jnp.bfloat16))
        value = value - planes[-1].astype(jnp.float32)
    planes = reorder(planes)
    moved_phase = planes[0] + planes[1] + planes[2]
    prop_ref[0] = jnp.cos(moved_phase)
    prop_ref[1] = jnp.sin(moved_phase)
    loads[5].wait()

    def widen_own(block, _):
        span = pl.ds(pl.multiple_of(block * SIDE, SIDE), SIDE)
        for plane in range(4):
            field[plane, block, :SIDE, :] = own[plane, :, span].astype(jnp.bfloat16).astype(jnp.float32)
        return 0

    lax.fori_loop(0, SPAN, widen_own, 0)

    def relay(step, _):
        source = lax.rem(strip + 16 - step, 16)
        amp_copy(source, source).wait_recv()
        meta_copy(source, source).wait_recv()
        to_twin(source, core).start()
        return 0

    lax.fori_loop(1, 16, relay, 0)
    meta_to_twin(core).start()

    def finish(step, _):
        target = lax.rem(strip + step, 16)
        amp_copy(target, strip).wait_send()
        meta_copy(target, strip).wait_send()
        return 0

    lax.fori_loop(1, 16, finish, 0)

    def finish_twin(source, _):
        to_twin(source, core).wait_send()
        to_twin(source, 1 - core).wait_recv()
        return 0

    lax.fori_loop(0, 16, finish_twin, 0)
    meta_to_twin(core).wait_send()
    meta_to_twin(1 - core).wait_recv()
    for number in range(PIECES):
        for step in range(1, 4):
            spread(chunk, lax.rem(x + step, 4), number, (strip, pos), 0).wait_recv()

    def widen_halo(step, _):
        part = step // 2
        block = 2 * core + step
        for plane in range(4):
            field[plane, block, SIDE:, :] = halo_ref[part, 2 * plane + step % 2].astype(jnp.float32)
        return 0

    lax.fori_loop(0, 8, widen_halo, 0)
    for plane in range(4):
        for block in range(2):
            field[plane, 8 - 8 * core + block, SIDE:, :] = halo_ref[plane, 8 + block].astype(jnp.float32)
    for number in range(PIECES):
        for step in range(4):
            spread(chunk, x, number, (strip, pos), step).wait_send()


def send_call(obj, measured, phase, order, offsets):
    hbm = pl.BlockSpec(memory_space=pltpu.HBM)
    vmem = pl.BlockSpec(memory_space=pltpu.VMEM)
    dma = pltpu.SemaphoreType.DMA
    return pl.pallas_call(
        send_kernel,
        out_shape=(
            jax.ShapeDtypeStruct((4, SPAN, 2 * SIDE, SIDE), jnp.float32),
            jax.ShapeDtypeStruct((2, 16, CAP, SIDE, SIDE), AMP),
            jax.ShapeDtypeStruct((2, 16, *META_TILE), jnp.int32),
            jax.ShapeDtypeStruct((2, SIDE, SIDE), jnp.float32),
        ),
        in_specs=[hbm] * 4 + [pl.BlockSpec(memory_space=pltpu.SMEM)],
        out_specs=(vmem,) * 4,
        scratch_shapes=[
            pltpu.VMEM((4, SIDE, 2 * SIDE), jnp.float32),
            pltpu.VMEM((SIDE, 2 * SIDE), jnp.float32),
            pltpu.VMEM(measured.shape, jnp.float32),
            pltpu.VMEM((4, SIDE, SPAN * SIDE), jnp.float32),
            pltpu.VMEM((SIDE, SIDE), jnp.float32),
            pltpu.VMEM((SIDE, SIDE), jnp.bfloat16),
            pltpu.VMEM((4, 10, SIDE, SIDE), jnp.bfloat16),
            pltpu.VMEM(measured.shape, AMP),
            pltpu.VMEM((10, SIDE, SIDE), jnp.bfloat16),
            pltpu.VMEM((16, CAP, SIDE, SIDE), AMP),
            pltpu.VMEM((16, *META_TILE), jnp.int32),
            dma((6,)),
            dma((4, PIECES)),
            dma((4, PIECES)),
            dma((16,)),
            dma((16,)),
            dma((16,)),
            dma((16,)),
            dma((17,)),
            dma((17,)),
        ],
        compiler_params=pltpu.CompilerParams(collective_id=0, has_side_effects=True, vmem_limit_bytes=20 * 2**20),
        name="exchange_inputs",
    )(*[pltpu.with_memory_space_constraint(x, pltpu.HBM) for x in (obj, measured, phase, order)], offsets)


def sum_kernel(grad_ref, out_ref, theirs, joined, parts, low_in, low_out, twin_send, twin_recv, x_send, x_recv, low_send, low_recv):
    strip, pos = lax.axis_index("obj"), lax.axis_index("pos")
    x, core = pos // 2, pos % 2
    twin = (strip, x * 2 + 1 - core)
    below, above = (lax.rem(strip + 1, 16), pos), (lax.rem(strip + 15, 16), pos)
    shared = 3 - 3 * core
    mine = 2 * shared + 2 * core
    barrier = pltpu.get_barrier_semaphore()
    for step in range(1, 8):
        pl.semaphore_signal(barrier, inc=1, device_id=(strip, lax.rem(pos + step, 8)), device_id_type=MESH)
    for device in (below, above):
        pl.semaphore_signal(barrier, inc=1, device_id=device, device_id_type=MESH)
    pl.semaphore_wait(barrier, 9)
    to_twin = pltpu.make_async_remote_copy(
        src_ref=grad_ref.at[pl.ds(8 - 8 * core, 2)], dst_ref=theirs, send_sem=twin_send, recv_sem=twin_recv,
        device_id=twin, device_id_type=MESH,
    )
    to_twin.start()
    halves = (pl.ds(SIDE, SIDE), pl.ds(0, SIDE))

    def remote(pair, source, half, target, start):
        return pltpu.make_async_remote_copy(
            src_ref=source.at[:, :, halves[half]], dst_ref=parts.at[start, half], send_sem=x_send.at[pair, half],
            recv_sem=x_recv.at[start, half], device_id=(strip, target), device_id_type=MESH,
        )

    def local(source, half):
        return pltpu.make_async_copy(source.at[:, :, halves[half]], parts.at[x, half], x_recv.at[x, half])

    def give(pair, source, half):
        target = 4 * core + pair

        @pl.when(target != pos)
        def _():
            remote(pair, source, half, target, x).start()

        @pl.when(target == pos)
        def _():
            local(source, half).start()

    def block_pair(pair):
        return grad_ref.at[pl.ds(2 * pair + 2 * core, 2)]

    pairs = [lax.rem(shared + step, 4) for step in range(1, 4)]
    for half in range(2):
        for pair in pairs:
            give(pair, block_pair(pair), half)
    to_twin.wait_recv()
    for half in range(2):
        for block in range(2):
            for plane in range(4):
                rows = slice(SIDE, None) if half == 0 else slice(0, SIDE)
                joined[block, plane, rows] = (
                    grad_ref[mine + block, plane, rows].astype(jnp.float32) + theirs[block, plane, rows].astype(jnp.float32)
                ).astype(jnp.bfloat16)
        give(shared, joined, half)

    def arrived(half):
        for start in range(4):
            remote(0, joined, half, pos, start).wait_recv()

    def total(half, block, plane):
        value = parts[0, half, block, plane].astype(jnp.float32)
        for start in range(1, 4):
            value += parts[start, half, block, plane].astype(jnp.float32)
        return value

    arrived(0)
    for block in range(2):
        for plane in range(4):
            low_out[block, plane] = total(0, block, plane).astype(jnp.bfloat16)
    shift = pltpu.make_async_remote_copy(
        src_ref=low_out, dst_ref=low_in, send_sem=low_send, recv_sem=low_recv, device_id=below, device_id_type=MESH,
    )
    shift.start()
    arrived(1)
    shift.wait_recv()
    for block in range(2):
        for plane in range(4):
            out_ref[plane, :, block * SIDE : (block + 1) * SIDE] = total(1, block, plane) + low_in[block, plane].astype(jnp.float32)
    shift.wait_send()
    to_twin.wait_send()
    for half in range(2):
        for pair in range(4):
            target = 4 * core + pair

            @pl.when(target != pos)
            def _():
                remote(pair, joined, half, target, x).wait_send()


def sum_call(grad):
    dma = pltpu.SemaphoreType.DMA
    two = (2, 4, 2 * SIDE, SIDE)
    return pl.pallas_call(
        sum_kernel,
        out_shape=jax.ShapeDtypeStruct((4, SIDE, 2 * SIDE), jnp.float32),
        in_specs=[pl.BlockSpec(memory_space=pltpu.VMEM)],
        out_specs=pl.BlockSpec(memory_space=pltpu.VMEM),
        scratch_shapes=[
            pltpu.VMEM(two, jnp.bfloat16),
            pltpu.VMEM(two, jnp.bfloat16),
            pltpu.VMEM((4, 2, 2, 4, SIDE, SIDE), jnp.bfloat16),
            pltpu.VMEM((2, 4, SIDE, SIDE), jnp.bfloat16),
            pltpu.VMEM((2, 4, SIDE, SIDE), jnp.bfloat16),
            dma,
            dma,
            dma((4, 2)),
            dma((4, 2)),
            dma,
            dma,
        ],
        compiler_params=pltpu.CompilerParams(collective_id=1, has_side_effects=True, vmem_limit_bytes=20 * 2**20),
        name="sum_gradients",
    )(grad)


def per_device(object_field, probe_modes, propagator_phase, offsets, measured):
    obj = object_field.reshape(4, SIDE, object_field.shape[3])
    waves, order = [jnp.asarray(x) for x in dft_operands()]
    field, amp, meta, prop = send_call(obj, measured, propagator_phase, order, offsets.T)
    grad = grads_call(field, amp, meta, probe_modes, prop, waves)
    return sum_call(grad).reshape(2, 2, SIDE, 2 * SIDE)


def solution(mesh):
    placed = (
        P(None, None, "obj", None),
        P(),
        P(),
        P(("obj", "pos"), None),
        P(("obj", "pos"), None, None),
    )
    return jax.shard_map(
        per_device,
        mesh=mesh,
        in_specs=placed,
        out_specs=P(None, None, "obj", "pos"),
        check_vma=False,
    )
```

```python
import functools
import math

import jax
import jax.numpy as jnp
import numpy as np
from jax import lax
from jax.experimental import pallas as pl
from jax.experimental.pallas import tpu as pltpu
from jax.sharding import PartitionSpec as P

CAP = 2
SIDE = 128
META_TILE = (1, 128)
PIECES = 4
CHAINS, LAST_CHAINS = 5, 3
K2_LIMIT = 30
SPAN = 10
LOW_COL, HIGH_COL = 768, 1152
AMP = jnp.int16
AMP_MIDDLE, AMP_STEPS = 2.625, 16384.0
MESH = pl.DeviceIdType.MESH


def dft_operands():
    index = np.arange(SIDE)
    angles = (index[:, None] * index[None, :] % SIDE) * (2.0 * math.pi / SIDE)
    wave = np.cos(angles) / math.sqrt(SIDE)
    wave[SIDE // 2 + 1 :] = np.sin(angles[1 : SIDE // 2]) / math.sqrt(SIDE)

    def product(block):
        block = block.astype(np.float32)
        high = block.astype(jnp.bfloat16)
        low = (block - high.astype(np.float32)).astype(jnp.bfloat16)
        return np.block([[high, high], [low, np.zeros_like(low)]])

    order = np.zeros((SIDE, SIDE), jnp.bfloat16)
    order[index, np.where(index <= SIDE // 2, index, SIDE + SIDE // 2 - index)] = 1
    return np.stack([product(wave), product(wave.T)]), order


def coded(measured):
    return jnp.round((jnp.sqrt(measured) - AMP_MIDDLE) * AMP_STEPS)


def decoded(code):
    return code.astype(jnp.int32).astype(jnp.float32) * (1.0 / AMP_STEPS) + AMP_MIDDLE


def multiply(left, planes):
    x = jnp.concatenate(planes, axis=1)
    high = x.astype(jnp.bfloat16)
    low = (x - high.astype(jnp.float32)).astype(jnp.bfloat16)
    y = jnp.dot(left, jnp.concatenate([high, low], axis=0), preferred_element_type=jnp.float32)
    y = y[:SIDE] + y[SIDE:]
    return [y[:, k * SIDE : (k + 1) * SIDE] for k in range(len(planes))]


def halves(plane):
    return plane[: SIDE // 2], plane[SIDE // 2 :]


def with_first_row(first, rest):
    row = lax.broadcasted_iota(jnp.int32, (8, SIDE), 0)
    return jnp.concatenate([jnp.where(row == 0, first[:8], rest[:8]), rest[8:]], axis=0)


def unfold(real, imag):
    (tr, br), (ti, bi) = halves(real), halves(imag)
    return (
        jnp.concatenate([with_first_row(tr, tr + bi), with_first_row(br, tr - bi)], axis=0),
        jnp.concatenate([with_first_row(ti, ti - br), with_first_row(bi, ti + br)], axis=0),
    )


def fold(real, imag):
    (tr, br), (ti, bi) = halves(real), halves(imag)
    return (
        jnp.concatenate([with_first_row(tr, tr + br), with_first_row(br, bi - ti)], axis=0),
        jnp.concatenate([with_first_row(ti, ti + bi), with_first_row(bi, tr - br)], axis=0),
    )


def to_frequency(waves, fields):
    for turn in (True, False):
        planes = multiply(waves[0], [plane for field in fields for plane in field])
        yield
        fields = [unfold(*planes[k : k + 2]) for k in range(0, len(planes), 2)]
        if turn:
            fields = [(real.T, imag.T) for real, imag in fields]
    return fields


def from_frequency(waves, fields):
    for turn in (True, False):
        planes = multiply(waves[1], [plane for field in fields for plane in fold(*field)])
        yield
        if turn:
            planes = [plane.T for plane in planes]
        fields = [tuple(planes[k : k + 2]) for k in range(0, len(planes), 2)]
    return fields


def product(left, right):
    return left[0] * right[0] - left[1] * right[1], left[0] * right[1] + left[1] * right[0]


def conjugate_product(left, right):
    return left[0] * right[0] + left[1] * right[1], left[0] * right[1] - left[1] * right[0]


def grads_kernel(field, amp, meta_hbm, probe, prop_ref, waves_hbm, packed, grad, waves, meta_ref, order, sems):
    core = lax.axis_index("pos") % 2
    base = 6 * core
    meta_load = pltpu.make_async_copy(meta_hbm, meta_ref, sems.at[0])
    meta_load.start()
    waves_load = pltpu.make_async_copy(waves_hbm, waves, sems.at[1])
    waves_load.start()

    meta_load.wait()

    def read(slot):
        code = meta_ref[slot // 32, slot % 32 // 2, 0, slot % 2] - 1
        return code >= 0, code // 2048, code % 2048

    def tally(slot, counts):
        valid, _, col = read(slot)
        here = valid.astype(jnp.int32)
        first = here * (col < LOW_COL).astype(jnp.int32)
        last = here * (col > HIGH_COL).astype(jnp.int32)
        return counts[0] + here, counts[1] + first, counts[2] + last

    def tally_and_clear(index, counts):
        for k in range(8):
            counts = tally(8 * index + k, counts)
        for k in range(SPAN // 2):
            tile = SPAN // 2 * index + k
            grad[tile // 4, tile % 4] = jnp.zeros((2 * SIDE, SIDE), jnp.float32)
        return counts

    whole, first_only, last_only = lax.fori_loop(0, 8, tally_and_clear, (0, 0, 0))
    either = whole - first_only - last_only
    to_first = jnp.clip((whole + 1) // 2 - first_only, 0, either)

    def collect(slot, state):
        count, seen = state
        valid, _, col = read(slot)
        free = (col >= LOW_COL) & (col <= HIGH_COL)
        on_first = (col < LOW_COL) | (free & (seen < to_first))
        order[count] = slot
        mine = valid & (on_first == (core == 0))
        return count + mine.astype(jnp.int32), seen + (valid & free).astype(jnp.int32)

    count, _ = lax.fori_loop(0, 64, collect, (0, 0), unroll=8)
    waves_load.wait()
    lane = lax.broadcasted_iota(jnp.int32, (SIDE, SIDE), 1)

    def place(slot):
        valid, row, col = read(slot)
        row, col = jnp.where(valid, row, 0), jnp.where(valid, col, base * SIDE)
        block, shift = jnp.clip(col // SIDE - base, 0, SPAN - 1), col % SIDE
        return pl.ds(row, SIDE), block, jnp.minimum(block + 1, SPAN - 1), shift

    def cut(plane, where):
        rows, block, next_block, shift = where
        back = (SIDE - shift) % SIDE
        first = pltpu.roll(field[plane, block, rows, :], back, 1)
        second = pltpu.roll(field[plane, next_block, rows, :], back, 1)
        return jnp.where(lane < SIDE - shift, first, second)

    def add(plane, where, value):
        rows, block, next_block, shift = where
        moved = pltpu.roll(value.astype(jnp.bfloat16).astype(jnp.float32), shift, 1)
        zero = jnp.zeros_like(moved)
        grad[block, plane, rows, :] += jnp.where(lane >= shift, moved, zero)
        grad[next_block, plane, rows, :] += jnp.where(lane < shift, moved, zero)

    def stages(where, slot, weight):
        t0, t1 = [(cut(k, where), cut(k + 2, where)) for k in range(2)]
        probes = [(probe[m, 0], probe[m, 1]) for m in range(2)]
        prop = (prop_ref[0], prop_ref[1])
        fields = [product(p, t0) for p in probes]
        yield
        fields = yield from to_frequency(waves, fields)
        middle = yield from from_frequency(waves, [product(f, prop) for f in fields])
        far = yield from to_frequency(waves, [product(u, t1) for u in middle])
        model = 1.0 + sum(real * real + imag * imag for real, imag in far)
        factor = weight * (1.0 - decoded(amp[slot // 32, slot % 32 // 2, slot % 2]) * lax.rsqrt(model))
        fields = yield from from_frequency(waves, [(real * factor, imag * factor) for real, imag in far])

        def add_slice(k, parts):
            add(k, where, parts[0][0] + parts[1][0])
            add(k + 2, where, parts[0][1] + parts[1][1])

        add_slice(1, [conjugate_product(u, g) for u, g in zip(middle, fields)])
        fields = yield from to_frequency(waves, [conjugate_product(t1, g) for g in fields])
        fields = yield from from_frequency(waves, [conjugate_product(prop, h) for h in fields])
        add_slice(0, [conjugate_product(p, e) for p, e in zip(probes, fields)])

    def step(groups, start, index, _):
        running = []
        for group in range(groups):
            item = start + index * groups + group
            slot = order[jnp.minimum(item, count - 1)]
            weight = jnp.where(item < count, 2.0, 0.0).astype(jnp.float32)
            running.append(stages(place(slot), slot, weight))
        while running:
            running = [machine for machine in running if next(machine, 0) is None]
        return 0

    full = (count + CHAINS - 1 - LAST_CHAINS) // CHAINS
    lax.fori_loop(0, full, functools.partial(step, CHAINS, 0), 0)
    rest = jnp.clip(count - CHAINS * full, 0, 1)
    lax.fori_loop(0, rest, functools.partial(step, LAST_CHAINS, CHAINS * full), 0)

    def pack(block, _):
        packed[block] = grad[block].astype(jnp.bfloat16)
        return 0

    lax.fori_loop(0, SPAN, pack, 0)


def grads_call(field, amp, meta, probe, prop, waves):
    hbm = pl.BlockSpec(memory_space=pltpu.HBM)
    vmem = pl.BlockSpec(memory_space=pltpu.VMEM)
    return pl.pallas_call(
        grads_kernel,
        out_shape=jax.ShapeDtypeStruct((SPAN, 4, 2 * SIDE, SIDE), jnp.bfloat16),
        in_specs=[vmem] * 5 + [hbm],
        out_specs=vmem,
        scratch_shapes=[
            pltpu.VMEM((SPAN, 4, 2 * SIDE, SIDE), jnp.float32),
            pltpu.VMEM(waves.shape, jnp.bfloat16),
            pltpu.SMEM(meta.shape, jnp.int32),
            pltpu.SMEM((65,), jnp.int32),
            pltpu.SemaphoreType.DMA((2,)),
        ],
        compiler_params=pltpu.CompilerParams(vmem_limit_bytes=K2_LIMIT * 2**20),
        name="window_gradients",
    )(field, amp, meta, probe, prop, pltpu.with_memory_space_constraint(waves, pltpu.HBM))


def send_kernel(obj_ref, measured_ref, phase_hbm, turn_hbm, offsets_ref, field, amp_ref, meta_ref, prop_ref,
                wide, measured, own, phase, turn, halo_ref, codes_ref, chunk, amp_out, meta_out, local_sem, halo_send, halo_recv, shared_sem, slot_sem, twin_sem):
    strip, pos = lax.axis_index("obj"), lax.axis_index("pos")
    x, core = pos // 2, pos % 2
    twin = (strip, x * 2 + 1 - core)

    def span(block):
        return pl.ds(pl.multiple_of(block * SIDE, SIDE), 2 * SIDE)

    loads = [
        pltpu.make_async_copy(obj_ref.at[:, :, span(8 * core + 2 * x)], wide, local_sem.at[0]),
        pltpu.make_async_copy(measured_ref, measured, local_sem.at[1]),
        pltpu.make_async_copy(turn_hbm, turn, local_sem.at[2]),
        pltpu.make_async_copy(phase_hbm, phase, local_sem.at[3]),
        pltpu.make_async_copy(obj_ref.at[:, :, pl.ds(pl.multiple_of(6 * core * SIDE, SIDE), SPAN * SIDE)], own, local_sem.at[4]),
    ]
    for load in loads:
        load.start()
    barrier = pltpu.get_barrier_semaphore()

    def greet_strip(step, _):
        pl.semaphore_signal(barrier, inc=1, device_id=(lax.rem(strip + step, 16), pos), device_id_type=MESH)
        return 0

    lax.fori_loop(1, 16, greet_strip, 0)
    for step in range(1, 4):
        other = lax.rem(x + step, 4) * 2 + core
        pl.semaphore_signal(barrier, inc=1, device_id=(strip, other), device_id_type=MESH)
    pl.semaphore_signal(barrier, inc=1, device_id=twin, device_id_type=MESH)
    loads[0].wait()
    for block in range(2):
        lanes = slice(block * SIDE, (block + 1) * SIDE)
        for plane in range(4):
            chunk[plane * 2 + block] = wide[plane, :, lanes].astype(jnp.bfloat16)
    pl.semaphore_wait(barrier, 19)

    def piece(number):
        return pl.ds(number * (8 // PIECES), 8 // PIECES)

    def spread(source, index, number, where, send):
        return pltpu.make_async_remote_copy(
            src_ref=source.at[piece(number)], dst_ref=halo_ref.at[index, piece(number)], send_sem=halo_send.at[send, number],
            recv_sem=halo_recv.at[index, number], device_id=where, device_id_type=MESH,
        )

    above = (lax.rem(strip + 15, 16), pos)
    for number in range(PIECES):
        spread(chunk, x, number, above, 0).start()

    def amp_copy(target):
        return pltpu.make_async_remote_copy(
            src_ref=amp_out.at[target], dst_ref=amp_ref.at[core, strip], send_sem=slot_sem.at[0],
            recv_sem=slot_sem.at[1], device_id=(target, pos), device_id_type=MESH,
        )

    def meta_copy(target):
        return pltpu.make_async_remote_copy(
            src_ref=meta_out.at[target], dst_ref=meta_ref.at[core, strip], send_sem=slot_sem.at[2],
            recv_sem=slot_sem.at[3], device_id=(target, pos), device_id_type=MESH,
        )

    def all_copies():
        others = pl.ds(0, 15)
        return [
            pltpu.make_async_remote_copy(
                src_ref=source.at[others], dst_ref=target.at[core, others], send_sem=slot_sem.at[2 * k],
                recv_sem=slot_sem.at[2 * k + 1], device_id=twin, device_id_type=MESH,
            )
            for k, (source, target) in enumerate(((amp_out, amp_ref), (meta_out, meta_ref)))
        ]

    def to_twin(side):
        return [
            pltpu.make_async_remote_copy(
                src_ref=ref.at[core], dst_ref=ref.at[side], send_sem=twin_sem.at[2 * k], recv_sem=twin_sem.at[2 * k + 1],
                device_id=twin, device_id_type=MESH,
            )
            for k, ref in enumerate((amp_ref, meta_ref))
        ]

    lane = lax.broadcasted_iota(jnp.int32, META_TILE, 1)
    loads[1].wait()
    loads[2].wait()
    turn_back = turn[...].astype(jnp.float32).T.astype(jnp.bfloat16)

    def reorder(planes):
        rows = jnp.dot(jnp.concatenate(planes, axis=0).astype(jnp.bfloat16), turn_back, preferred_element_type=jnp.float32)
        rows = [rows[k * SIDE : (k + 1) * SIDE].T for k in range(len(planes))]
        rows = jnp.dot(jnp.concatenate(rows, axis=0).astype(jnp.bfloat16), turn_back, preferred_element_type=jnp.float32)
        return [rows[k * SIDE : (k + 1) * SIDE] for k in range(len(planes))]

    def encode(group, _):
        codes = [coded(measured[4 * group + k]) for k in range(4)]
        high = [jnp.floor(code * (1.0 / 256.0)) for code in codes]
        planes = reorder(high + [code - 256.0 * part for code, part in zip(codes, high)])
        for k in range(4):
            codes_ref[4 * group + k] = (256.0 * planes[k] + planes[4 + k]).astype(jnp.int32).astype(AMP)
        return 0

    lax.fori_loop(0, measured.shape[0] // 4, encode, 0)

    def packed(target):
        where, codes, seen = [jnp.int32(0)] * CAP, [jnp.int32(0)] * CAP, jnp.int32(0)
        for item in range(offsets_ref.shape[1]):
            row, col = offsets_ref[0, item], offsets_ref[1, item]
            here = row // SIDE == target
            for k in range(CAP):
                take = here & (seen == k)
                where[k] = jnp.where(take, item, where[k])
                codes[k] = jnp.where(take, 1 + row % SIDE * 2048 + col, codes[k])
            seen = seen + here.astype(jnp.int32)
        return jnp.where(lane == 0, codes[0], codes[1]), [codes_ref[index] for index in where]

    def pack(step, _):
        target = (strip // 4 + step % 4) % 4 * 4 + (strip + step // 4) % 4
        codes, values = packed(target)
        meta_out[target] = codes
        for k in range(CAP):
            amp_out[target, k] = values[k]
        amp_copy(target).start()
        meta_copy(target).start()
        return 0

    def forward(number):
        spread(chunk, x, number, above, 0).wait_recv()
        for step in (2, 1, 3):
            spread(halo_ref.at[x], x, number, (strip, lax.rem(x + step, 4) * 2 + core), step).start()

    bounds = [1, 6] + [6 + (10 * k) // PIECES for k in range(1, PIECES)] + [16]
    lax.fori_loop(1, 16, pack, 0)
    for number in range(PIECES):
        forward(number)
    codes, values = packed(strip)
    meta_ref[core, strip] = codes
    for k in range(CAP):
        amp_ref[core, strip, k] = values[k]

    loads[3].wait()
    value, planes = phase[...], []
    for _ in range(3):
        planes.append(value.astype(jnp.bfloat16))
        value = value - planes[-1].astype(jnp.float32)
    planes = reorder(planes)
    moved_phase = planes[0] + planes[1] + planes[2]
    prop_ref[0] = jnp.cos(moved_phase)
    prop_ref[1] = jnp.sin(moved_phase)
    loads[4].wait()

    def widen_own(block, _):
        span = pl.ds(pl.multiple_of(block * SIDE, SIDE), SIDE)
        for plane in range(4):
            field[plane, block, :SIDE, :] = own[plane, :, span].astype(jnp.bfloat16).astype(jnp.float32)
        return 0

    lax.fori_loop(0, SPAN, widen_own, 0)

    arrivals = all_copies()
    for copy in arrivals:
        copy.wait_recv()
    relays = to_twin(core)
    for copy in relays:
        copy.start()
    for number in range(PIECES):
        for step in range(1, 4):
            spread(chunk, lax.rem(x + step, 4), number, (strip, pos), 0).wait_recv()

    shared = pltpu.make_async_remote_copy(
        src_ref=halo_ref.at[3 - 3 * core], dst_ref=halo_ref.at[4], send_sem=shared_sem.at[0], recv_sem=shared_sem.at[1],
        device_id=twin, device_id_type=MESH,
    )
    shared.start()

    def widen_halo(step, _):
        part = step // 2
        block = 2 * core + step
        for plane in range(4):
            field[plane, block, SIDE:, :] = halo_ref[part, 2 * plane + step % 2].astype(jnp.float32)
        return 0

    lax.fori_loop(0, 8, widen_halo, 0)
    shared.wait()
    for plane in range(4):
        for block in range(2):
            field[plane, 8 - 8 * core + block, SIDE:, :] = halo_ref[4, 2 * plane + block].astype(jnp.float32)
    for copy in arrivals + relays:
        copy.wait_send()
    for copy in to_twin(1 - core):
        copy.wait_recv()
    for number in range(PIECES):
        for step in range(4):
            spread(chunk, x, number, (strip, pos), step).wait_send()


def send_call(obj, measured, phase, order, offsets):
    hbm = pl.BlockSpec(memory_space=pltpu.HBM)
    vmem = pl.BlockSpec(memory_space=pltpu.VMEM)
    dma = pltpu.SemaphoreType.DMA
    return pl.pallas_call(
        send_kernel,
        out_shape=(
            jax.ShapeDtypeStruct((4, SPAN, 2 * SIDE, SIDE), jnp.float32),
            jax.ShapeDtypeStruct((2, 16, CAP, SIDE, SIDE), AMP),
            jax.ShapeDtypeStruct((2, 16, *META_TILE), jnp.int32),
            jax.ShapeDtypeStruct((2, SIDE, SIDE), jnp.float32),
        ),
        in_specs=[hbm] * 4 + [pl.BlockSpec(memory_space=pltpu.SMEM)],
        out_specs=(vmem,) * 4,
        scratch_shapes=[
            pltpu.VMEM((4, SIDE, 2 * SIDE), jnp.float32),
            pltpu.VMEM(measured.shape, jnp.float32),
            pltpu.VMEM((4, SIDE, SPAN * SIDE), jnp.float32),
            pltpu.VMEM((SIDE, SIDE), jnp.float32),
            pltpu.VMEM((SIDE, SIDE), jnp.bfloat16),
            pltpu.VMEM((5, 8, SIDE, SIDE), jnp.bfloat16),
            pltpu.VMEM(measured.shape, AMP),
            pltpu.VMEM((8, SIDE, SIDE), jnp.bfloat16),
            pltpu.VMEM((16, CAP, SIDE, SIDE), AMP),
            pltpu.VMEM((16, *META_TILE), jnp.int32),
            dma((5,)),
            dma((4, PIECES)),
            dma((4, PIECES)),
            dma((2,)),
            dma((4,)),
            dma((4,)),
        ],
        compiler_params=pltpu.CompilerParams(collective_id=0, has_side_effects=True, vmem_limit_bytes=20 * 2**20),
        name="exchange_inputs",
    )(*[pltpu.with_memory_space_constraint(x, pltpu.HBM) for x in (obj, measured, phase, order)], offsets)


def sum_kernel(grad_ref, out_ref, theirs, joined, parts, low_in, low_out, twin_send, twin_recv, x_send, x_recv, low_send, low_recv):
    strip, pos = lax.axis_index("obj"), lax.axis_index("pos")
    x, core = pos // 2, pos % 2
    twin = (strip, x * 2 + 1 - core)
    below, above = (lax.rem(strip + 1, 16), pos), (lax.rem(strip + 15, 16), pos)
    shared = 3 - 3 * core
    mine = 2 * shared + 2 * core
    barrier = pltpu.get_barrier_semaphore()
    for step in range(1, 8):
        pl.semaphore_signal(barrier, inc=1, device_id=(strip, lax.rem(pos + step, 8)), device_id_type=MESH)
    for device in (below, above):
        pl.semaphore_signal(barrier, inc=1, device_id=device, device_id_type=MESH)
    pl.semaphore_wait(barrier, 9)
    to_twin = pltpu.make_async_remote_copy(
        src_ref=grad_ref.at[pl.ds(8 - 8 * core, 2)], dst_ref=theirs, send_sem=twin_send, recv_sem=twin_recv,
        device_id=twin, device_id_type=MESH,
    )
    to_twin.start()
    halves = (pl.ds(SIDE, SIDE), pl.ds(0, SIDE))

    def remote(pair, source, half, target, start):
        return pltpu.make_async_remote_copy(
            src_ref=source.at[:, :, halves[half]], dst_ref=parts.at[start, half], send_sem=x_send.at[pair, half],
            recv_sem=x_recv.at[start, half], device_id=(strip, target), device_id_type=MESH,
        )

    def local(source, half):
        return pltpu.make_async_copy(source.at[:, :, halves[half]], parts.at[x, half], x_recv.at[x, half])

    def give(pair, source, half):
        target = 4 * core + pair

        @pl.when(target != pos)
        def _():
            remote(pair, source, half, target, x).start()

        @pl.when(target == pos)
        def _():
            local(source, half).start()

    def block_pair(pair):
        return grad_ref.at[pl.ds(2 * pair + 2 * core, 2)]

    pairs = [lax.rem(shared + step, 4) for step in range(1, 4)]
    for half in range(2):
        for pair in pairs:
            give(pair, block_pair(pair), half)
    to_twin.wait_recv()
    for half in range(2):
        for block in range(2):
            for plane in range(4):
                rows = slice(SIDE, None) if half == 0 else slice(0, SIDE)
                joined[block, plane, rows] = (
                    grad_ref[mine + block, plane, rows].astype(jnp.float32) + theirs[block, plane, rows].astype(jnp.float32)
                ).astype(jnp.bfloat16)
        give(shared, joined, half)

    def arrived(half):
        for start in range(4):
            remote(0, joined, half, pos, start).wait_recv()

    def total(half, block, plane):
        value = parts[0, half, block, plane].astype(jnp.float32)
        for start in range(1, 4):
            value += parts[start, half, block, plane].astype(jnp.float32)
        return value

    arrived(0)
    for block in range(2):
        for plane in range(4):
            low_out[block, plane] = total(0, block, plane).astype(jnp.bfloat16)
    shift = pltpu.make_async_remote_copy(
        src_ref=low_out, dst_ref=low_in, send_sem=low_send, recv_sem=low_recv, device_id=below, device_id_type=MESH,
    )
    shift.start()
    arrived(1)
    shift.wait_recv()
    for block in range(2):
        for plane in range(4):
            out_ref[plane, :, block * SIDE : (block + 1) * SIDE] = total(1, block, plane) + low_in[block, plane].astype(jnp.float32)
    shift.wait_send()
    to_twin.wait_send()
    for half in range(2):
        for pair in range(4):
            target = 4 * core + pair

            @pl.when(target != pos)
            def _():
                remote(pair, joined, half, target, x).wait_send()


def sum_call(grad):
    dma = pltpu.SemaphoreType.DMA
    two = (2, 4, 2 * SIDE, SIDE)
    return pl.pallas_call(
        sum_kernel,
        out_shape=jax.ShapeDtypeStruct((4, SIDE, 2 * SIDE), jnp.float32),
        in_specs=[pl.BlockSpec(memory_space=pltpu.VMEM)],
        out_specs=pl.BlockSpec(memory_space=pltpu.VMEM),
        scratch_shapes=[
            pltpu.VMEM(two, jnp.bfloat16),
            pltpu.VMEM(two, jnp.bfloat16),
            pltpu.VMEM((4, 2, 2, 4, SIDE, SIDE), jnp.bfloat16),
            pltpu.VMEM((2, 4, SIDE, SIDE), jnp.bfloat16),
            pltpu.VMEM((2, 4, SIDE, SIDE), jnp.bfloat16),
            dma,
            dma,
            dma((4, 2)),
            dma((4, 2)),
            dma,
            dma,
        ],
        compiler_params=pltpu.CompilerParams(collective_id=1, has_side_effects=True, vmem_limit_bytes=20 * 2**20),
        name="sum_gradients",
    )(grad)


def per_device(object_field, probe_modes, propagator_phase, offsets, measured):
    obj = object_field.reshape(4, SIDE, object_field.shape[3])
    waves, order = [jnp.asarray(x) for x in dft_operands()]
    field, amp, meta, prop = send_call(obj, measured, propagator_phase, order, offsets.T)
    grad = grads_call(field, amp, meta, probe_modes, prop, waves)
    return sum_call(grad).reshape(2, 2, SIDE, 2 * SIDE)


def solution(mesh):
    placed = (
        P(None, None, "obj", None),
        P(),
        P(),
        P(("obj", "pos"), None),
        P(("obj", "pos"), None, None),
    )
    return jax.shard_map(
        per_device,
        mesh=mesh,
        in_specs=placed,
        out_specs=P(None, None, "obj", "pos"),
        check_vma=False,
    )
```

```python
import functools
import math

import jax
import jax.numpy as jnp
import numpy as np
from jax import lax
from jax.experimental import pallas as pl
from jax.experimental.pallas import tpu as pltpu
from jax.sharding import PartitionSpec as P

CAP = 2
SIDE = 128
META_TILE = (1, 128)
PIECES = 4
CHAINS, LAST_CHAINS = 5, 3
K2_LIMIT = 30
SPAN = 10
LOW_COL, HIGH_COL = 768, 1152
AMP = jnp.int16
AMP_MIDDLE, AMP_STEPS = 2.625, 16384.0
MESH = pl.DeviceIdType.MESH


def dft_operands():
    index = np.arange(SIDE)
    angles = (index[:, None] * index[None, :] % SIDE) * (2.0 * math.pi / SIDE)
    wave = np.cos(angles) / math.sqrt(SIDE)
    wave[SIDE // 2 + 1 :] = np.sin(angles[1 : SIDE // 2]) / math.sqrt(SIDE)

    def product(block):
        block = block.astype(np.float32)
        high = block.astype(jnp.bfloat16)
        low = (block - high.astype(np.float32)).astype(jnp.bfloat16)
        return np.block([[high, high], [low, np.zeros_like(low)]])

    order = np.zeros((SIDE, SIDE), jnp.bfloat16)
    order[index, np.where(index <= SIDE // 2, index, SIDE + SIDE // 2 - index)] = 1
    return np.stack([product(wave), product(wave.T)]), order


def coded(measured):
    return jnp.round((jnp.sqrt(measured) - AMP_MIDDLE) * AMP_STEPS)


def decoded(code):
    return code.astype(jnp.int32).astype(jnp.float32) * (1.0 / AMP_STEPS) + AMP_MIDDLE


def multiply(left, planes):
    x = jnp.concatenate(planes, axis=1)
    high = x.astype(jnp.bfloat16)
    low = (x - high.astype(jnp.float32)).astype(jnp.bfloat16)
    y = jnp.dot(left, jnp.concatenate([high, low], axis=0), preferred_element_type=jnp.float32)
    y = y[:SIDE] + y[SIDE:]
    return [y[:, k * SIDE : (k + 1) * SIDE] for k in range(len(planes))]


def halves(plane):
    return plane[: SIDE // 2], plane[SIDE // 2 :]


def with_first_row(first, rest):
    row = lax.broadcasted_iota(jnp.int32, (8, SIDE), 0)
    return jnp.concatenate([jnp.where(row == 0, first[:8], rest[:8]), rest[8:]], axis=0)


def unfold(real, imag):
    (tr, br), (ti, bi) = halves(real), halves(imag)
    return (
        jnp.concatenate([with_first_row(tr, tr + bi), with_first_row(br, tr - bi)], axis=0),
        jnp.concatenate([with_first_row(ti, ti - br), with_first_row(bi, ti + br)], axis=0),
    )


def fold(real, imag):
    (tr, br), (ti, bi) = halves(real), halves(imag)
    return (
        jnp.concatenate([with_first_row(tr, tr + br), with_first_row(br, bi - ti)], axis=0),
        jnp.concatenate([with_first_row(ti, ti + bi), with_first_row(bi, tr - br)], axis=0),
    )


def to_frequency(waves, fields):
    for turn in (True, False):
        planes = multiply(waves[0], [plane for field in fields for plane in field])
        yield
        fields = [unfold(*planes[k : k + 2]) for k in range(0, len(planes), 2)]
        if turn:
            fields = [(real.T, imag.T) for real, imag in fields]
    return fields


def from_frequency(waves, fields):
    for turn in (True, False):
        planes = multiply(waves[1], [plane for field in fields for plane in fold(*field)])
        yield
        if turn:
            planes = [plane.T for plane in planes]
        fields = [tuple(planes[k : k + 2]) for k in range(0, len(planes), 2)]
    return fields


def product(left, right):
    return left[0] * right[0] - left[1] * right[1], left[0] * right[1] + left[1] * right[0]


def conjugate_product(left, right):
    return left[0] * right[0] + left[1] * right[1], left[0] * right[1] - left[1] * right[0]


def grads_kernel(field, amp, meta_hbm, probe, prop_ref, waves_hbm, packed, grad, waves, meta_ref, order, sems):
    core = lax.axis_index("pos") % 2
    base = 6 * core
    meta_load = pltpu.make_async_copy(meta_hbm, meta_ref, sems.at[0])
    meta_load.start()
    waves_load = pltpu.make_async_copy(waves_hbm, waves, sems.at[1])
    waves_load.start()

    meta_load.wait()

    def read(slot):
        code = meta_ref[slot // 32, slot % 32 // 2, 0, slot % 2] - 1
        return code >= 0, code // 2048, code % 2048

    def tally(slot, counts):
        valid, _, col = read(slot)
        here = valid.astype(jnp.int32)
        first = here * (col < LOW_COL).astype(jnp.int32)
        last = here * (col > HIGH_COL).astype(jnp.int32)
        return counts[0] + here, counts[1] + first, counts[2] + last

    def tally_and_clear(index, counts):
        for k in range(8):
            counts = tally(8 * index + k, counts)
        for k in range(SPAN // 2):
            tile = SPAN // 2 * index + k
            grad[tile // 4, tile % 4] = jnp.zeros((2 * SIDE, SIDE), jnp.float32)
        return counts

    whole, first_only, last_only = lax.fori_loop(0, 8, tally_and_clear, (0, 0, 0))
    either = whole - first_only - last_only
    to_first = jnp.clip((whole + 1) // 2 - first_only, 0, either)

    def collect(slot, state):
        count, seen = state
        valid, _, col = read(slot)
        free = (col >= LOW_COL) & (col <= HIGH_COL)
        on_first = (col < LOW_COL) | (free & (seen < to_first))
        order[count] = slot
        mine = valid & (on_first == (core == 0))
        return count + mine.astype(jnp.int32), seen + (valid & free).astype(jnp.int32)

    count, _ = lax.fori_loop(0, 64, collect, (0, 0), unroll=8)
    waves_load.wait()
    lane = lax.broadcasted_iota(jnp.int32, (SIDE, SIDE), 1)

    def place(slot):
        valid, row, col = read(slot)
        row, col = jnp.where(valid, row, 0), jnp.where(valid, col, base * SIDE)
        block, shift = jnp.clip(col // SIDE - base, 0, SPAN - 1), col % SIDE
        return pl.ds(row, SIDE), block, jnp.minimum(block + 1, SPAN - 1), shift

    def cut(plane, where):
        rows, block, next_block, shift = where
        back = (SIDE - shift) % SIDE
        first = pltpu.roll(field[plane, block, rows, :], back, 1)
        second = pltpu.roll(field[plane, next_block, rows, :], back, 1)
        return jnp.where(lane < SIDE - shift, first, second)

    def add(plane, where, value):
        rows, block, next_block, shift = where
        moved = pltpu.roll(value.astype(jnp.bfloat16).astype(jnp.float32), shift, 1)
        zero = jnp.zeros_like(moved)
        grad[block, plane, rows, :] += jnp.where(lane >= shift, moved, zero)
        grad[next_block, plane, rows, :] += jnp.where(lane < shift, moved, zero)

    def stages(where, slot, weight):
        t0, t1 = [(cut(k, where), cut(k + 2, where)) for k in range(2)]
        probes = [(probe[m, 0], probe[m, 1]) for m in range(2)]
        prop = (prop_ref[0], prop_ref[1])
        fields = [product(p, t0) for p in probes]
        yield
        fields = yield from to_frequency(waves, fields)
        middle = yield from from_frequency(waves, [product(f, prop) for f in fields])
        far = yield from to_frequency(waves, [product(u, t1) for u in middle])
        model = 1.0 + sum(real * real + imag * imag for real, imag in far)
        factor = weight * (1.0 - decoded(amp[slot // 32, slot % 32 // 2, slot % 2]) * lax.rsqrt(model))
        fields = yield from from_frequency(waves, [(real * factor, imag * factor) for real, imag in far])

        def add_slice(k, parts):
            add(k, where, parts[0][0] + parts[1][0])
            add(k + 2, where, parts[0][1] + parts[1][1])

        add_slice(1, [conjugate_product(u, g) for u, g in zip(middle, fields)])
        fields = yield from to_frequency(waves, [conjugate_product(t1, g) for g in fields])
        fields = yield from from_frequency(waves, [conjugate_product(prop, h) for h in fields])
        add_slice(0, [conjugate_product(p, e) for p, e in zip(probes, fields)])

    def step(groups, start, index, _):
        running = []
        for group in range(groups):
            item = start + index * groups + group
            slot = order[jnp.minimum(item, count - 1)]
            weight = jnp.where(item < count, 2.0, 0.0).astype(jnp.float32)
            running.append(stages(place(slot), slot, weight))
        while running:
            running = [machine for machine in running if next(machine, 0) is None]
        return 0

    full = (count + CHAINS - 1 - LAST_CHAINS) // CHAINS
    lax.fori_loop(0, full, functools.partial(step, CHAINS, 0), 0)
    rest = jnp.clip(count - CHAINS * full, 0, 1)
    lax.fori_loop(0, rest, functools.partial(step, LAST_CHAINS, CHAINS * full), 0)

    def pack(block, _):
        packed[block] = grad[block].astype(jnp.bfloat16)
        return 0

    lax.fori_loop(0, SPAN, pack, 0)


def grads_call(field, amp, meta, probe, prop, waves):
    hbm = pl.BlockSpec(memory_space=pltpu.HBM)
    vmem = pl.BlockSpec(memory_space=pltpu.VMEM)
    return pl.pallas_call(
        grads_kernel,
        out_shape=jax.ShapeDtypeStruct((SPAN, 4, 2 * SIDE, SIDE), jnp.bfloat16),
        in_specs=[vmem] * 5 + [hbm],
        out_specs=vmem,
        scratch_shapes=[
            pltpu.VMEM((SPAN, 4, 2 * SIDE, SIDE), jnp.float32),
            pltpu.VMEM(waves.shape, jnp.bfloat16),
            pltpu.SMEM(meta.shape, jnp.int32),
            pltpu.SMEM((65,), jnp.int32),
            pltpu.SemaphoreType.DMA((2,)),
        ],
        compiler_params=pltpu.CompilerParams(vmem_limit_bytes=K2_LIMIT * 2**20),
        name="window_gradients",
    )(field, amp, meta, probe, prop, pltpu.with_memory_space_constraint(waves, pltpu.HBM))


def send_kernel(obj_ref, measured_ref, phase_hbm, turn_hbm, offsets_ref, field, amp_ref, meta_ref, prop_ref,
                wide, measured, own, phase, turn, halo_ref, codes_ref, chunk, amp_out, meta_out, local_sem, halo_send, halo_recv, shared_sem, slot_sem, twin_sem):
    strip, pos = lax.axis_index("obj"), lax.axis_index("pos")
    x, core = pos // 2, pos % 2
    twin = (strip, x * 2 + 1 - core)

    def span(block):
        return pl.ds(pl.multiple_of(block * SIDE, SIDE), 2 * SIDE)

    loads = [
        pltpu.make_async_copy(obj_ref.at[:, :, span(8 * core + 2 * x)], wide, local_sem.at[0]),
        pltpu.make_async_copy(measured_ref, measured, local_sem.at[1]),
        pltpu.make_async_copy(turn_hbm, turn, local_sem.at[2]),
        pltpu.make_async_copy(phase_hbm, phase, local_sem.at[3]),
        pltpu.make_async_copy(obj_ref.at[:, :, pl.ds(pl.multiple_of(6 * core * SIDE, SIDE), SPAN * SIDE)], own, local_sem.at[4]),
    ]
    for load in loads:
        load.start()
    barrier = pltpu.get_barrier_semaphore()

    def greet_strip(step, _):
        pl.semaphore_signal(barrier, inc=1, device_id=(lax.rem(strip + step, 16), pos), device_id_type=MESH)
        return 0

    lax.fori_loop(1, 16, greet_strip, 0)
    for step in range(1, 4):
        other = lax.rem(x + step, 4) * 2 + core
        pl.semaphore_signal(barrier, inc=1, device_id=(strip, other), device_id_type=MESH)
    pl.semaphore_signal(barrier, inc=1, device_id=twin, device_id_type=MESH)
    loads[0].wait()
    for block in range(2):
        lanes = slice(block * SIDE, (block + 1) * SIDE)
        for plane in range(4):
            chunk[plane * 2 + block] = wide[plane, :, lanes].astype(jnp.bfloat16)
    pl.semaphore_wait(barrier, 19)

    def piece(number):
        return pl.ds(number * (8 // PIECES), 8 // PIECES)

    def spread(source, index, number, where, send):
        return pltpu.make_async_remote_copy(
            src_ref=source.at[piece(number)], dst_ref=halo_ref.at[index, piece(number)], send_sem=halo_send.at[send, number],
            recv_sem=halo_recv.at[index, number], device_id=where, device_id_type=MESH,
        )

    above = (lax.rem(strip + 15, 16), pos)
    for number in range(PIECES):
        spread(chunk, x, number, above, 0).start()

    def amp_copy(target):
        return pltpu.make_async_remote_copy(
            src_ref=amp_out.at[target], dst_ref=amp_ref.at[core, strip], send_sem=slot_sem.at[0],
            recv_sem=slot_sem.at[1], device_id=(target, pos), device_id_type=MESH,
        )

    def meta_copy(target):
        return pltpu.make_async_remote_copy(
            src_ref=meta_out.at[target], dst_ref=meta_ref.at[core, strip], send_sem=slot_sem.at[2],
            recv_sem=slot_sem.at[3], device_id=(target, pos), device_id_type=MESH,
        )

    def all_copies():
        others = pl.ds(0, 15)
        return [
            pltpu.make_async_remote_copy(
                src_ref=source.at[others], dst_ref=target.at[core, others], send_sem=slot_sem.at[2 * k],
                recv_sem=slot_sem.at[2 * k + 1], device_id=twin, device_id_type=MESH,
            )
            for k, (source, target) in enumerate(((amp_out, amp_ref), (meta_out, meta_ref)))
        ]

    def to_twin(side):
        return [
            pltpu.make_async_remote_copy(
                src_ref=ref.at[core], dst_ref=ref.at[side], send_sem=twin_sem.at[2 * k], recv_sem=twin_sem.at[2 * k + 1],
                device_id=twin, device_id_type=MESH,
            )
            for k, ref in enumerate((amp_ref, meta_ref))
        ]

    lane = lax.broadcasted_iota(jnp.int32, META_TILE, 1)
    loads[1].wait()
    loads[2].wait()
    turn_back = turn[...].astype(jnp.float32).T.astype(jnp.bfloat16)

    def reorder(planes):
        rows = jnp.dot(jnp.concatenate(planes, axis=0).astype(jnp.bfloat16), turn_back, preferred_element_type=jnp.float32)
        rows = [rows[k * SIDE : (k + 1) * SIDE].T for k in range(len(planes))]
        rows = jnp.dot(jnp.concatenate(rows, axis=0).astype(jnp.bfloat16), turn_back, preferred_element_type=jnp.float32)
        return [rows[k * SIDE : (k + 1) * SIDE] for k in range(len(planes))]

    def encode(group, _):
        codes = [coded(measured[4 * group + k]) for k in range(4)]
        high = [jnp.floor(code * (1.0 / 256.0)) for code in codes]
        planes = reorder(high + [code - 256.0 * part for code, part in zip(codes, high)])
        for k in range(4):
            codes_ref[4 * group + k] = (256.0 * planes[k] + planes[4 + k]).astype(jnp.int32).astype(AMP)
        return 0

    lax.fori_loop(0, measured.shape[0] // 4, encode, 0)

    def packed(target):
        where, codes, seen = [jnp.int32(0)] * CAP, [jnp.int32(0)] * CAP, jnp.int32(0)
        for item in range(offsets_ref.shape[1]):
            row, col = offsets_ref[0, item], offsets_ref[1, item]
            here = row // SIDE == target
            for k in range(CAP):
                take = here & (seen == k)
                where[k] = jnp.where(take, item, where[k])
                codes[k] = jnp.where(take, 1 + row % SIDE * 2048 + col, codes[k])
            seen = seen + here.astype(jnp.int32)
        return jnp.where(lane == 0, codes[0], codes[1]), [codes_ref[index] for index in where]

    def pack(step, _):
        target = (strip // 4 + step % 4) % 4 * 4 + (strip + step // 4) % 4
        codes, values = packed(target)
        meta_out[target] = codes
        for k in range(CAP):
            amp_out[target, k] = values[k]
        amp_copy(target).start()
        meta_copy(target).start()
        return 0

    def forward(number):
        spread(chunk, x, number, above, 0).wait_recv()
        for step in (2, 1, 3):
            spread(halo_ref.at[x], x, number, (strip, lax.rem(x + step, 4) * 2 + core), step).start()

    bounds = [1, 6] + [6 + (10 * k) // PIECES for k in range(1, PIECES)] + [16]
    lax.fori_loop(1, 16, pack, 0)
    for number in range(PIECES):
        forward(number)
    codes, values = packed(strip)
    meta_ref[core, strip] = codes
    for k in range(CAP):
        amp_ref[core, strip, k] = values[k]

    loads[3].wait()
    value, planes = phase[...], []
    for _ in range(3):
        planes.append(value.astype(jnp.bfloat16))
        value = value - planes[-1].astype(jnp.float32)
    planes = reorder(planes)
    moved_phase = planes[0] + planes[1] + planes[2]
    prop_ref[0] = jnp.cos(moved_phase)
    prop_ref[1] = jnp.sin(moved_phase)
    loads[4].wait()

    def widen_own(block, _):
        span = pl.ds(pl.multiple_of(block * SIDE, SIDE), SIDE)
        for plane in range(4):
            field[plane, block, :SIDE, :] = own[plane, :, span].astype(jnp.bfloat16).astype(jnp.float32)
        return 0

    lax.fori_loop(0, SPAN, widen_own, 0)

    arrivals = all_copies()
    for copy in arrivals:
        copy.wait_recv()
    relays = to_twin(core)
    for copy in relays:
        copy.start()
    for number in range(PIECES):
        for step in range(1, 4):
            spread(chunk, lax.rem(x + step, 4), number, (strip, pos), 0).wait_recv()

    shared = pltpu.make_async_remote_copy(
        src_ref=halo_ref.at[3 - 3 * core], dst_ref=halo_ref.at[4], send_sem=shared_sem.at[0], recv_sem=shared_sem.at[1],
        device_id=twin, device_id_type=MESH,
    )
    shared.start()

    def widen_halo(step, _):
        part = step // 2
        block = 2 * core + step
        for plane in range(4):
            field[plane, block, SIDE:, :] = halo_ref[part, 2 * plane + step % 2].astype(jnp.float32)
        return 0

    lax.fori_loop(0, 8, widen_halo, 0)
    shared.wait()
    for plane in range(4):
        for block in range(2):
            field[plane, 8 - 8 * core + block, SIDE:, :] = halo_ref[4, 2 * plane + block].astype(jnp.float32)
    for copy in arrivals + relays:
        copy.wait_send()
    for copy in to_twin(1 - core):
        copy.wait_recv()
    for number in range(PIECES):
        for step in range(4):
            spread(chunk, x, number, (strip, pos), step).wait_send()


def send_call(obj, measured, phase, order, offsets):
    hbm = pl.BlockSpec(memory_space=pltpu.HBM)
    vmem = pl.BlockSpec(memory_space=pltpu.VMEM)
    dma = pltpu.SemaphoreType.DMA
    return pl.pallas_call(
        send_kernel,
        out_shape=(
            jax.ShapeDtypeStruct((4, SPAN, 2 * SIDE, SIDE), jnp.float32),
            jax.ShapeDtypeStruct((2, 16, CAP, SIDE, SIDE), AMP),
            jax.ShapeDtypeStruct((2, 16, *META_TILE), jnp.int32),
            jax.ShapeDtypeStruct((2, SIDE, SIDE), jnp.float32),
        ),
        in_specs=[hbm] * 4 + [pl.BlockSpec(memory_space=pltpu.SMEM)],
        out_specs=(vmem,) * 4,
        scratch_shapes=[
            pltpu.VMEM((4, SIDE, 2 * SIDE), jnp.float32),
            pltpu.VMEM(measured.shape, jnp.float32),
            pltpu.VMEM((4, SIDE, SPAN * SIDE), jnp.float32),
            pltpu.VMEM((SIDE, SIDE), jnp.float32),
            pltpu.VMEM((SIDE, SIDE), jnp.bfloat16),
            pltpu.VMEM((5, 8, SIDE, SIDE), jnp.bfloat16),
            pltpu.VMEM(measured.shape, AMP),
            pltpu.VMEM((8, SIDE, SIDE), jnp.bfloat16),
            pltpu.VMEM((16, CAP, SIDE, SIDE), AMP),
            pltpu.VMEM((16, *META_TILE), jnp.int32),
            dma((5,)),
            dma((4, PIECES)),
            dma((4, PIECES)),
            dma((2,)),
            dma((4,)),
            dma((4,)),
        ],
        compiler_params=pltpu.CompilerParams(collective_id=0, has_side_effects=True, vmem_limit_bytes=20 * 2**20),
        name="exchange_inputs",
    )(*[pltpu.with_memory_space_constraint(x, pltpu.HBM) for x in (obj, measured, phase, order)], offsets)


def sum_kernel(grad_ref, out_ref, theirs, joined, from_above, raised, parts, low_in, low_out, twin_sem, z_send, z_recv, x_send, x_recv, low_sem):
    strip, pos = lax.axis_index("obj"), lax.axis_index("pos")
    x, core = pos // 2, pos % 2
    twin = (strip, x * 2 + 1 - core)
    below, above = (lax.rem(strip + 1, 16), pos), (lax.rem(strip + 15, 16), pos)
    barrier = pltpu.get_barrier_semaphore()
    for step in range(1, 8):
        pl.semaphore_signal(barrier, inc=1, device_id=(strip, lax.rem(pos + step, 8)), device_id_type=MESH)
    for device in (below, above):
        pl.semaphore_signal(barrier, inc=1, device_id=device, device_id_type=MESH)
    pl.semaphore_wait(barrier, 9)

    shared = 3 - 3 * core
    plain = lax.rem(shared + 2, 4)
    early = [lax.rem(shared + 1, 4), lax.rem(shared + 3, 4)]
    lower, upper = pl.ds(SIDE, SIDE), pl.ds(0, SIDE)
    halves = (lower, upper)

    def place(pair, block):
        return 2 * pair + 2 * core + block

    to_twin = pltpu.make_async_remote_copy(
        src_ref=grad_ref.at[pl.ds(8 - 8 * core, 2)], dst_ref=theirs, send_sem=twin_sem.at[0], recv_sem=twin_sem.at[1],
        device_id=twin, device_id_type=MESH,
    )
    to_twin.start()

    def downward(which, block):
        return pltpu.make_async_remote_copy(
            src_ref=grad_ref.at[place(early[which], block), :, lower], dst_ref=from_above.at[which, block],
            send_sem=z_send.at[which, block], recv_sem=z_recv.at[which, block], device_id=below, device_id_type=MESH,
        )

    for block in range(2):
        for which in range(2):
            downward(which, block).start()

    def remote(pair, source, half, block, target, start):
        return pltpu.make_async_remote_copy(
            src_ref=source, dst_ref=parts.at[start, half, block], send_sem=x_send.at[pair, half, block],
            recv_sem=x_recv.at[start, half, block], device_id=(strip, target), device_id_type=MESH,
        )

    def give(pair, source, half, block):
        target = 4 * core + pair

        @pl.when(target != pos)
        def _():
            remote(pair, source, half, block, target, x).start()

        @pl.when(target == pos)
        def _():
            pltpu.make_async_copy(source, parts.at[x, half, block], x_recv.at[x, half, block]).start()

    for half in range(2):
        for block in range(2):
            give(plain, grad_ref.at[place(plain, block), :, halves[half]], half, block)
    to_twin.wait_recv()
    for half in range(2):
        rows = slice(SIDE, None) if half == 0 else slice(0, SIDE)
        for block in range(2):
            for plane in range(4):
                own = grad_ref[place(shared, block), plane, rows].astype(jnp.float32)
                joined[block, plane, rows] = (own + theirs[block, plane, rows].astype(jnp.float32)).astype(jnp.bfloat16)
            give(shared, joined.at[block, :, halves[half]], half, block)
    for block in range(2):
        for which in range(2):
            downward(which, block).wait_recv()
            for plane in range(4):
                own = grad_ref[place(early[which], block), plane, :SIDE].astype(jnp.float32)
                raised[which, block, plane] = (own + from_above[which, block, plane].astype(jnp.float32)).astype(jnp.bfloat16)
            give(early[which], raised.at[which, block], 1, block)

    def arrived(half, block):
        for start in range(4):
            remote(0, joined.at[block, :, upper], half, block, pos, start).wait_recv()

    def total(half, block, plane):
        value = parts[0, half, block, plane].astype(jnp.float32)
        for start in range(1, 4):
            value += parts[start, half, block, plane].astype(jnp.float32)
        return value

    shift = pltpu.make_async_remote_copy(
        src_ref=low_out, dst_ref=low_in, send_sem=low_sem.at[0], recv_sem=low_sem.at[1], device_id=below, device_id_type=MESH,
    )
    sends_low = lax.rem(pos, 4) % 2 != pos // 4

    @pl.when(sends_low)
    def _():
        for block in range(2):
            arrived(0, block)
            for plane in range(4):
                low_out[block, plane] = total(0, block, plane).astype(jnp.bfloat16)
        shift.start()

    for block in range(2):
        arrived(1, block)
        for plane in range(4):
            out_ref[plane, :, block * SIDE : (block + 1) * SIDE] = total(1, block, plane)

    @pl.when(sends_low)
    def _():
        shift.wait_recv()
        for block in range(2):
            for plane in range(4):
                out_ref[plane, :, block * SIDE : (block + 1) * SIDE] += low_in[block, plane].astype(jnp.float32)
        shift.wait_send()

    to_twin.wait_send()
    for block in range(2):
        for which in range(2):
            downward(which, block).wait_send()
    for pair, sent in ((plain, (0, 1)), (shared, (0, 1)), (early[0], (1,)), (early[1], (1,))):

        @pl.when(4 * core + pair != pos)
        def _():
            for half in sent:
                for block in range(2):
                    remote(pair, joined.at[block, :, upper], half, block, twin[1], x).wait_send()


def sum_call(grad):
    dma = pltpu.SemaphoreType.DMA
    two = (2, 4, 2 * SIDE, SIDE)
    return pl.pallas_call(
        sum_kernel,
        out_shape=jax.ShapeDtypeStruct((4, SIDE, 2 * SIDE), jnp.float32),
        in_specs=[pl.BlockSpec(memory_space=pltpu.VMEM)],
        out_specs=pl.BlockSpec(memory_space=pltpu.VMEM),
        scratch_shapes=[
            pltpu.VMEM(two, jnp.bfloat16),
            pltpu.VMEM(two, jnp.bfloat16),
            pltpu.VMEM((2, 2, 4, SIDE, SIDE), jnp.bfloat16),
            pltpu.VMEM((2, 2, 4, SIDE, SIDE), jnp.bfloat16),
            pltpu.VMEM((4, 2, 2, 4, SIDE, SIDE), jnp.bfloat16),
            pltpu.VMEM((2, 4, SIDE, SIDE), jnp.bfloat16),
            pltpu.VMEM((2, 4, SIDE, SIDE), jnp.bfloat16),
            dma((2,)),
            dma((2, 2)),
            dma((2, 2)),
            dma((4, 2, 2)),
            dma((4, 2, 2)),
            dma((2,)),
        ],
        compiler_params=pltpu.CompilerParams(collective_id=1, has_side_effects=True, vmem_limit_bytes=20 * 2**20),
        name="sum_gradients",
    )(grad)


def per_device(object_field, probe_modes, propagator_phase, offsets, measured):
    obj = object_field.reshape(4, SIDE, object_field.shape[3])
    waves, order = [jnp.asarray(x) for x in dft_operands()]
    field, amp, meta, prop = send_call(obj, measured, propagator_phase, order, offsets.T)
    grad = grads_call(field, amp, meta, probe_modes, prop, waves)
    return sum_call(grad).reshape(2, 2, SIDE, 2 * SIDE)


def solution(mesh):
    placed = (
        P(None, None, "obj", None),
        P(),
        P(),
        P(("obj", "pos"), None),
        P(("obj", "pos"), None, None),
    )
    return jax.shard_map(
        per_device,
        mesh=mesh,
        in_specs=placed,
        out_specs=P(None, None, "obj", "pos"),
        check_vma=False,
    )
```

```python
import functools
import math

import jax
import jax.numpy as jnp
import numpy as np
from jax import lax
from jax.experimental import pallas as pl
from jax.experimental.pallas import tpu as pltpu
from jax.sharding import PartitionSpec as P

CAP = 2
SIDE = 128
META_TILE = (1, 128)
PIECES = 4
CHAINS, LAST_CHAINS = 5, 3
K2_LIMIT = 24
SPAN = 10
LOW_COL, HIGH_COL = 768, 1152
AMP = jnp.int16
AMP_MIDDLE, AMP_STEPS = 2.625, 16384.0
MESH = pl.DeviceIdType.MESH


def dft_operands():
    index = np.arange(SIDE)
    angles = (index[:, None] * index[None, :] % SIDE) * (2.0 * math.pi / SIDE)
    wave = np.cos(angles) / math.sqrt(SIDE)
    wave[SIDE // 2 + 1 :] = np.sin(angles[1 : SIDE // 2]) / math.sqrt(SIDE)

    def product(block):
        block = block.astype(np.float32)
        high = block.astype(jnp.bfloat16)
        low = (block - high.astype(np.float32)).astype(jnp.bfloat16)
        return np.block([[high, high], [low, np.zeros_like(low)]])

    order = np.zeros((SIDE, SIDE), jnp.bfloat16)
    order[index, np.where(index <= SIDE // 2, index, SIDE + SIDE // 2 - index)] = 1
    return np.stack([product(wave), product(wave.T)]), order


def coded(measured):
    return jnp.round((jnp.sqrt(measured) - AMP_MIDDLE) * AMP_STEPS)


def decoded(code):
    return code.astype(jnp.int32).astype(jnp.float32) * (1.0 / AMP_STEPS) + AMP_MIDDLE


def multiply(left, planes):
    x = jnp.concatenate(planes, axis=1)
    high = x.astype(jnp.bfloat16)
    low = (x - high.astype(jnp.float32)).astype(jnp.bfloat16)
    y = jnp.dot(left, jnp.concatenate([high, low], axis=0), preferred_element_type=jnp.float32)
    y = y[:SIDE] + y[SIDE:]
    return [y[:, k * SIDE : (k + 1) * SIDE] for k in range(len(planes))]


def halves(plane):
    return plane[: SIDE // 2], plane[SIDE // 2 :]


def with_first_row(first, rest):
    row = lax.broadcasted_iota(jnp.int32, (8, SIDE), 0)
    return jnp.concatenate([jnp.where(row == 0, first[:8], rest[:8]), rest[8:]], axis=0)


def unfold(real, imag):
    (tr, br), (ti, bi) = halves(real), halves(imag)
    return (
        jnp.concatenate([with_first_row(tr, tr + bi), with_first_row(br, tr - bi)], axis=0),
        jnp.concatenate([with_first_row(ti, ti - br), with_first_row(bi, ti + br)], axis=0),
    )


def fold(real, imag):
    (tr, br), (ti, bi) = halves(real), halves(imag)
    return (
        jnp.concatenate([with_first_row(tr, tr + br), with_first_row(br, bi - ti)], axis=0),
        jnp.concatenate([with_first_row(ti, ti + bi), with_first_row(bi, tr - br)], axis=0),
    )


def to_frequency(waves, fields):
    for turn in (True, False):
        planes = multiply(waves[0], [plane for field in fields for plane in field])
        yield
        fields = [unfold(*planes[k : k + 2]) for k in range(0, len(planes), 2)]
        if turn:
            fields = [(real.T, imag.T) for real, imag in fields]
    return fields


def from_frequency(waves, fields):
    for turn in (True, False):
        planes = multiply(waves[1], [plane for field in fields for plane in fold(*field)])
        yield
        if turn:
            planes = [plane.T for plane in planes]
        fields = [tuple(planes[k : k + 2]) for k in range(0, len(planes), 2)]
    return fields


def product(left, right):
    return left[0] * right[0] - left[1] * right[1], left[0] * right[1] + left[1] * right[0]


def conjugate_product(left, right):
    return left[0] * right[0] + left[1] * right[1], left[0] * right[1] - left[1] * right[0]


def grads_kernel(field, amp, meta_hbm, probe, prop_ref, waves_hbm, grad, waves, meta_ref, order, sems):
    core = lax.axis_index("pos") % 2
    base = 6 * core
    meta_load = pltpu.make_async_copy(meta_hbm, meta_ref, sems.at[0])
    meta_load.start()
    waves_load = pltpu.make_async_copy(waves_hbm, waves, sems.at[1])
    waves_load.start()

    meta_load.wait()

    def read(slot):
        code = meta_ref[slot // 32, slot % 32 // 2, 0, slot % 2] - 1
        return code >= 0, code // 2048, code % 2048

    def tally(slot, counts):
        valid, _, col = read(slot)
        here = valid.astype(jnp.int32)
        first = here * (col < LOW_COL).astype(jnp.int32)
        last = here * (col > HIGH_COL).astype(jnp.int32)
        return counts[0] + here, counts[1] + first, counts[2] + last

    def tally_and_clear(index, counts):
        for k in range(8):
            counts = tally(8 * index + k, counts)
        for k in range(SPAN // 2):
            tile = SPAN // 2 * index + k
            grad[tile // 4, tile % 4] = jnp.zeros((2 * SIDE, SIDE), jnp.float32)
        return counts

    whole, first_only, last_only = lax.fori_loop(0, 8, tally_and_clear, (0, 0, 0))
    either = whole - first_only - last_only
    to_first = jnp.clip((whole + 1) // 2 - first_only, 0, either)

    def collect(slot, state):
        count, seen = state
        valid, _, col = read(slot)
        free = (col >= LOW_COL) & (col <= HIGH_COL)
        on_first = (col < LOW_COL) | (free & (seen < to_first))
        order[count] = slot
        mine = valid & (on_first == (core == 0))
        return count + mine.astype(jnp.int32), seen + (valid & free).astype(jnp.int32)

    count, _ = lax.fori_loop(0, 64, collect, (0, 0), unroll=8)
    waves_load.wait()
    lane = lax.broadcasted_iota(jnp.int32, (SIDE, SIDE), 1)

    def place(slot):
        valid, row, col = read(slot)
        row, col = jnp.where(valid, row, 0), jnp.where(valid, col, base * SIDE)
        block, shift = jnp.clip(col // SIDE - base, 0, SPAN - 1), col % SIDE
        return pl.ds(row, SIDE), block, jnp.minimum(block + 1, SPAN - 1), shift

    def cut(plane, where):
        rows, block, next_block, shift = where
        back = (SIDE - shift) % SIDE
        first = pltpu.roll(field[plane, block, rows, :], back, 1)
        second = pltpu.roll(field[plane, next_block, rows, :], back, 1)
        return jnp.where(lane < SIDE - shift, first, second)

    def add(plane, where, value):
        rows, block, next_block, shift = where
        moved = pltpu.roll(value.astype(jnp.bfloat16).astype(jnp.float32), shift, 1)
        zero = jnp.zeros_like(moved)
        grad[block, plane, rows, :] += jnp.where(lane >= shift, moved, zero)
        grad[next_block, plane, rows, :] += jnp.where(lane < shift, moved, zero)

    def stages(where, slot, weight):
        t0, t1 = [(cut(k, where), cut(k + 2, where)) for k in range(2)]
        probes = [(probe[m, 0], probe[m, 1]) for m in range(2)]
        prop = (prop_ref[0], prop_ref[1])
        fields = [product(p, t0) for p in probes]
        yield
        fields = yield from to_frequency(waves, fields)
        middle = yield from from_frequency(waves, [product(f, prop) for f in fields])
        far = yield from to_frequency(waves, [product(u, t1) for u in middle])
        model = 1.0 + sum(real * real + imag * imag for real, imag in far)
        factor = weight * (1.0 - decoded(amp[slot // 32, slot % 32 // 2, slot % 2]) * lax.rsqrt(model))
        fields = yield from from_frequency(waves, [(real * factor, imag * factor) for real, imag in far])

        def add_slice(k, parts):
            add(k, where, parts[0][0] + parts[1][0])
            add(k + 2, where, parts[0][1] + parts[1][1])

        add_slice(1, [conjugate_product(u, g) for u, g in zip(middle, fields)])
        fields = yield from to_frequency(waves, [conjugate_product(t1, g) for g in fields])
        fields = yield from from_frequency(waves, [conjugate_product(prop, h) for h in fields])
        add_slice(0, [conjugate_product(p, e) for p, e in zip(probes, fields)])

    def step(groups, start, index, _):
        running = []
        for group in range(groups):
            item = start + index * groups + group
            slot = order[jnp.minimum(item, count - 1)]
            weight = jnp.where(item < count, 2.0, 0.0).astype(jnp.float32)
            running.append(stages(place(slot), slot, weight))
        while running:
            running = [machine for machine in running if next(machine, 0) is None]
        return 0

    full = (count + CHAINS - 1 - LAST_CHAINS) // CHAINS
    lax.fori_loop(0, full, functools.partial(step, CHAINS, 0), 0)
    rest = jnp.clip(count - CHAINS * full, 0, 1)
    lax.fori_loop(0, rest, functools.partial(step, LAST_CHAINS, CHAINS * full), 0)


def grads_call(field, amp, meta, probe, prop, waves):
    hbm = pl.BlockSpec(memory_space=pltpu.HBM)
    vmem = pl.BlockSpec(memory_space=pltpu.VMEM)
    return pl.pallas_call(
        grads_kernel,
        out_shape=jax.ShapeDtypeStruct((SPAN, 4, 2 * SIDE, SIDE), jnp.float32),
        in_specs=[vmem] * 5 + [hbm],
        out_specs=vmem,
        scratch_shapes=[
            pltpu.VMEM(waves.shape, jnp.bfloat16),
            pltpu.SMEM(meta.shape, jnp.int32),
            pltpu.SMEM((65,), jnp.int32),
            pltpu.SemaphoreType.DMA((2,)),
        ],
        compiler_params=pltpu.CompilerParams(vmem_limit_bytes=K2_LIMIT * 2**20),
        name="window_gradients",
    )(field, amp, meta, probe, prop, pltpu.with_memory_space_constraint(waves, pltpu.HBM))


def send_kernel(obj_ref, measured_ref, phase_hbm, turn_hbm, offsets_hbm, field, amp_ref, meta_ref, prop_ref,
                offsets_ref, wide, measured, own, phase, turn, halo_ref, codes_ref, chunk, amp_out, meta_out, local_sem, halo_send, halo_recv, shared_sem, slot_sem, twin_sem):
    strip, pos = lax.axis_index("obj"), lax.axis_index("pos")
    x, core = pos // 2, pos % 2
    twin = (strip, x * 2 + 1 - core)

    def span(block):
        return pl.ds(pl.multiple_of(block * SIDE, SIDE), 2 * SIDE)

    loads = [
        pltpu.make_async_copy(obj_ref.at[:, :, span(8 * core + 2 * x)], wide, local_sem.at[0]),
        pltpu.make_async_copy(measured_ref, measured, local_sem.at[1]),
        pltpu.make_async_copy(turn_hbm, turn, local_sem.at[2]),
        pltpu.make_async_copy(phase_hbm, phase, local_sem.at[3]),
        pltpu.make_async_copy(obj_ref.at[:, :, pl.ds(pl.multiple_of(6 * core * SIDE, SIDE), SPAN * SIDE)], own, local_sem.at[4]),
    ]
    loads.append(pltpu.make_async_copy(offsets_hbm, offsets_ref, local_sem.at[5]))
    for load in loads:
        load.start()
    barrier = pltpu.get_barrier_semaphore()

    def greet_strip(step, _):
        pl.semaphore_signal(barrier, inc=1, device_id=(lax.rem(strip + step, 16), pos), device_id_type=MESH)
        return 0

    lax.fori_loop(1, 16, greet_strip, 0)
    for step in range(1, 4):
        other = lax.rem(x + step, 4) * 2 + core
        pl.semaphore_signal(barrier, inc=1, device_id=(strip, other), device_id_type=MESH)
    pl.semaphore_signal(barrier, inc=1, device_id=twin, device_id_type=MESH)
    loads[0].wait()
    for block in range(2):
        lanes = slice(block * SIDE, (block + 1) * SIDE)
        for plane in range(4):
            chunk[plane * 2 + block] = wide[plane, :, lanes].astype(jnp.bfloat16)
    pl.semaphore_wait(barrier, 19)

    def piece(number):
        return pl.ds(number * (8 // PIECES), 8 // PIECES)

    def spread(source, index, number, where, send):
        return pltpu.make_async_remote_copy(
            src_ref=source.at[piece(number)], dst_ref=halo_ref.at[index, piece(number)], send_sem=halo_send.at[send, number],
            recv_sem=halo_recv.at[index, number], device_id=where, device_id_type=MESH,
        )

    above = (lax.rem(strip + 15, 16), pos)
    for number in range(PIECES):
        spread(chunk, x, number, above, 0).start()

    def amp_copy(target):
        return pltpu.make_async_remote_copy(
            src_ref=amp_out.at[target], dst_ref=amp_ref.at[core, strip], send_sem=slot_sem.at[0],
            recv_sem=slot_sem.at[1], device_id=(target, pos), device_id_type=MESH,
        )

    def meta_copy(target):
        return pltpu.make_async_remote_copy(
            src_ref=meta_out.at[target], dst_ref=meta_ref.at[core, strip], send_sem=slot_sem.at[2],
            recv_sem=slot_sem.at[3], device_id=(target, pos), device_id_type=MESH,
        )

    def all_copies():
        others = pl.ds(0, 15)
        return [
            pltpu.make_async_remote_copy(
                src_ref=source.at[others], dst_ref=target.at[core, others], send_sem=slot_sem.at[2 * k],
                recv_sem=slot_sem.at[2 * k + 1], device_id=twin, device_id_type=MESH,
            )
            for k, (source, target) in enumerate(((amp_out, amp_ref), (meta_out, meta_ref)))
        ]

    def to_twin(side):
        return [
            pltpu.make_async_remote_copy(
                src_ref=ref.at[core], dst_ref=ref.at[side], send_sem=twin_sem.at[2 * k], recv_sem=twin_sem.at[2 * k + 1],
                device_id=twin, device_id_type=MESH,
            )
            for k, ref in enumerate((amp_ref, meta_ref))
        ]

    lane = lax.broadcasted_iota(jnp.int32, META_TILE, 1)
    loads[1].wait()
    loads[5].wait()
    loads[2].wait()
    turn_back = turn[...].astype(jnp.float32).T.astype(jnp.bfloat16)

    def reorder(planes):
        rows = jnp.dot(jnp.concatenate(planes, axis=0).astype(jnp.bfloat16), turn_back, preferred_element_type=jnp.float32)
        rows = [rows[k * SIDE : (k + 1) * SIDE].T for k in range(len(planes))]
        rows = jnp.dot(jnp.concatenate(rows, axis=0).astype(jnp.bfloat16), turn_back, preferred_element_type=jnp.float32)
        return [rows[k * SIDE : (k + 1) * SIDE] for k in range(len(planes))]

    def encode(group, _):
        codes = [coded(measured[4 * group + k]) for k in range(4)]
        high = [jnp.floor(code * (1.0 / 256.0)) for code in codes]
        planes = reorder(high + [code - 256.0 * part for code, part in zip(codes, high)])
        for k in range(4):
            codes_ref[4 * group + k] = (256.0 * planes[k] + planes[4 + k]).astype(jnp.int32).astype(AMP)
        return 0

    lax.fori_loop(0, measured.shape[0] // 4, encode, 0)

    def packed(target):
        where, codes, seen = [jnp.int32(0)] * CAP, [jnp.int32(0)] * CAP, jnp.int32(0)
        for item in range(offsets_ref.shape[1]):
            row, col = offsets_ref[0, item], offsets_ref[1, item]
            here = row // SIDE == target
            for k in range(CAP):
                take = here & (seen == k)
                where[k] = jnp.where(take, item, where[k])
                codes[k] = jnp.where(take, 1 + row % SIDE * 2048 + col, codes[k])
            seen = seen + here.astype(jnp.int32)
        return jnp.where(lane == 0, codes[0], codes[1]), [codes_ref[index] for index in where]

    def pack(step, _):
        target = (strip // 4 + step % 4) % 4 * 4 + (strip + step // 4) % 4
        codes, values = packed(target)
        meta_out[target] = codes
        for k in range(CAP):
            amp_out[target, k] = values[k]
        amp_copy(target).start()
        meta_copy(target).start()
        return 0

    def forward(number):
        spread(chunk, x, number, above, 0).wait_recv()
        for step in (2, 1, 3):
            spread(halo_ref.at[x], x, number, (strip, lax.rem(x + step, 4) * 2 + core), step).start()

    bounds = [1, 6] + [6 + (10 * k) // PIECES for k in range(1, PIECES)] + [16]
    lax.fori_loop(1, 16, pack, 0)
    for number in range(PIECES):
        forward(number)
    codes, values = packed(strip)
    meta_ref[core, strip] = codes
    for k in range(CAP):
        amp_ref[core, strip, k] = values[k]

    loads[3].wait()
    value, planes = phase[...], []
    for _ in range(3):
        planes.append(value.astype(jnp.bfloat16))
        value = value - planes[-1].astype(jnp.float32)
    planes = reorder(planes)
    moved_phase = planes[0] + planes[1] + planes[2]
    prop_ref[0] = jnp.cos(moved_phase)
    prop_ref[1] = jnp.sin(moved_phase)
    loads[4].wait()

    def widen_own(block, _):
        span = pl.ds(pl.multiple_of(block * SIDE, SIDE), SIDE)
        for plane in range(4):
            field[plane, block, :SIDE, :] = own[plane, :, span].astype(jnp.bfloat16).astype(jnp.float32)
        return 0

    lax.fori_loop(0, SPAN, widen_own, 0)

    arrivals = all_copies()
    for copy in arrivals:
        copy.wait_recv()
    relays = to_twin(core)
    for copy in relays:
        copy.start()
    for number in range(PIECES):
        for step in range(1, 4):
            spread(chunk, lax.rem(x + step, 4), number, (strip, pos), 0).wait_recv()

    shared = pltpu.make_async_remote_copy(
        src_ref=halo_ref.at[3 - 3 * core], dst_ref=halo_ref.at[4], send_sem=shared_sem.at[0], recv_sem=shared_sem.at[1],
        device_id=twin, device_id_type=MESH,
    )
    shared.start()

    def widen_halo(step, _):
        part = step // 2
        block = 2 * core + step
        for plane in range(4):
            field[plane, block, SIDE:, :] = halo_ref[part, 2 * plane + step % 2].astype(jnp.float32)
        return 0

    lax.fori_loop(0, 8, widen_halo, 0)
    shared.wait()
    for plane in range(4):
        for block in range(2):
            field[plane, 8 - 8 * core + block, SIDE:, :] = halo_ref[4, 2 * plane + block].astype(jnp.float32)
    for copy in arrivals + relays:
        copy.wait_send()
    for copy in to_twin(1 - core):
        copy.wait_recv()
    for number in range(PIECES):
        for step in range(4):
            spread(chunk, x, number, (strip, pos), step).wait_send()


def send_call(obj, measured, phase, order, offsets):
    hbm = pl.BlockSpec(memory_space=pltpu.HBM)
    vmem = pl.BlockSpec(memory_space=pltpu.VMEM)
    dma = pltpu.SemaphoreType.DMA
    return pl.pallas_call(
        send_kernel,
        out_shape=(
            jax.ShapeDtypeStruct((4, SPAN, 2 * SIDE, SIDE), jnp.float32),
            jax.ShapeDtypeStruct((2, 16, CAP, SIDE, SIDE), AMP),
            jax.ShapeDtypeStruct((2, 16, *META_TILE), jnp.int32),
            jax.ShapeDtypeStruct((2, SIDE, SIDE), jnp.float32),
        ),
        in_specs=[hbm] * 5,
        out_specs=(vmem,) * 4,
        scratch_shapes=[
            pltpu.SMEM(offsets.shape, jnp.int32),
            pltpu.VMEM((4, SIDE, 2 * SIDE), jnp.float32),
            pltpu.VMEM(measured.shape, jnp.float32),
            pltpu.VMEM((4, SIDE, SPAN * SIDE), jnp.float32),
            pltpu.VMEM((SIDE, SIDE), jnp.float32),
            pltpu.VMEM((SIDE, SIDE), jnp.bfloat16),
            pltpu.VMEM((5, 8, SIDE, SIDE), jnp.bfloat16),
            pltpu.VMEM(measured.shape, AMP),
            pltpu.VMEM((8, SIDE, SIDE), jnp.bfloat16),
            pltpu.VMEM((16, CAP, SIDE, SIDE), AMP),
            pltpu.VMEM((16, *META_TILE), jnp.int32),
            dma((6,)),
            dma((4, PIECES)),
            dma((4, PIECES)),
            dma((2,)),
            dma((4,)),
            dma((4,)),
        ],
        compiler_params=pltpu.CompilerParams(collective_id=0, has_side_effects=True, vmem_limit_bytes=20 * 2**20),
        name="exchange_inputs",
    )(*[pltpu.with_memory_space_constraint(x, pltpu.HBM) for x in (obj, measured, phase, order, offsets)])


def sum_kernel(grad_ref, out_ref, twin_out, plain_out, down_out, theirs, joined, from_above, raised, parts, low_in, low_out, twin_sem, z_send, z_recv, x_send, x_recv, low_sem):
    strip, pos = lax.axis_index("obj"), lax.axis_index("pos")
    x, core = pos // 2, pos % 2
    twin = (strip, x * 2 + 1 - core)
    below, above = (lax.rem(strip + 1, 16), pos), (lax.rem(strip + 15, 16), pos)
    barrier = pltpu.get_barrier_semaphore()
    for step in range(1, 8):
        pl.semaphore_signal(barrier, inc=1, device_id=(strip, lax.rem(pos + step, 8)), device_id_type=MESH)
    for device in (below, above):
        pl.semaphore_signal(barrier, inc=1, device_id=device, device_id_type=MESH)

    shared = 3 - 3 * core
    plain = lax.rem(shared + 2, 4)
    early = [lax.rem(shared + 1, 4), lax.rem(shared + 3, 4)]
    lower, upper = pl.ds(SIDE, SIDE), pl.ds(0, SIDE)
    halves = (lower, upper)

    def place(pair, block):
        return 2 * pair + 2 * core + block

    for block in range(2):
        for plane in range(4):
            twin_out[block, plane] = grad_ref[8 - 8 * core + block, plane].astype(jnp.bfloat16)
            plain_out[block, plane] = grad_ref[place(plain, block), plane].astype(jnp.bfloat16)
            for which in range(2):
                down_out[which, block, plane] = grad_ref[place(early[which], block), plane, SIDE:].astype(jnp.bfloat16)
    pl.semaphore_wait(barrier, 9)
    to_twin = pltpu.make_async_remote_copy(
        src_ref=twin_out, dst_ref=theirs, send_sem=twin_sem.at[0], recv_sem=twin_sem.at[1],
        device_id=twin, device_id_type=MESH,
    )
    to_twin.start()

    def downward(which, block):
        return pltpu.make_async_remote_copy(
            src_ref=down_out.at[which, block], dst_ref=from_above.at[which, block],
            send_sem=z_send.at[which, block], recv_sem=z_recv.at[which, block], device_id=below, device_id_type=MESH,
        )

    for block in range(2):
        for which in range(2):
            downward(which, block).start()

    def remote(pair, source, half, block, target, start):
        return pltpu.make_async_remote_copy(
            src_ref=source, dst_ref=parts.at[start, half, block], send_sem=x_send.at[pair, half, block],
            recv_sem=x_recv.at[start, half, block], device_id=(strip, target), device_id_type=MESH,
        )

    def give(pair, source, half, block):
        target = 4 * core + pair

        @pl.when(target != pos)
        def _():
            remote(pair, source, half, block, target, x).start()

        @pl.when(target == pos)
        def _():
            pltpu.make_async_copy(source, parts.at[x, half, block], x_recv.at[x, half, block]).start()

    for half in range(2):
        for block in range(2):
            give(plain, plain_out.at[block, :, halves[half]], half, block)
    to_twin.wait_recv()
    for half in range(2):
        rows = slice(SIDE, None) if half == 0 else slice(0, SIDE)
        for block in range(2):
            for plane in range(4):
                own = grad_ref[place(shared, block), plane, rows]
                joined[block, plane, rows] = (own + theirs[block, plane, rows].astype(jnp.float32)).astype(jnp.bfloat16)
            give(shared, joined.at[block, :, halves[half]], half, block)
    for block in range(2):
        for which in range(2):
            downward(which, block).wait_recv()
            for plane in range(4):
                own = grad_ref[place(early[which], block), plane, :SIDE]
                raised[which, block, plane] = (own + from_above[which, block, plane].astype(jnp.float32)).astype(jnp.bfloat16)
            give(early[which], raised.at[which, block], 1, block)

    def arrived(half, block):
        for start in range(4):
            remote(0, joined.at[block, :, upper], half, block, pos, start).wait_recv()

    def total(half, block, plane):
        value = parts[0, half, block, plane].astype(jnp.float32)
        for start in range(1, 4):
            value += parts[start, half, block, plane].astype(jnp.float32)
        return value

    shift = pltpu.make_async_remote_copy(
        src_ref=low_out, dst_ref=low_in, send_sem=low_sem.at[0], recv_sem=low_sem.at[1], device_id=below, device_id_type=MESH,
    )
    sends_low = lax.rem(pos, 4) % 2 != pos // 4

    @pl.when(sends_low)
    def _():
        for block in range(2):
            arrived(0, block)
            for plane in range(4):
                low_out[block, plane] = total(0, block, plane).astype(jnp.bfloat16)
        shift.start()

    for block in range(2):
        arrived(1, block)
        for plane in range(4):
            out_ref[plane, :, block * SIDE : (block + 1) * SIDE] = total(1, block, plane)

    @pl.when(sends_low)
    def _():
        shift.wait_recv()
        for block in range(2):
            for plane in range(4):
                out_ref[plane, :, block * SIDE : (block + 1) * SIDE] += low_in[block, plane].astype(jnp.float32)
        shift.wait_send()

    to_twin.wait_send()
    for block in range(2):
        for which in range(2):
            downward(which, block).wait_send()
    for pair, sent in ((plain, (0, 1)), (shared, (0, 1)), (early[0], (1,)), (early[1], (1,))):

        @pl.when(4 * core + pair != pos)
        def _():
            for half in sent:
                for block in range(2):
                    remote(pair, joined.at[block, :, upper], half, block, twin[1], x).wait_send()


def sum_call(grad):
    dma = pltpu.SemaphoreType.DMA
    two = (2, 4, 2 * SIDE, SIDE)
    return pl.pallas_call(
        sum_kernel,
        out_shape=jax.ShapeDtypeStruct((4, SIDE, 2 * SIDE), jnp.float32),
        in_specs=[pl.BlockSpec(memory_space=pltpu.VMEM)],
        out_specs=pl.BlockSpec(memory_space=pltpu.VMEM),
        scratch_shapes=[
            pltpu.VMEM(two, jnp.bfloat16),
            pltpu.VMEM(two, jnp.bfloat16),
            pltpu.VMEM((2, 2, 4, SIDE, SIDE), jnp.bfloat16),
            pltpu.VMEM(two, jnp.bfloat16),
            pltpu.VMEM(two, jnp.bfloat16),
            pltpu.VMEM((2, 2, 4, SIDE, SIDE), jnp.bfloat16),
            pltpu.VMEM((2, 2, 4, SIDE, SIDE), jnp.bfloat16),
            pltpu.VMEM((4, 2, 2, 4, SIDE, SIDE), jnp.bfloat16),
            pltpu.VMEM((2, 4, SIDE, SIDE), jnp.bfloat16),
            pltpu.VMEM((2, 4, SIDE, SIDE), jnp.bfloat16),
            dma((2,)),
            dma((2, 2)),
            dma((2, 2)),
            dma((4, 2, 2)),
            dma((4, 2, 2)),
            dma((2,)),
        ],
        compiler_params=pltpu.CompilerParams(collective_id=1, has_side_effects=True, vmem_limit_bytes=20 * 2**20),
        name="sum_gradients",
    )(grad)


def per_device(object_field, probe_modes, propagator_phase, offsets, measured):
    obj = object_field.reshape(4, SIDE, object_field.shape[3])
    waves, order = [jnp.asarray(x) for x in dft_operands()]
    field, amp, meta, prop = send_call(obj, measured, propagator_phase, order, offsets.T)
    grad = grads_call(field, amp, meta, probe_modes, prop, waves)
    return sum_call(grad).reshape(2, 2, SIDE, 2 * SIDE)


def solution(mesh):
    placed = (
        P(None, None, "obj", None),
        P(),
        P(),
        P(("obj", "pos"), None),
        P(("obj", "pos"), None, None),
    )
    return jax.shard_map(
        per_device,
        mesh=mesh,
        in_specs=placed,
        out_specs=P(None, None, "obj", "pos"),
        check_vma=False,
    )
```

```python
import functools
import math

import jax
import jax.numpy as jnp
import numpy as np
from jax import lax
from jax.experimental import pallas as pl
from jax.experimental.pallas import tpu as pltpu
from jax.sharding import PartitionSpec as P

CAP = 2
SIDE = 128
META_TILE = (1, 128)
PIECES = 4
CHAINS, LAST_CHAINS = 5, 3
K2_LIMIT = 24
SPAN = 10
LOW_COL, HIGH_COL = 768, 1152
AMP = jnp.int16
AMP_MIDDLE, AMP_STEPS = 2.625, 16384.0
MESH = pl.DeviceIdType.MESH


def dft_operands():
    index = np.arange(SIDE)
    angles = (index[:, None] * index[None, :] % SIDE) * (2.0 * math.pi / SIDE)
    wave = np.cos(angles) / math.sqrt(SIDE)
    wave[SIDE // 2 + 1 :] = np.sin(angles[1 : SIDE // 2]) / math.sqrt(SIDE)

    def product(block):
        block = block.astype(np.float32)
        high = block.astype(jnp.bfloat16)
        low = (block - high.astype(np.float32)).astype(jnp.bfloat16)
        return np.block([[high, high], [low, np.zeros_like(low)]])

    order = np.zeros((SIDE, SIDE), jnp.bfloat16)
    order[index, np.where(index <= SIDE // 2, index, SIDE + SIDE // 2 - index)] = 1
    return np.stack([product(wave), product(wave.T)]), order


def coded(measured):
    return jnp.round((jnp.sqrt(measured) - AMP_MIDDLE) * AMP_STEPS)


def decoded(code):
    return code.astype(jnp.int32).astype(jnp.float32) * (1.0 / AMP_STEPS) + AMP_MIDDLE


def multiply(left, planes):
    x = jnp.concatenate(planes, axis=1)
    high = x.astype(jnp.bfloat16)
    low = (x - high.astype(jnp.float32)).astype(jnp.bfloat16)
    y = jnp.dot(left, jnp.concatenate([high, low], axis=0), preferred_element_type=jnp.float32)
    y = y[:SIDE] + y[SIDE:]
    return [y[:, k * SIDE : (k + 1) * SIDE] for k in range(len(planes))]


def halves(plane):
    return plane[: SIDE // 2], plane[SIDE // 2 :]


def with_first_row(first, rest):
    row = lax.broadcasted_iota(jnp.int32, (8, SIDE), 0)
    return jnp.concatenate([jnp.where(row == 0, first[:8], rest[:8]), rest[8:]], axis=0)


def unfold(real, imag):
    (tr, br), (ti, bi) = halves(real), halves(imag)
    return (
        jnp.concatenate([with_first_row(tr, tr + bi), with_first_row(br, tr - bi)], axis=0),
        jnp.concatenate([with_first_row(ti, ti - br), with_first_row(bi, ti + br)], axis=0),
    )


def fold(real, imag):
    (tr, br), (ti, bi) = halves(real), halves(imag)
    return (
        jnp.concatenate([with_first_row(tr, tr + br), with_first_row(br, bi - ti)], axis=0),
        jnp.concatenate([with_first_row(ti, ti + bi), with_first_row(bi, tr - br)], axis=0),
    )


def to_frequency(waves, fields):
    for turn in (True, False):
        planes = multiply(waves[0], [plane for field in fields for plane in field])
        yield
        fields = [unfold(*planes[k : k + 2]) for k in range(0, len(planes), 2)]
        if turn:
            fields = [(real.T, imag.T) for real, imag in fields]
    return fields


def from_frequency(waves, fields):
    for turn in (True, False):
        planes = multiply(waves[1], [plane for field in fields for plane in fold(*field)])
        yield
        if turn:
            planes = [plane.T for plane in planes]
        fields = [tuple(planes[k : k + 2]) for k in range(0, len(planes), 2)]
    return fields


def product(left, right):
    return left[0] * right[0] - left[1] * right[1], left[0] * right[1] + left[1] * right[0]


def conjugate_product(left, right):
    return left[0] * right[0] + left[1] * right[1], left[0] * right[1] - left[1] * right[0]


def grads_kernel(field, amp, meta_hbm, probe, prop_ref, waves_hbm, grad, waves, meta_ref, order, sems):
    core = lax.axis_index("pos") % 2
    base = 6 * core
    meta_load = pltpu.make_async_copy(meta_hbm, meta_ref, sems.at[0])
    meta_load.start()
    waves_load = pltpu.make_async_copy(waves_hbm, waves, sems.at[1])
    waves_load.start()

    def clear(tiles):
        for tile in tiles:
            grad[tile // 4, tile % 4] = jnp.zeros((2 * SIDE, SIDE), jnp.float32)

    def read(slot):
        code = meta_ref[slot >> 5, (slot >> 1) & 15, 0, slot & 1] - 1
        return code >= 0, code >> 11, code & 2047

    clear(range(2 * SPAN))
    meta_load.wait()
    whole, first_only, last_only = [jnp.int32(0)] * 3
    for slot in range(64):
        valid, _, col = read(slot)
        whole = whole + valid.astype(jnp.int32)
        first_only = first_only + (valid & (col < LOW_COL)).astype(jnp.int32)
        last_only = last_only + (valid & (col > HIGH_COL)).astype(jnp.int32)
    clear(range(2 * SPAN, 4 * SPAN))
    to_first = jnp.clip(((whole + 1) >> 1) - first_only, 0, whole - first_only - last_only)
    count, seen = jnp.int32(0), jnp.int32(0)
    for slot in range(64):
        valid, _, col = read(slot)
        free = (col >= LOW_COL) & (col <= HIGH_COL)
        on_first = (col < LOW_COL) | (free & (seen < to_first))
        order[count] = jnp.int32(slot)
        count = count + (valid & (on_first == (core == 0))).astype(jnp.int32)
        seen = seen + (valid & free).astype(jnp.int32)
    waves_load.wait()
    lane = lax.broadcasted_iota(jnp.int32, (SIDE, SIDE), 1)

    def place(slot):
        valid, row, col = read(slot)
        row, col = jnp.where(valid, row, 0), jnp.where(valid, col, base * SIDE)
        block, shift = jnp.clip((col >> 7) - base, 0, SPAN - 1), col & (SIDE - 1)
        return pl.ds(row, SIDE), block, jnp.minimum(block + 1, SPAN - 1), shift

    def cut(plane, where):
        rows, block, next_block, shift = where
        back = (SIDE - shift) & (SIDE - 1)
        first = pltpu.roll(field[plane, block, rows, :], back, 1)
        second = pltpu.roll(field[plane, next_block, rows, :], back, 1)
        return jnp.where(lane < SIDE - shift, first, second)

    def add(plane, where, value):
        rows, block, next_block, shift = where
        moved = pltpu.roll(value.astype(jnp.bfloat16).astype(jnp.float32), shift, 1)
        zero = jnp.zeros_like(moved)
        grad[block, plane, rows, :] += jnp.where(lane >= shift, moved, zero)
        grad[next_block, plane, rows, :] += jnp.where(lane < shift, moved, zero)

    def stages(where, slot, weight):
        t0, t1 = [(cut(k, where), cut(k + 2, where)) for k in range(2)]
        probes = [(probe[m, 0], probe[m, 1]) for m in range(2)]
        prop = (prop_ref[0], prop_ref[1])
        fields = [product(p, t0) for p in probes]
        yield
        fields = yield from to_frequency(waves, fields)
        middle = yield from from_frequency(waves, [product(f, prop) for f in fields])
        far = yield from to_frequency(waves, [product(u, t1) for u in middle])
        model = 1.0 + sum(real * real + imag * imag for real, imag in far)
        factor = weight * (1.0 - decoded(amp[slot >> 5, (slot >> 1) & 15, slot & 1]) * lax.rsqrt(model))
        fields = yield from from_frequency(waves, [(real * factor, imag * factor) for real, imag in far])

        def add_slice(k, parts):
            add(k, where, parts[0][0] + parts[1][0])
            add(k + 2, where, parts[0][1] + parts[1][1])

        add_slice(1, [conjugate_product(u, g) for u, g in zip(middle, fields)])
        fields = yield from to_frequency(waves, [conjugate_product(t1, g) for g in fields])
        fields = yield from from_frequency(waves, [conjugate_product(prop, h) for h in fields])
        add_slice(0, [conjugate_product(p, e) for p, e in zip(probes, fields)])

    def step(groups, start, index, _):
        running = []
        for group in range(groups):
            item = start + index * groups + group
            slot = order[jnp.minimum(item, count - 1)]
            weight = jnp.where(item < count, 2.0, 0.0).astype(jnp.float32)
            running.append(stages(place(slot), slot, weight))
        while running:
            running = [machine for machine in running if next(machine, 0) is None]
        return 0

    full = (count + CHAINS - 1 - LAST_CHAINS) // CHAINS
    lax.fori_loop(0, full, functools.partial(step, CHAINS, 0), 0)
    rest = jnp.clip(count - CHAINS * full, 0, 1)
    lax.fori_loop(0, rest, functools.partial(step, LAST_CHAINS, CHAINS * full), 0)


def grads_call(field, amp, meta, probe, prop, waves):
    hbm = pl.BlockSpec(memory_space=pltpu.HBM)
    vmem = pl.BlockSpec(memory_space=pltpu.VMEM)
    return pl.pallas_call(
        grads_kernel,
        out_shape=jax.ShapeDtypeStruct((SPAN, 4, 2 * SIDE, SIDE), jnp.float32),
        in_specs=[vmem] * 5 + [hbm],
        out_specs=vmem,
        scratch_shapes=[
            pltpu.VMEM(waves.shape, jnp.bfloat16),
            pltpu.SMEM(meta.shape, jnp.int32),
            pltpu.SMEM((65,), jnp.int32),
            pltpu.SemaphoreType.DMA((2,)),
        ],
        compiler_params=pltpu.CompilerParams(vmem_limit_bytes=K2_LIMIT * 2**20),
        name="window_gradients",
    )(field, amp, meta, probe, prop, pltpu.with_memory_space_constraint(waves, pltpu.HBM))


def send_kernel(obj_ref, measured_ref, phase_hbm, turn_hbm, offsets_hbm, field, amp_ref, meta_ref, prop_ref,
                offsets_ref, wide, measured, own, phase, turn, halo_ref, codes_ref, chunk, amp_out, meta_out, local_sem, halo_send, halo_recv, shared_sem, slot_sem, twin_sem):
    strip, pos = lax.axis_index("obj"), lax.axis_index("pos")
    x, core = pos // 2, pos % 2
    twin = (strip, x * 2 + 1 - core)

    def span(block):
        return pl.ds(pl.multiple_of(block * SIDE, SIDE), 2 * SIDE)

    loads = [
        pltpu.make_async_copy(obj_ref.at[:, :, span(8 * core + 2 * x)], wide, local_sem.at[0]),
        pltpu.make_async_copy(measured_ref, measured, local_sem.at[1]),
        pltpu.make_async_copy(turn_hbm, turn, local_sem.at[2]),
        pltpu.make_async_copy(phase_hbm, phase, local_sem.at[3]),
        pltpu.make_async_copy(obj_ref.at[:, :, pl.ds(pl.multiple_of(6 * core * SIDE, SIDE), SPAN * SIDE)], own, local_sem.at[4]),
    ]
    loads.append(pltpu.make_async_copy(offsets_hbm, offsets_ref, local_sem.at[5]))
    for load in loads:
        load.start()
    barrier = pltpu.get_barrier_semaphore()

    def greet_strip(step, _):
        pl.semaphore_signal(barrier, inc=1, device_id=(lax.rem(strip + step, 16), pos), device_id_type=MESH)
        return 0

    lax.fori_loop(1, 16, greet_strip, 0)
    for step in range(1, 4):
        other = lax.rem(x + step, 4) * 2 + core
        pl.semaphore_signal(barrier, inc=1, device_id=(strip, other), device_id_type=MESH)
    pl.semaphore_signal(barrier, inc=1, device_id=twin, device_id_type=MESH)
    loads[0].wait()
    for block in range(2):
        lanes = slice(block * SIDE, (block + 1) * SIDE)
        for plane in range(4):
            chunk[plane * 2 + block] = wide[plane, :, lanes].astype(jnp.bfloat16)
    pl.semaphore_wait(barrier, 19)

    def piece(number):
        return pl.ds(number * (8 // PIECES), 8 // PIECES)

    def spread(source, index, number, where, send):
        return pltpu.make_async_remote_copy(
            src_ref=source.at[piece(number)], dst_ref=halo_ref.at[index, piece(number)], send_sem=halo_send.at[send, number],
            recv_sem=halo_recv.at[index, number], device_id=where, device_id_type=MESH,
        )

    above = (lax.rem(strip + 15, 16), pos)
    for number in range(PIECES):
        spread(chunk, x, number, above, 0).start()

    def amp_copy(target):
        return pltpu.make_async_remote_copy(
            src_ref=amp_out.at[target], dst_ref=amp_ref.at[core, strip], send_sem=slot_sem.at[0],
            recv_sem=slot_sem.at[1], device_id=(target, pos), device_id_type=MESH,
        )

    def meta_copy(target):
        return pltpu.make_async_remote_copy(
            src_ref=meta_out.at[target], dst_ref=meta_ref.at[core, strip], send_sem=slot_sem.at[2],
            recv_sem=slot_sem.at[3], device_id=(target, pos), device_id_type=MESH,
        )

    def all_copies():
        others = pl.ds(0, 15)
        return [
            pltpu.make_async_remote_copy(
                src_ref=source.at[others], dst_ref=target.at[core, others], send_sem=slot_sem.at[2 * k],
                recv_sem=slot_sem.at[2 * k + 1], device_id=twin, device_id_type=MESH,
            )
            for k, (source, target) in enumerate(((amp_out, amp_ref), (meta_out, meta_ref)))
        ]

    def to_twin(side):
        return [
            pltpu.make_async_remote_copy(
                src_ref=ref.at[core], dst_ref=ref.at[side], send_sem=twin_sem.at[2 * k], recv_sem=twin_sem.at[2 * k + 1],
                device_id=twin, device_id_type=MESH,
            )
            for k, ref in enumerate((amp_ref, meta_ref))
        ]

    lane = lax.broadcasted_iota(jnp.int32, META_TILE, 1)
    loads[1].wait()
    loads[5].wait()
    loads[2].wait()
    turn_back = turn[...].astype(jnp.float32).T.astype(jnp.bfloat16)

    def reorder(planes):
        rows = jnp.dot(jnp.concatenate(planes, axis=0).astype(jnp.bfloat16), turn_back, preferred_element_type=jnp.float32)
        rows = [rows[k * SIDE : (k + 1) * SIDE].T for k in range(len(planes))]
        rows = jnp.dot(jnp.concatenate(rows, axis=0).astype(jnp.bfloat16), turn_back, preferred_element_type=jnp.float32)
        return [rows[k * SIDE : (k + 1) * SIDE] for k in range(len(planes))]

    def encode(group, _):
        codes = [coded(measured[4 * group + k]) for k in range(4)]
        high = [jnp.floor(code * (1.0 / 256.0)) for code in codes]
        planes = reorder(high + [code - 256.0 * part for code, part in zip(codes, high)])
        for k in range(4):
            codes_ref[4 * group + k] = (256.0 * planes[k] + planes[4 + k]).astype(jnp.int32).astype(AMP)
        return 0

    lax.fori_loop(0, measured.shape[0] // 4, encode, 0)

    def packed(target):
        where, codes, seen = [jnp.int32(0)] * CAP, [jnp.int32(0)] * CAP, jnp.int32(0)
        for item in range(offsets_ref.shape[1]):
            row, col = offsets_ref[0, item], offsets_ref[1, item]
            here = row // SIDE == target
            for k in range(CAP):
                take = here & (seen == k)
                where[k] = jnp.where(take, item, where[k])
                codes[k] = jnp.where(take, 1 + row % SIDE * 2048 + col, codes[k])
            seen = seen + here.astype(jnp.int32)
        return jnp.where(lane == 0, codes[0], codes[1]), [codes_ref[index] for index in where]

    def pack(step, _):
        target = (strip // 4 + step % 4) % 4 * 4 + (strip + step // 4) % 4
        codes, values = packed(target)
        meta_out[target] = codes
        for k in range(CAP):
            amp_out[target, k] = values[k]
        amp_copy(target).start()
        meta_copy(target).start()
        return 0

    def forward(number):
        spread(chunk, x, number, above, 0).wait_recv()
        for step in (2, 1, 3):
            spread(halo_ref.at[x], x, number, (strip, lax.rem(x + step, 4) * 2 + core), step).start()

    bounds = [1, 6] + [6 + (10 * k) // PIECES for k in range(1, PIECES)] + [16]
    lax.fori_loop(1, 16, pack, 0)
    for number in range(PIECES):
        forward(number)
    codes, values = packed(strip)
    meta_ref[core, strip] = codes
    for k in range(CAP):
        amp_ref[core, strip, k] = values[k]

    loads[3].wait()
    value, planes = phase[...], []
    for _ in range(3):
        planes.append(value.astype(jnp.bfloat16))
        value = value - planes[-1].astype(jnp.float32)
    planes = reorder(planes)
    moved_phase = planes[0] + planes[1] + planes[2]
    prop_ref[0] = jnp.cos(moved_phase)
    prop_ref[1] = jnp.sin(moved_phase)
    loads[4].wait()

    def widen_own(block, _):
        span = pl.ds(pl.multiple_of(block * SIDE, SIDE), SIDE)
        for plane in range(4):
            field[plane, block, :SIDE, :] = own[plane, :, span].astype(jnp.bfloat16).astype(jnp.float32)
        return 0

    lax.fori_loop(0, SPAN, widen_own, 0)

    arrivals = all_copies()
    for copy in arrivals:
        copy.wait_recv()
    relays = to_twin(core)
    for copy in relays:
        copy.start()
    for number in range(PIECES):
        for step in range(1, 4):
            spread(chunk, lax.rem(x + step, 4), number, (strip, pos), 0).wait_recv()

    shared = pltpu.make_async_remote_copy(
        src_ref=halo_ref.at[3 - 3 * core], dst_ref=halo_ref.at[4], send_sem=shared_sem.at[0], recv_sem=shared_sem.at[1],
        device_id=twin, device_id_type=MESH,
    )
    shared.start()

    def widen_halo(step, _):
        part = step // 2
        block = 2 * core + step
        for plane in range(4):
            field[plane, block, SIDE:, :] = halo_ref[part, 2 * plane + step % 2].astype(jnp.float32)
        return 0

    lax.fori_loop(0, 8, widen_halo, 0)
    shared.wait()
    for plane in range(4):
        for block in range(2):
            field[plane, 8 - 8 * core + block, SIDE:, :] = halo_ref[4, 2 * plane + block].astype(jnp.float32)
    for copy in arrivals + relays:
        copy.wait_send()
    for copy in to_twin(1 - core):
        copy.wait_recv()
    for number in range(PIECES):
        for step in range(4):
            spread(chunk, x, number, (strip, pos), step).wait_send()


def send_call(obj, measured, phase, order, offsets):
    hbm = pl.BlockSpec(memory_space=pltpu.HBM)
    vmem = pl.BlockSpec(memory_space=pltpu.VMEM)
    dma = pltpu.SemaphoreType.DMA
    return pl.pallas_call(
        send_kernel,
        out_shape=(
            jax.ShapeDtypeStruct((4, SPAN, 2 * SIDE, SIDE), jnp.float32),
            jax.ShapeDtypeStruct((2, 16, CAP, SIDE, SIDE), AMP),
            jax.ShapeDtypeStruct((2, 16, *META_TILE), jnp.int32),
            jax.ShapeDtypeStruct((2, SIDE, SIDE), jnp.float32),
        ),
        in_specs=[hbm] * 5,
        out_specs=(vmem,) * 4,
        scratch_shapes=[
            pltpu.SMEM(offsets.shape, jnp.int32),
            pltpu.VMEM((4, SIDE, 2 * SIDE), jnp.float32),
            pltpu.VMEM(measured.shape, jnp.float32),
            pltpu.VMEM((4, SIDE, SPAN * SIDE), jnp.float32),
            pltpu.VMEM((SIDE, SIDE), jnp.float32),
            pltpu.VMEM((SIDE, SIDE), jnp.bfloat16),
            pltpu.VMEM((5, 8, SIDE, SIDE), jnp.bfloat16),
            pltpu.VMEM(measured.shape, AMP),
            pltpu.VMEM((8, SIDE, SIDE), jnp.bfloat16),
            pltpu.VMEM((16, CAP, SIDE, SIDE), AMP),
            pltpu.VMEM((16, *META_TILE), jnp.int32),
            dma((6,)),
            dma((4, PIECES)),
            dma((4, PIECES)),
            dma((2,)),
            dma((4,)),
            dma((4,)),
        ],
        compiler_params=pltpu.CompilerParams(collective_id=0, has_side_effects=True, vmem_limit_bytes=20 * 2**20),
        name="exchange_inputs",
    )(*[pltpu.with_memory_space_constraint(x, pltpu.HBM) for x in (obj, measured, phase, order, offsets)])


def sum_kernel(grad_ref, out_ref, twin_out, plain_out, down_out, theirs, joined, from_above, raised, parts, low_in, low_out, twin_sem, z_send, z_recv, x_send, x_recv, low_sem):
    strip, pos = lax.axis_index("obj"), lax.axis_index("pos")
    x, core = pos // 2, pos % 2
    twin = (strip, x * 2 + 1 - core)
    below, above = (lax.rem(strip + 1, 16), pos), (lax.rem(strip + 15, 16), pos)
    barrier = pltpu.get_barrier_semaphore()
    for step in range(1, 8):
        pl.semaphore_signal(barrier, inc=1, device_id=(strip, lax.rem(pos + step, 8)), device_id_type=MESH)
    for device in (below, above):
        pl.semaphore_signal(barrier, inc=1, device_id=device, device_id_type=MESH)

    shared = 3 - 3 * core
    plain = lax.rem(shared + 2, 4)
    early = [lax.rem(shared + 1, 4), lax.rem(shared + 3, 4)]
    lower, upper = pl.ds(SIDE, SIDE), pl.ds(0, SIDE)
    halves = (lower, upper)

    def place(pair, block):
        return 2 * pair + 2 * core + block

    for block in range(2):
        for plane in range(4):
            twin_out[block, plane] = grad_ref[8 - 8 * core + block, plane].astype(jnp.bfloat16)
            plain_out[block, plane] = grad_ref[place(plain, block), plane].astype(jnp.bfloat16)
            for which in range(2):
                down_out[which, block, plane] = grad_ref[place(early[which], block), plane, SIDE:].astype(jnp.bfloat16)
    pl.semaphore_wait(barrier, 9)
    to_twin = pltpu.make_async_remote_copy(
        src_ref=twin_out, dst_ref=theirs, send_sem=twin_sem.at[0], recv_sem=twin_sem.at[1],
        device_id=twin, device_id_type=MESH,
    )
    to_twin.start()

    def downward(which, block):
        return pltpu.make_async_remote_copy(
            src_ref=down_out.at[which, block], dst_ref=from_above.at[which, block],
            send_sem=z_send.at[which, block], recv_sem=z_recv.at[which, block], device_id=below, device_id_type=MESH,
        )

    for block in range(2):
        for which in range(2):
            downward(which, block).start()

    def remote(pair, source, half, block, target, start):
        return pltpu.make_async_remote_copy(
            src_ref=source, dst_ref=parts.at[start, half, block], send_sem=x_send.at[pair, half, block],
            recv_sem=x_recv.at[start, half, block], device_id=(strip, target), device_id_type=MESH,
        )

    def give(pair, source, half, block):
        target = 4 * core + pair

        @pl.when(target != pos)
        def _():
            remote(pair, source, half, block, target, x).start()

        @pl.when(target == pos)
        def _():
            pltpu.make_async_copy(source, parts.at[x, half, block], x_recv.at[x, half, block]).start()

    for half in range(2):
        for block in range(2):
            give(plain, plain_out.at[block, :, halves[half]], half, block)
    to_twin.wait_recv()
    for half in range(2):
        rows = slice(SIDE, None) if half == 0 else slice(0, SIDE)
        for block in range(2):
            for plane in range(4):
                own = grad_ref[place(shared, block), plane, rows]
                joined[block, plane, rows] = (own + theirs[block, plane, rows].astype(jnp.float32)).astype(jnp.bfloat16)
            give(shared, joined.at[block, :, halves[half]], half, block)
    for block in range(2):
        for which in range(2):
            downward(which, block).wait_recv()
            for plane in range(4):
                own = grad_ref[place(early[which], block), plane, :SIDE]
                raised[which, block, plane] = (own + from_above[which, block, plane].astype(jnp.float32)).astype(jnp.bfloat16)
            give(early[which], raised.at[which, block], 1, block)

    def arrived(half, block):
        for start in range(4):
            remote(0, joined.at[block, :, upper], half, block, pos, start).wait_recv()

    def total(half, block, plane):
        value = parts[0, half, block, plane].astype(jnp.float32)
        for start in range(1, 4):
            value += parts[start, half, block, plane].astype(jnp.float32)
        return value

    shift = pltpu.make_async_remote_copy(
        src_ref=low_out, dst_ref=low_in, send_sem=low_sem.at[0], recv_sem=low_sem.at[1], device_id=below, device_id_type=MESH,
    )
    sends_low = lax.rem(pos, 4) % 2 != pos // 4

    @pl.when(sends_low)
    def _():
        for block in range(2):
            arrived(0, block)
            for plane in range(4):
                low_out[block, plane] = total(0, block, plane).astype(jnp.bfloat16)
        shift.start()

    for block in range(2):
        arrived(1, block)
        for plane in range(4):
            out_ref[plane, :, block * SIDE : (block + 1) * SIDE] = total(1, block, plane)

    @pl.when(sends_low)
    def _():
        shift.wait_recv()
        for block in range(2):
            for plane in range(4):
                out_ref[plane, :, block * SIDE : (block + 1) * SIDE] += low_in[block, plane].astype(jnp.float32)
        shift.wait_send()

    to_twin.wait_send()
    for block in range(2):
        for which in range(2):
            downward(which, block).wait_send()
    for pair, sent in ((plain, (0, 1)), (shared, (0, 1)), (early[0], (1,)), (early[1], (1,))):

        @pl.when(4 * core + pair != pos)
        def _():
            for half in sent:
                for block in range(2):
                    remote(pair, joined.at[block, :, upper], half, block, twin[1], x).wait_send()


def sum_call(grad):
    dma = pltpu.SemaphoreType.DMA
    two = (2, 4, 2 * SIDE, SIDE)
    return pl.pallas_call(
        sum_kernel,
        out_shape=jax.ShapeDtypeStruct((4, SIDE, 2 * SIDE), jnp.float32),
        in_specs=[pl.BlockSpec(memory_space=pltpu.VMEM)],
        out_specs=pl.BlockSpec(memory_space=pltpu.VMEM),
        scratch_shapes=[
            pltpu.VMEM(two, jnp.bfloat16),
            pltpu.VMEM(two, jnp.bfloat16),
            pltpu.VMEM((2, 2, 4, SIDE, SIDE), jnp.bfloat16),
            pltpu.VMEM(two, jnp.bfloat16),
            pltpu.VMEM(two, jnp.bfloat16),
            pltpu.VMEM((2, 2, 4, SIDE, SIDE), jnp.bfloat16),
            pltpu.VMEM((2, 2, 4, SIDE, SIDE), jnp.bfloat16),
            pltpu.VMEM((4, 2, 2, 4, SIDE, SIDE), jnp.bfloat16),
            pltpu.VMEM((2, 4, SIDE, SIDE), jnp.bfloat16),
            pltpu.VMEM((2, 4, SIDE, SIDE), jnp.bfloat16),
            dma((2,)),
            dma((2, 2)),
            dma((2, 2)),
            dma((4, 2, 2)),
            dma((4, 2, 2)),
            dma((2,)),
        ],
        compiler_params=pltpu.CompilerParams(collective_id=1, has_side_effects=True, vmem_limit_bytes=20 * 2**20),
        name="sum_gradients",
    )(grad)


def per_device(object_field, probe_modes, propagator_phase, offsets, measured):
    obj = object_field.reshape(4, SIDE, object_field.shape[3])
    waves, order = [jnp.asarray(x) for x in dft_operands()]
    field, amp, meta, prop = send_call(obj, measured, propagator_phase, order, offsets.T)
    grad = grads_call(field, amp, meta, probe_modes, prop, waves)
    return sum_call(grad).reshape(2, 2, SIDE, 2 * SIDE)


def solution(mesh):
    placed = (
        P(None, None, "obj", None),
        P(),
        P(),
        P(("obj", "pos"), None),
        P(("obj", "pos"), None, None),
    )
    return jax.shard_map(
        per_device,
        mesh=mesh,
        in_specs=placed,
        out_specs=P(None, None, "obj", "pos"),
        check_vma=False,
    )
```

```python
import functools
import math

import jax
import jax.numpy as jnp
import numpy as np
from jax import lax
from jax.experimental import pallas as pl
from jax.experimental.pallas import tpu as pltpu
from jax.sharding import PartitionSpec as P

CAP = 2
SIDE = 128
META_TILE = (1, 128)
PIECES = 4
CHAINS, LAST_CHAINS = 5, 3
K2_LIMIT = 24
SPAN = 10
LOW_COL, HIGH_COL = 768, 1152
AMP = jnp.int16
AMP_MIDDLE, AMP_STEPS = 2.625, 16384.0
MESH = pl.DeviceIdType.MESH


def dft_operands():
    index = np.arange(SIDE)
    angles = (index[:, None] * index[None, :] % SIDE) * (2.0 * math.pi / SIDE)
    wave = np.cos(angles) / math.sqrt(SIDE)
    wave[SIDE // 2 + 1 :] = np.sin(angles[1 : SIDE // 2]) / math.sqrt(SIDE)

    def product(block):
        block = block.astype(np.float32)
        high = block.astype(jnp.bfloat16)
        low = (block - high.astype(np.float32)).astype(jnp.bfloat16)
        return np.block([[high, high], [low, np.zeros_like(low)]])

    order = np.zeros((SIDE, SIDE), jnp.bfloat16)
    order[index, np.where(index <= SIDE // 2, index, SIDE + SIDE // 2 - index)] = 1
    return np.stack([product(wave), product(wave.T)]), order


def coded(measured):
    return jnp.round((jnp.sqrt(measured) - AMP_MIDDLE) * AMP_STEPS)


def decoded(code):
    return code.astype(jnp.int32).astype(jnp.float32) * (1.0 / AMP_STEPS) + AMP_MIDDLE


def multiply(left, planes):
    x = jnp.concatenate(planes, axis=1)
    high = x.astype(jnp.bfloat16)
    low = (x - high.astype(jnp.float32)).astype(jnp.bfloat16)
    y = jnp.dot(left, jnp.concatenate([high, low], axis=0), preferred_element_type=jnp.float32)
    y = y[:SIDE] + y[SIDE:]
    return [y[:, k * SIDE : (k + 1) * SIDE] for k in range(len(planes))]


def halves(plane):
    return plane[: SIDE // 2], plane[SIDE // 2 :]


def with_first_row(first, rest):
    row = lax.broadcasted_iota(jnp.int32, (8, SIDE), 0)
    return jnp.concatenate([jnp.where(row == 0, first[:8], rest[:8]), rest[8:]], axis=0)


def unfold(real, imag):
    (tr, br), (ti, bi) = halves(real), halves(imag)
    return (
        jnp.concatenate([with_first_row(tr, tr + bi), with_first_row(br, tr - bi)], axis=0),
        jnp.concatenate([with_first_row(ti, ti - br), with_first_row(bi, ti + br)], axis=0),
    )


def fold(real, imag):
    (tr, br), (ti, bi) = halves(real), halves(imag)
    return (
        jnp.concatenate([with_first_row(tr, tr + br), with_first_row(br, bi - ti)], axis=0),
        jnp.concatenate([with_first_row(ti, ti + bi), with_first_row(bi, tr - br)], axis=0),
    )


def to_frequency(waves, fields):
    for turn in (True, False):
        planes = multiply(waves[0], [plane for field in fields for plane in field])
        yield
        fields = [unfold(*planes[k : k + 2]) for k in range(0, len(planes), 2)]
        if turn:
            fields = [(real.T, imag.T) for real, imag in fields]
    return fields


def from_frequency(waves, fields):
    for turn in (True, False):
        planes = multiply(waves[1], [plane for field in fields for plane in fold(*field)])
        yield
        if turn:
            planes = [plane.T for plane in planes]
        fields = [tuple(planes[k : k + 2]) for k in range(0, len(planes), 2)]
    return fields


def product(left, right):
    return left[0] * right[0] - left[1] * right[1], left[0] * right[1] + left[1] * right[0]


def conjugate_product(left, right):
    return left[0] * right[0] + left[1] * right[1], left[0] * right[1] - left[1] * right[0]


def grads_kernel(field, amp, meta_hbm, probe, prop_ref, waves_hbm, grad, waves, meta_ref, order, sems):
    core = lax.axis_index("pos") % 2
    base = 6 * core
    meta_load = pltpu.make_async_copy(meta_hbm, meta_ref, sems.at[0])
    meta_load.start()
    waves_load = pltpu.make_async_copy(waves_hbm, waves, sems.at[1])
    waves_load.start()

    def clear(tiles):
        for tile in tiles:
            grad[tile // 4, tile % 4] = jnp.zeros((2 * SIDE, SIDE), jnp.float32)

    def read(slot):
        code = meta_ref[slot >> 5, (slot >> 1) & 15, 0, slot & 1] - 1
        return code >= 0, code >> 11, code & 2047

    clear(range(2 * SPAN))
    meta_load.wait()
    whole, first_only, last_only = [jnp.int32(0)] * 3
    for slot in range(64):
        valid, _, col = read(slot)
        whole = whole + valid.astype(jnp.int32)
        first_only = first_only + (valid & (col < LOW_COL)).astype(jnp.int32)
        last_only = last_only + (valid & (col > HIGH_COL)).astype(jnp.int32)
    clear(range(2 * SPAN, 4 * SPAN))
    to_first = jnp.clip(((whole + 1) >> 1) - first_only, 0, whole - first_only - last_only)
    count, seen = jnp.int32(0), jnp.int32(0)
    for slot in range(64):
        valid, _, col = read(slot)
        free = (col >= LOW_COL) & (col <= HIGH_COL)
        on_first = (col < LOW_COL) | (free & (seen < to_first))
        order[count] = jnp.int32(slot)
        count = count + (valid & (on_first == (core == 0))).astype(jnp.int32)
        seen = seen + (valid & free).astype(jnp.int32)
    waves_load.wait()
    lane = lax.broadcasted_iota(jnp.int32, (SIDE, SIDE), 1)

    def place(slot):
        valid, row, col = read(slot)
        row, col = jnp.where(valid, row, 0), jnp.where(valid, col, base * SIDE)
        block, shift = jnp.clip((col >> 7) - base, 0, SPAN - 1), col & (SIDE - 1)
        return pl.ds(row, SIDE), block, jnp.minimum(block + 1, SPAN - 1), shift

    def cut(plane, where):
        rows, block, next_block, shift = where
        back = (SIDE - shift) & (SIDE - 1)
        first = pltpu.roll(field[plane, block, rows, :], back, 1)
        second = pltpu.roll(field[plane, next_block, rows, :], back, 1)
        return jnp.where(lane < SIDE - shift, first, second)

    def add(plane, where, value):
        rows, block, next_block, shift = where
        moved = pltpu.roll(value.astype(jnp.bfloat16).astype(jnp.float32), shift, 1)
        zero = jnp.zeros_like(moved)
        grad[block, plane, rows, :] += jnp.where(lane >= shift, moved, zero)
        grad[next_block, plane, rows, :] += jnp.where(lane < shift, moved, zero)

    def stages(where, slot, weight):
        t0, t1 = [(cut(k, where), cut(k + 2, where)) for k in range(2)]
        probes = [(probe[m, 0], probe[m, 1]) for m in range(2)]
        prop = (prop_ref[0], prop_ref[1])
        fields = [product(p, t0) for p in probes]
        yield
        fields = yield from to_frequency(waves, fields)
        middle = yield from from_frequency(waves, [product(f, prop) for f in fields])
        far = yield from to_frequency(waves, [product(u, t1) for u in middle])
        model = 1.0 + sum(real * real + imag * imag for real, imag in far)
        factor = weight * (1.0 - decoded(amp[slot >> 5, (slot >> 1) & 15, slot & 1]) * lax.rsqrt(model))
        fields = yield from from_frequency(waves, [(real * factor, imag * factor) for real, imag in far])

        def add_slice(k, parts):
            add(k, where, parts[0][0] + parts[1][0])
            add(k + 2, where, parts[0][1] + parts[1][1])

        add_slice(1, [conjugate_product(u, g) for u, g in zip(middle, fields)])
        fields = yield from to_frequency(waves, [conjugate_product(t1, g) for g in fields])
        fields = yield from from_frequency(waves, [conjugate_product(prop, h) for h in fields])
        add_slice(0, [conjugate_product(p, e) for p, e in zip(probes, fields)])

    def step(groups, start, index, _):
        running = []
        for group in range(groups):
            item = start + index * groups + group
            slot = order[jnp.minimum(item, count - 1)]
            weight = jnp.where(item < count, 2.0, 0.0).astype(jnp.float32)
            running.append(stages(place(slot), slot, weight))
        while running:
            running = [machine for machine in running if next(machine, 0) is None]
        return 0

    full = (count + CHAINS - 1 - LAST_CHAINS) // CHAINS
    lax.fori_loop(0, full, functools.partial(step, CHAINS, 0), 0)
    rest = jnp.clip(count - CHAINS * full, 0, 1)
    lax.fori_loop(0, rest, functools.partial(step, LAST_CHAINS, CHAINS * full), 0)


def grads_call(field, amp, meta, probe, prop, waves):
    hbm = pl.BlockSpec(memory_space=pltpu.HBM)
    vmem = pl.BlockSpec(memory_space=pltpu.VMEM)
    return pl.pallas_call(
        grads_kernel,
        out_shape=jax.ShapeDtypeStruct((SPAN, 4, 2 * SIDE, SIDE), jnp.float32),
        in_specs=[vmem] * 5 + [hbm],
        out_specs=vmem,
        scratch_shapes=[
            pltpu.VMEM(waves.shape, jnp.bfloat16),
            pltpu.SMEM(meta.shape, jnp.int32),
            pltpu.SMEM((65,), jnp.int32),
            pltpu.SemaphoreType.DMA((2,)),
        ],
        compiler_params=pltpu.CompilerParams(vmem_limit_bytes=K2_LIMIT * 2**20),
        name="window_gradients",
    )(field, amp, meta, probe, prop, pltpu.with_memory_space_constraint(waves, pltpu.HBM))


def send_kernel(obj_ref, measured_ref, phase_hbm, turn_hbm, offsets_hbm, field, amp_ref, meta_ref, prop_ref,
                offsets_ref, wide, measured, own, phase, turn, halo_ref, codes_ref, chunk, amp_out, meta_out, local_sem, halo_send, halo_recv, shared_sem, slot_sem, twin_sem):
    strip, pos = lax.axis_index("obj"), lax.axis_index("pos")
    x, core = pos // 2, pos % 2
    twin = (strip, x * 2 + 1 - core)

    def span(block):
        return pl.ds(pl.multiple_of(block * SIDE, SIDE), 2 * SIDE)

    loads = [
        pltpu.make_async_copy(obj_ref.at[:, :, span(8 * core + 2 * x)], wide, local_sem.at[0]),
        pltpu.make_async_copy(measured_ref, measured, local_sem.at[1]),
        pltpu.make_async_copy(turn_hbm, turn, local_sem.at[2]),
        pltpu.make_async_copy(phase_hbm, phase, local_sem.at[3]),
        pltpu.make_async_copy(obj_ref.at[:, :, pl.ds(pl.multiple_of(6 * core * SIDE, SIDE), SPAN * SIDE)], own, local_sem.at[4]),
    ]
    loads.append(pltpu.make_async_copy(offsets_hbm, offsets_ref, local_sem.at[5]))
    for load in loads:
        load.start()
    barrier = pltpu.get_barrier_semaphore()

    def greet_strip(step, _):
        pl.semaphore_signal(barrier, inc=1, device_id=(lax.rem(strip + step, 16), pos), device_id_type=MESH)
        return 0

    lax.fori_loop(1, 16, greet_strip, 0)
    for step in range(1, 4):
        other = lax.rem(x + step, 4) * 2 + core
        pl.semaphore_signal(barrier, inc=1, device_id=(strip, other), device_id_type=MESH)
    pl.semaphore_signal(barrier, inc=1, device_id=twin, device_id_type=MESH)
    loads[0].wait()
    for block in range(2):
        lanes = slice(block * SIDE, (block + 1) * SIDE)
        for plane in range(4):
            chunk[plane * 2 + block] = wide[plane, :, lanes].astype(jnp.bfloat16)
    pl.semaphore_wait(barrier, 19)

    def piece(number):
        return pl.ds(number * (8 // PIECES), 8 // PIECES)

    def spread(source, index, number, where, send):
        return pltpu.make_async_remote_copy(
            src_ref=source.at[piece(number)], dst_ref=halo_ref.at[index, piece(number)], send_sem=halo_send.at[send, number],
            recv_sem=halo_recv.at[index, number], device_id=where, device_id_type=MESH,
        )

    above = (lax.rem(strip + 15, 16), pos)
    for number in range(PIECES):
        spread(chunk, x, number, above, 0).start()

    def amp_copy(target):
        return pltpu.make_async_remote_copy(
            src_ref=amp_out.at[target], dst_ref=amp_ref.at[core, strip], send_sem=slot_sem.at[0],
            recv_sem=slot_sem.at[1], device_id=(target, pos), device_id_type=MESH,
        )

    def meta_copy(target):
        return pltpu.make_async_remote_copy(
            src_ref=meta_out.at[target], dst_ref=meta_ref.at[core, strip], send_sem=slot_sem.at[2],
            recv_sem=slot_sem.at[3], device_id=(target, pos), device_id_type=MESH,
        )

    def all_copies():
        others = pl.ds(0, 15)
        return [
            pltpu.make_async_remote_copy(
                src_ref=source.at[others], dst_ref=target.at[core, others], send_sem=slot_sem.at[2 * k],
                recv_sem=slot_sem.at[2 * k + 1], device_id=twin, device_id_type=MESH,
            )
            for k, (source, target) in enumerate(((amp_out, amp_ref), (meta_out, meta_ref)))
        ]

    def to_twin(side):
        return [
            pltpu.make_async_remote_copy(
                src_ref=ref.at[core], dst_ref=ref.at[side], send_sem=twin_sem.at[2 * k], recv_sem=twin_sem.at[2 * k + 1],
                device_id=twin, device_id_type=MESH,
            )
            for k, ref in enumerate((amp_ref, meta_ref))
        ]

    lane = lax.broadcasted_iota(jnp.int32, META_TILE, 1)
    loads[1].wait()
    loads[5].wait()
    loads[2].wait()
    turn_back = turn[...].astype(jnp.float32).T.astype(jnp.bfloat16)

    def reorder(planes):
        rows = jnp.dot(jnp.concatenate(planes, axis=0).astype(jnp.bfloat16), turn_back, preferred_element_type=jnp.float32)
        rows = [rows[k * SIDE : (k + 1) * SIDE].T for k in range(len(planes))]
        rows = jnp.dot(jnp.concatenate(rows, axis=0).astype(jnp.bfloat16), turn_back, preferred_element_type=jnp.float32)
        return [rows[k * SIDE : (k + 1) * SIDE] for k in range(len(planes))]

    def encode(group, _):
        codes = [coded(measured[4 * group + k]) for k in range(4)]
        high = [jnp.floor(code * (1.0 / 256.0)) for code in codes]
        planes = reorder(high + [code - 256.0 * part for code, part in zip(codes, high)])
        for k in range(4):
            codes_ref[4 * group + k] = (256.0 * planes[k] + planes[4 + k]).astype(jnp.int32).astype(AMP)
        return 0

    lax.fori_loop(0, measured.shape[0] // 4, encode, 0)

    def packed(target):
        where, codes, seen = [jnp.int32(0)] * CAP, [jnp.int32(0)] * CAP, jnp.int32(0)
        for item in range(offsets_ref.shape[1]):
            row, col = offsets_ref[0, item], offsets_ref[1, item]
            here = row // SIDE == target
            for k in range(CAP):
                take = here & (seen == k)
                where[k] = jnp.where(take, item, where[k])
                codes[k] = jnp.where(take, 1 + row % SIDE * 2048 + col, codes[k])
            seen = seen + here.astype(jnp.int32)
        return jnp.where(lane == 0, codes[0], codes[1]), [codes_ref[index] for index in where]

    def pack(step, _):
        target = (strip // 4 + step % 4) % 4 * 4 + (strip + step // 4) % 4
        codes, values = packed(target)
        meta_out[target] = codes
        for k in range(CAP):
            amp_out[target, k] = values[k]
        amp_copy(target).start()
        meta_copy(target).start()
        return 0

    def forward(number):
        spread(chunk, x, number, above, 0).wait_recv()
        for step in (2, 1, 3):
            spread(halo_ref.at[x], x, number, (strip, lax.rem(x + step, 4) * 2 + core), step).start()

    bounds = [1, 6] + [6 + (10 * k) // PIECES for k in range(1, PIECES)] + [16]
    lax.fori_loop(1, 16, pack, 0)
    for number in range(PIECES):
        forward(number)
    codes, values = packed(strip)
    meta_ref[core, strip] = codes
    for k in range(CAP):
        amp_ref[core, strip, k] = values[k]

    loads[3].wait()
    value, planes = phase[...], []
    for _ in range(3):
        planes.append(value.astype(jnp.bfloat16))
        value = value - planes[-1].astype(jnp.float32)
    planes = reorder(planes)
    moved_phase = planes[0] + planes[1] + planes[2]
    prop_ref[0] = jnp.cos(moved_phase)
    prop_ref[1] = jnp.sin(moved_phase)
    loads[4].wait()

    def widen_own(block, _):
        span = pl.ds(pl.multiple_of(block * SIDE, SIDE), SIDE)
        for plane in range(4):
            field[plane, block, :SIDE, :] = own[plane, :, span].astype(jnp.bfloat16).astype(jnp.float32)
        return 0

    lax.fori_loop(0, SPAN, widen_own, 0)

    for number in range(PIECES):
        for step in range(1, 4):
            spread(chunk, lax.rem(x + step, 4), number, (strip, pos), 0).wait_recv()

    shared = pltpu.make_async_remote_copy(
        src_ref=halo_ref.at[3 - 3 * core], dst_ref=halo_ref.at[4], send_sem=shared_sem.at[0], recv_sem=shared_sem.at[1],
        device_id=twin, device_id_type=MESH,
    )
    shared.start()

    arrivals = all_copies()
    for copy in arrivals:
        copy.wait_recv()
    relays = to_twin(core)
    for copy in relays:
        copy.start()

    def widen_halo(step, _):
        part = step // 2
        block = 2 * core + step
        for plane in range(4):
            field[plane, block, SIDE:, :] = halo_ref[part, 2 * plane + step % 2].astype(jnp.float32)
        return 0

    lax.fori_loop(0, 8, widen_halo, 0)
    shared.wait()
    for plane in range(4):
        for block in range(2):
            field[plane, 8 - 8 * core + block, SIDE:, :] = halo_ref[4, 2 * plane + block].astype(jnp.float32)
    for copy in arrivals + relays:
        copy.wait_send()
    for copy in to_twin(1 - core):
        copy.wait_recv()
    for number in range(PIECES):
        for step in range(4):
            spread(chunk, x, number, (strip, pos), step).wait_send()


def send_call(obj, measured, phase, order, offsets):
    hbm = pl.BlockSpec(memory_space=pltpu.HBM)
    vmem = pl.BlockSpec(memory_space=pltpu.VMEM)
    dma = pltpu.SemaphoreType.DMA
    return pl.pallas_call(
        send_kernel,
        out_shape=(
            jax.ShapeDtypeStruct((4, SPAN, 2 * SIDE, SIDE), jnp.float32),
            jax.ShapeDtypeStruct((2, 16, CAP, SIDE, SIDE), AMP),
            jax.ShapeDtypeStruct((2, 16, *META_TILE), jnp.int32),
            jax.ShapeDtypeStruct((2, SIDE, SIDE), jnp.float32),
        ),
        in_specs=[hbm] * 5,
        out_specs=(vmem,) * 4,
        scratch_shapes=[
            pltpu.SMEM(offsets.shape, jnp.int32),
            pltpu.VMEM((4, SIDE, 2 * SIDE), jnp.float32),
            pltpu.VMEM(measured.shape, jnp.float32),
            pltpu.VMEM((4, SIDE, SPAN * SIDE), jnp.float32),
            pltpu.VMEM((SIDE, SIDE), jnp.float32),
            pltpu.VMEM((SIDE, SIDE), jnp.bfloat16),
            pltpu.VMEM((5, 8, SIDE, SIDE), jnp.bfloat16),
            pltpu.VMEM(measured.shape, AMP),
            pltpu.VMEM((8, SIDE, SIDE), jnp.bfloat16),
            pltpu.VMEM((16, CAP, SIDE, SIDE), AMP),
            pltpu.VMEM((16, *META_TILE), jnp.int32),
            dma((6,)),
            dma((4, PIECES)),
            dma((4, PIECES)),
            dma((2,)),
            dma((4,)),
            dma((4,)),
        ],
        compiler_params=pltpu.CompilerParams(collective_id=0, has_side_effects=True, vmem_limit_bytes=20 * 2**20),
        name="exchange_inputs",
    )(*[pltpu.with_memory_space_constraint(x, pltpu.HBM) for x in (obj, measured, phase, order, offsets)])


def sum_kernel(grad_ref, out_ref, twin_out, plain_out, down_out, theirs, joined, from_above, raised, parts, low_in, low_out, twin_sem, z_send, z_recv, x_send, x_recv, low_sem):
    strip, pos = lax.axis_index("obj"), lax.axis_index("pos")
    x, core = pos // 2, pos % 2
    twin = (strip, x * 2 + 1 - core)
    below, above = (lax.rem(strip + 1, 16), pos), (lax.rem(strip + 15, 16), pos)
    barrier = pltpu.get_barrier_semaphore()
    for step in range(1, 8):
        pl.semaphore_signal(barrier, inc=1, device_id=(strip, lax.rem(pos + step, 8)), device_id_type=MESH)
    for device in (below, above):
        pl.semaphore_signal(barrier, inc=1, device_id=device, device_id_type=MESH)

    shared = 3 - 3 * core
    plain = lax.rem(shared + 2, 4)
    early = [lax.rem(shared + 1, 4), lax.rem(shared + 3, 4)]
    lower, upper = pl.ds(SIDE, SIDE), pl.ds(0, SIDE)
    halves = (lower, upper)

    def place(pair, block):
        return 2 * pair + 2 * core + block

    for block in range(2):
        for plane in range(4):
            twin_out[block, plane] = grad_ref[8 - 8 * core + block, plane].astype(jnp.bfloat16)
            plain_out[block, plane] = grad_ref[place(plain, block), plane].astype(jnp.bfloat16)
            for which in range(2):
                down_out[which, block, plane] = grad_ref[place(early[which], block), plane, SIDE:].astype(jnp.bfloat16)
    pl.semaphore_wait(barrier, 9)
    to_twin = pltpu.make_async_remote_copy(
        src_ref=twin_out, dst_ref=theirs, send_sem=twin_sem.at[0], recv_sem=twin_sem.at[1],
        device_id=twin, device_id_type=MESH,
    )
    to_twin.start()

    def downward(which, block):
        return pltpu.make_async_remote_copy(
            src_ref=down_out.at[which, block], dst_ref=from_above.at[which, block],
            send_sem=z_send.at[which, block], recv_sem=z_recv.at[which, block], device_id=below, device_id_type=MESH,
        )

    for block in range(2):
        for which in range(2):
            downward(which, block).start()

    def remote(pair, source, half, block, target, start):
        return pltpu.make_async_remote_copy(
            src_ref=source, dst_ref=parts.at[start, half, block], send_sem=x_send.at[pair, half, block],
            recv_sem=x_recv.at[start, half, block], device_id=(strip, target), device_id_type=MESH,
        )

    def give(pair, source, half, block):
        target = 4 * core + pair

        @pl.when(target != pos)
        def _():
            remote(pair, source, half, block, target, x).start()

        @pl.when(target == pos)
        def _():
            pltpu.make_async_copy(source, parts.at[x, half, block], x_recv.at[x, half, block]).start()

    for half in range(2):
        for block in range(2):
            give(plain, plain_out.at[block, :, halves[half]], half, block)
    to_twin.wait_recv()
    for half in range(2):
        rows = slice(SIDE, None) if half == 0 else slice(0, SIDE)
        for block in range(2):
            for plane in range(4):
                own = grad_ref[place(shared, block), plane, rows]
                joined[block, plane, rows] = (own + theirs[block, plane, rows].astype(jnp.float32)).astype(jnp.bfloat16)
            give(shared, joined.at[block, :, halves[half]], half, block)
    for block in range(2):
        for which in range(2):
            downward(which, block).wait_recv()
            for plane in range(4):
                own = grad_ref[place(early[which], block), plane, :SIDE]
                raised[which, block, plane] = (own + from_above[which, block, plane].astype(jnp.float32)).astype(jnp.bfloat16)
            give(early[which], raised.at[which, block], 1, block)

    def arrived(half, block):
        for start in range(4):
            remote(0, joined.at[block, :, upper], half, block, pos, start).wait_recv()

    def total(half, block, plane):
        value = parts[0, half, block, plane].astype(jnp.float32)
        for start in range(1, 4):
            value += parts[start, half, block, plane].astype(jnp.float32)
        return value

    shift = pltpu.make_async_remote_copy(
        src_ref=low_out, dst_ref=low_in, send_sem=low_sem.at[0], recv_sem=low_sem.at[1], device_id=below, device_id_type=MESH,
    )
    sends_low = lax.rem(pos, 4) % 2 != pos // 4

    @pl.when(sends_low)
    def _():
        for block in range(2):
            arrived(0, block)
            for plane in range(4):
                low_out[block, plane] = total(0, block, plane).astype(jnp.bfloat16)
        shift.start()

    for block in range(2):
        arrived(1, block)
        for plane in range(4):
            out_ref[plane, :, block * SIDE : (block + 1) * SIDE] = total(1, block, plane)

    @pl.when(sends_low)
    def _():
        shift.wait_recv()
        for block in range(2):
            for plane in range(4):
                out_ref[plane, :, block * SIDE : (block + 1) * SIDE] += low_in[block, plane].astype(jnp.float32)
        shift.wait_send()

    to_twin.wait_send()
    for block in range(2):
        for which in range(2):
            downward(which, block).wait_send()
    for pair, sent in ((plain, (0, 1)), (shared, (0, 1)), (early[0], (1,)), (early[1], (1,))):

        @pl.when(4 * core + pair != pos)
        def _():
            for half in sent:
                for block in range(2):
                    remote(pair, joined.at[block, :, upper], half, block, twin[1], x).wait_send()


def sum_call(grad):
    dma = pltpu.SemaphoreType.DMA
    two = (2, 4, 2 * SIDE, SIDE)
    return pl.pallas_call(
        sum_kernel,
        out_shape=jax.ShapeDtypeStruct((4, SIDE, 2 * SIDE), jnp.float32),
        in_specs=[pl.BlockSpec(memory_space=pltpu.VMEM)],
        out_specs=pl.BlockSpec(memory_space=pltpu.VMEM),
        scratch_shapes=[
            pltpu.VMEM(two, jnp.bfloat16),
            pltpu.VMEM(two, jnp.bfloat16),
            pltpu.VMEM((2, 2, 4, SIDE, SIDE), jnp.bfloat16),
            pltpu.VMEM(two, jnp.bfloat16),
            pltpu.VMEM(two, jnp.bfloat16),
            pltpu.VMEM((2, 2, 4, SIDE, SIDE), jnp.bfloat16),
            pltpu.VMEM((2, 2, 4, SIDE, SIDE), jnp.bfloat16),
            pltpu.VMEM((4, 2, 2, 4, SIDE, SIDE), jnp.bfloat16),
            pltpu.VMEM((2, 4, SIDE, SIDE), jnp.bfloat16),
            pltpu.VMEM((2, 4, SIDE, SIDE), jnp.bfloat16),
            dma((2,)),
            dma((2, 2)),
            dma((2, 2)),
            dma((4, 2, 2)),
            dma((4, 2, 2)),
            dma((2,)),
        ],
        compiler_params=pltpu.CompilerParams(collective_id=1, has_side_effects=True, vmem_limit_bytes=20 * 2**20),
        name="sum_gradients",
    )(grad)


def per_device(object_field, probe_modes, propagator_phase, offsets, measured):
    obj = object_field.reshape(4, SIDE, object_field.shape[3])
    waves, order = [jnp.asarray(x) for x in dft_operands()]
    field, amp, meta, prop = send_call(obj, measured, propagator_phase, order, offsets.T)
    grad = grads_call(field, amp, meta, probe_modes, prop, waves)
    return sum_call(grad).reshape(2, 2, SIDE, 2 * SIDE)


def solution(mesh):
    placed = (
        P(None, None, "obj", None),
        P(),
        P(),
        P(("obj", "pos"), None),
        P(("obj", "pos"), None, None),
    )
    return jax.shard_map(
        per_device,
        mesh=mesh,
        in_specs=placed,
        out_specs=P(None, None, "obj", "pos"),
        check_vma=False,
    )
```
